256 devices in a mesh: mx: 16 (over z, core), my: 16 (over x, y).
Axes of the slice: x: 4, y: 4, z: 8, core: 2. Of those that a mesh axis runs over, the one named last changes fastest.
Arguments:
- features: bfloat16 [8192, 32, 512], P(('mx', 'my')), may hold values from -6 to 6
- coords: int32 [3, 8192], P(None, ('mx', 'my')), may hold values from 0 to 63, as said below
- counts: int32 [256], P(('mx', 'my')), may hold values from 16 to 32, as said below
- neighbours: int32 [6, 8192], P(None, ('mx', 'my')), may hold values from -1 to 8191, as said below
- fine_weights: bfloat16 [3, 32, 224], replicated, may hold values from -0.375 to 0.375
- down_weight: bfloat16 [2048, 256], replicated, may hold values from -0.25 to 0.25
- up_weight: bfloat16 [256, 2048], replicated, may hold values from -0.375 to 0.375
- norm_gain: float32 [256], replicated, may hold values from 0.1 to 1.9
- norm_bias: float32 [256], replicated, may hold values from -3 to 3
- coarse_weight: bfloat16 [6912, 256], P(None, 'my'), may hold values from -0.078125 to 0.078125
Outputs:
- fine_out: bfloat16 [8192, 32, 512], P(('mx', 'my'))
- coarse_out: bfloat16 [32, 32, 2, 256], P('mx', 'my')
The draws below stay inside these ranges and needn't reach their ends.
Inputs may be any that keep to these rules, and one draw needn't show every extreme that they name: The live slots of a device are its first counts entries; some device is full in every draw. `coords`: the live blocks of the device with mx index i and my index j lie at z in [i * 4, (i + 1) * 4), y in [j * 4, (j + 1) * 4), x in [0, 4), distinct, in Morton order of their coordinates inside that region; slots that are not live hold 0. `neighbours`: A live block's entry is the slot of the live block one step away in that direction, or -1 if there is none; the relation is symmetric; slots that are not live hold -1.
All inputs are finite; a program needn't handle non-finite values.
Results may differ from the reference program's by a relative error of at most 0.0095.
Values may be sent and summed in bfloat16 or wider, within the bound.
No kernel may reach another device: no remote copies, remote signals or barrier semaphores. Data moves between devices by JAX's collectives and lax.ppermute only.
A program may use at most 128 MiB of HBM per device.

```python
import jax
import jax.numpy as jnp
from jax import lax

C = 32
CC = 256
GROUPS = 32
SIDE = 8
RZ = 4
RY = 4
RX = 4
BLK_DEV = 32
SLOTS = 8192
N_MX = 16
N_MY = 16


def morton_code(local_z, local_y, local_x):
    morton = jnp.zeros_like(local_x)
    for bit_pos in range(8):
        morton = morton | (local_x >> bit_pos & 1) << 3 * bit_pos
        morton = morton | (local_y >> bit_pos & 1) << 3 * bit_pos + 1
        morton = morton | (local_z >> bit_pos & 1) << 3 * bit_pos + 2
    return morton


def geometry(key):
    device_total = N_MX * N_MY
    region = RZ * RY * RX
    folded = jax.random.fold_in(key, 11)
    count_key, full_key, choose_key = jax.random.split(folded, 3)
    counts = jax.random.randint(count_key, (device_total,), BLK_DEV // 2, BLK_DEV + 1, dtype=jnp.int32)
    fullest = jax.random.randint(full_key, (), 0, device_total, dtype=jnp.int32)
    device_ids = jnp.arange(device_total, dtype=jnp.int32)
    counts = jnp.where(device_ids == fullest, BLK_DEV, counts).astype(jnp.int32)
    cell_ids = jnp.arange(region, dtype=jnp.int32)
    local_z = cell_ids // (RY * RX)
    local_y = cell_ids // RX % RY
    local_x = cell_ids % RX
    morton = morton_code(local_z, local_y, local_x)

    def per_device(device_key, live_count):
        ranking = jax.random.permutation(device_key, region).astype(jnp.int32)
        chosen = ranking < live_count
        scores = jnp.where(chosen, morton, morton + (1 << 25))
        return jnp.argsort(scores)[:BLK_DEV].astype(jnp.int32)
    orderings = jax.vmap(per_device)(jax.random.split(choose_key, device_total), counts)
    is_live = jnp.arange(BLK_DEV, dtype=jnp.int32)[None, :] < counts[:, None]
    block_z = (device_ids // N_MY)[:, None] * RZ + local_z[orderings]
    block_y = (device_ids % N_MY)[:, None] * RY + local_y[orderings]
    block_x = local_x[orderings]
    block_z = jnp.where(is_live, block_z, 0).reshape(-1)
    block_y = jnp.where(is_live, block_y, 0).reshape(-1)
    block_x = jnp.where(is_live, block_x, 0).reshape(-1)
    is_live = is_live.reshape(-1)
    extent_z = RZ * N_MX
    extent_y = RY * N_MY
    grid_cells = extent_z * extent_y * RX
    linear = (block_z * extent_y + block_y) * RX + block_x
    slot_ids = jnp.arange(device_total * BLK_DEV, dtype=jnp.int32)
    lookup = jnp.full((grid_cells,), -1, jnp.int32).at[jnp.where(is_live, linear, grid_cells)].set(slot_ids, mode='drop')
    steps_list = ((0, 0, 1), (0, 0, -1), (0, 1, 0), (0, -1, 0), (1, 0, 0), (-1, 0, 0))
    link_rows = []
    for step_z, step_y, step_x in steps_list:
        near_z = block_z + step_z
        near_y = block_y + step_y
        near_x = block_x + step_x
        inside = (near_z >= 0) & (near_z < extent_z) & (near_y >= 0) & (near_y < extent_y) & (near_x >= 0) & (near_x < RX) & is_live
        near_linear = (near_z * extent_y + near_y) * RX + near_x
        link_rows.append(jnp.where(inside, lookup[jnp.clip(near_linear, 0, grid_cells - 1)], -1))
    neighbours = jnp.stack(link_rows).astype(jnp.int32)
    coords = jnp.stack([block_z, block_y, block_x]).astype(jnp.int32)
    return (counts, coords, neighbours)


def draw_counts(key, part):
    return geometry(key)[0]


def draw_coords(key, part):
    return geometry(key)[1]


def draw_neighbours(key, part):
    return geometry(key)[2]


def block_levels(rng, shape, cuts, low, top_value):
    def one(position, blocks):
        draws = jax.random.uniform(jax.random.fold_in(jax.random.fold_in(rng, 6), position), (blocks,), jnp.float32, low / len(cuts), top_value / len(cuts))
        return jnp.repeat(jnp.exp(draws), shape[position] // blocks).reshape((-1,) + (1,) * (len(shape) - position - 1))

    level = one(*cuts[0])
    for cut in cuts[1:]:
        level = level * one(*cut)
    return level


def normal_values(own_key, shape, width, most, cuts=(), kind=jnp.bfloat16):
    array = width * jax.random.normal(own_key, shape, jnp.float32)
    if cuts:
        array = array * block_levels(own_key, shape, cuts, -0.22, 0.18)
    return jnp.clip(array, -most, most).astype(kind)


def setup_inputs(seed: int = 0) -> dict:
    splits = jax.random.split(jax.random.key(seed), 11)
    return {
        "features": normal_values(splits[0], (SLOTS, C, SIDE * SIDE * SIDE), 1.0, 6.0, ((0, 256),)),
        "coords": draw_coords(jax.random.fold_in(splits[10], 71), 0),
        "counts": draw_counts(jax.random.fold_in(splits[10], 71), 0),
        "neighbours": draw_neighbours(jax.random.fold_in(splits[10], 71), 0),
        "fine_weights": normal_values(splits[4], (3, C, 7 * C), (7 * C) ** -0.5, 0.375),
        "down_weight": normal_values(splits[5], (64 * C, CC), (16 * C) ** -0.5, 0.25),
        "up_weight": normal_values(splits[6], (CC, 64 * C), CC ** -0.5, 0.375),
        "norm_gain": jnp.clip(1.0 + 0.18 * jax.random.normal(splits[7], (CC,), jnp.float32), 0.1, 1.9),
        "norm_bias": normal_values(splits[8], (CC,), 0.5, 3.0, (), jnp.float32),
        "coarse_weight": normal_values(splits[9], (27 * CC, CC), (27 * CC) ** -0.5, 0.078125, ((1, 16),)),
    }


def displaced_taps(signal, near_blocks, block_side):
    volume = block_side * block_side * block_side
    voxel_ids = jnp.arange(volume, dtype=jnp.int32)
    along_x = voxel_ids % block_side
    along_y = voxel_ids // block_side % block_side
    along_z = voxel_ids // (block_side * block_side)
    last_layer = block_side - 1
    square = block_side * block_side
    plans = ((along_x < last_layer, -1, last_layer), (along_x > 0, 1, -last_layer), (along_y < last_layer, -block_side, block_side * last_layer), (along_y > 0, block_side, -block_side * last_layer), (along_z < last_layer, -square, square * last_layer), (along_z > 0, square, -square * last_layer))
    tap_list = [signal]
    for (inside, own_shift, near_shift), block in zip(plans, near_blocks):
        tap_list.append(jnp.where(inside, jnp.roll(signal, own_shift, axis=2), jnp.roll(block, near_shift, axis=2)))
    tap_stack = jnp.stack(tap_list, axis=1)
    return tap_stack.reshape(signal.shape[0], 7 * signal.shape[1], volume)

def coarse_patches(padded, depth, height, breadth):
    channel_count = padded.shape[3]
    pieces = []
    for step_z in range(3):
        for step_y in range(3):
            for step_x in range(3):
                pieces.append(padded[step_z:step_z + depth, step_y:step_y + height, step_x:step_x + breadth])
    return jnp.stack(pieces, axis=3).reshape(depth * height * breadth, 27 * channel_count)

def residual_step(base, neighbours, kernel_weight):
    signal = jax.nn.silu(base.astype(jnp.float32)).astype(jnp.bfloat16)
    device_total = N_MX * N_MY
    slot_total, chans, volume = base.shape
    block_count = slot_total // device_total

    def per_device(device_id):
        first_row = device_id * block_count
        own_rows = lax.dynamic_slice_in_dim(signal, first_row, block_count, 0)
        kept_rows = lax.dynamic_slice_in_dim(base, first_row, block_count, 0)
        link_rows = lax.dynamic_slice_in_dim(neighbours, first_row, block_count, 1)
        near_blocks = []
        for direction in range(6):
            present = link_rows[direction] >= 0
            picked = signal[jnp.clip(link_rows[direction], 0, slot_total - 1)]
            near_blocks.append(jnp.where(present[:, None, None], picked, jnp.zeros_like(picked)))
        tap_stack = displaced_taps(own_rows, near_blocks, SIDE)
        convolution_result = jnp.einsum('pn,enh->eph', kernel_weight.astype(jnp.float32), tap_stack.astype(jnp.float32))
        return (kept_rows.astype(jnp.float32) + convolution_result).astype(jnp.bfloat16)
    result = lax.map(per_device, jnp.arange(device_total, dtype=jnp.int32))
    return result.reshape(slot_total, chans, volume)

def reference(features, coords, counts, neighbours, fine_weights, down_weight, up_weight, norm_gain, norm_bias, coarse_weight):
    device_total = N_MX * N_MY
    slot_total, chans, volume = features.shape
    block_count = slot_total // device_total
    slot_ids = jnp.arange(slot_total, dtype=jnp.int32)
    is_live = slot_ids % block_count < counts[slot_ids // block_count]
    first_level = residual_step(features, neighbours, fine_weights[0])
    half_side = SIDE // 2
    pooled = lax.optimization_barrier(jnp.mean(first_level.reshape(slot_total, chans, 2, half_side, 2, half_side, 2, half_side), axis=(3, 5, 7), dtype=jnp.float32))
    pooled = pooled.transpose(0, 2, 3, 4, 1).reshape(slot_total, 8 * chans).astype(jnp.bfloat16)
    grid_z = RZ // 2 * N_MX
    grid_y = RY // 2 * N_MY
    grid_x = RX // 2
    cell_count = grid_z * grid_y * grid_x
    block_z = coords[0]
    block_y = coords[1]
    block_x = coords[2]
    cell_ids = (block_z // 2 * grid_y + block_y // 2) * grid_x + block_x // 2
    octant_pos = block_z % 2 * 4 + block_y % 2 * 2 + block_x % 2
    target = jnp.where(is_live, cell_ids * 8 + octant_pos, cell_count * 8).astype(jnp.int32)
    gathered = jnp.zeros((cell_count * 8, 8 * chans), jnp.bfloat16).at[target].set(pooled, mode='drop')
    coarse_in = jnp.dot(gathered.reshape(cell_count, 64 * chans), down_weight, preferred_element_type=jnp.float32)
    coarse_width = coarse_in.shape[1]
    grouped = coarse_in.reshape(cell_count, GROUPS, coarse_width // GROUPS)
    group_mean = lax.optimization_barrier(jnp.mean(grouped, axis=(0, 2)))
    centred = grouped - group_mean[None, :, None]
    variance = lax.optimization_barrier(jnp.mean(centred * centred, axis=(0, 2)))
    normed = (centred / jnp.sqrt(variance + 1e-05)[None, :, None]).reshape(cell_count, coarse_width) * norm_gain + norm_bias
    activated = jax.nn.silu(normed).astype(jnp.bfloat16).reshape(grid_z, grid_y, grid_x, coarse_width)
    padded = jnp.pad(activated, ((1, 1), (1, 1), (1, 1), (0, 0)))
    convolution_result = jnp.dot(coarse_patches(padded, grid_z, grid_y, grid_x), coarse_weight, preferred_element_type=jnp.float32)
    coarse_out = (convolution_result + coarse_in).astype(jnp.bfloat16)
    lifted = jnp.dot(coarse_out, up_weight, preferred_element_type=jnp.float32).reshape(cell_count * 8, 8 * chans)
    per_block = lifted[jnp.clip(target, 0, cell_count * 8 - 1)]
    per_block = jnp.where(is_live[:, None], per_block, jnp.zeros_like(per_block))

    def join_device(device_id):
        first_row = device_id * block_count
        level_row_list = lax.dynamic_slice_in_dim(first_level, first_row, block_count, 0)
        lift_rows = lax.dynamic_slice_in_dim(per_block, first_row, block_count, 0)
        spread_up = lift_rows.reshape(block_count, 2, 2, 2, chans).transpose(0, 4, 1, 2, 3)
        spread_up = jnp.broadcast_to(spread_up[:, :, :, None, :, None, :, None], (block_count, chans, 2, half_side, 2, half_side, 2, half_side))
        return (level_row_list.astype(jnp.float32) + spread_up.reshape(block_count, chans, volume)).astype(jnp.bfloat16)
    merged_features = lax.map(join_device, jnp.arange(device_total, dtype=jnp.int32)).reshape(slot_total, chans, volume)
    second_level = residual_step(merged_features, neighbours, fine_weights[1])
    final_level = residual_step(second_level, neighbours, fine_weights[2])
    fine_out = jnp.where(is_live[:, None, None], final_level, jnp.zeros_like(final_level))
    return (fine_out, coarse_out.reshape(grid_z, grid_y, grid_x, coarse_width))
```

```python
import functools

import jax
import jax.numpy as jnp
import ml_dtypes
import numpy as np
from jax import lax
from jax.experimental import pallas as pl
from jax.experimental.pallas import tpu as pltpu
from jax.sharding import Mesh
from jax.sharding import PartitionSpec as P

MX = ("mx_0", "mx_1")
MY = ("my_0", "my_1")
MX_MY = MX + MY
BLOCKS = 32
CHANS = 32
VOXELS = 512
COARSE = 256
GROUP = 8
TAPS = 27
HALF_ROWS = TAPS * COARSE // 2
NORM_EPS = 1e-05
bf16 = jnp.bfloat16
f32 = jnp.float32


def octant(z, y, x):
    return z // 4 * 4 + y // 4 * 2 + x // 4


def voxel_zyx():
    voxel = np.arange(VOXELS)
    return voxel // 64, voxel // 8 % 8, voxel % 8


@functools.cache
def tables():
    z, y, x = voxel_zyx()
    voxel = np.arange(VOXELS)
    faces = np.zeros((VOXELS, 256), np.float32)
    y_lane = z % 2 * 64 + z // 2 * 8 + x
    faces[voxel[y == 0], y_lane[y == 0]] = 1
    faces[voxel[y == 7], y_lane[y == 7] + 32] = 1
    z_lane = y * 8 + x
    faces[voxel[z == 0], 128 + 64 + z_lane[z == 0]] = 1
    faces[voxel[z == 7], 128 + z_lane[z == 7]] = 1
    own = np.arange(256) // 32
    pool = (octant(z, y, x)[:, None] == own[None, :]).astype(np.float32) / 64
    spread = (own[:, None] == octant(z, y, x)[None, :]).astype(np.float32)
    lane = np.arange(128)
    y_octant = octant(lane % 32 // 8 * 2 + lane // 64, lane // 32 % 2 * 4, lane % 8)
    z_octant = octant((lane < 64) * 4, lane % 64 // 8, lane % 8)
    y_spread = (own[:, None] == y_octant[None, :]).astype(np.float32)
    z_spread = (own[:, None] == z_octant[None, :]).astype(np.float32)
    cells = [(a, b, c) for a in range(2) for b in range(2) for c in range(2)]
    cells += [(a, b, c) for b in (-1, 2) for a in range(2) for c in range(2)]
    cells += [(a, b, c) for a in (-1, 2) for b in range(2) for c in range(2)]

    def row_of(a, b, c):
        part = (a // 2 + 1) * 3 + b // 2 + 1
        return part * 8 + a % 2 * 4 + b % 2 * 2 + c

    patch = np.zeros((TAPS, 32, 128), np.float32)
    plain = np.zeros((32, 128), np.float32)
    for i, (a, b, c) in enumerate(cells):
        plain[i, row_of(a, b, c)] = 1
        for t in range(TAPS):
            near = (a + t // 9 - 1, b + t // 3 % 3 - 1, c + t % 3 - 1)
            if 0 <= near[2] < 2:
                patch[t, i, row_of(*near)] = 1
    kinds = (faces, pool, spread, y_spread, z_spread, patch.reshape(TAPS * 32, 128), plain)
    return tuple(k.astype(ml_dtypes.bfloat16) for k in kinds)


def lanes():
    return lax.broadcasted_iota(jnp.int32, (CHANS, 128), 1)


def silu(x):
    return x * (1.0 / (1.0 + jnp.exp(-x)))


def tile(k):
    return slice(k * 128, k * 128 + 128)


def take_faces(signal, faces_ref, y_bank, z_bank):
    for i in range(0, BLOCKS, 8):
        block = signal[i : i + 8].reshape(8 * CHANS, VOXELS)
        packed = jnp.dot(block, faces_ref[...], preferred_element_type=f32).astype(bf16)
        y_bank[i : i + 8] = packed[:, :128].reshape(8, CHANS, 128)
        z_bank[i : i + 8] = packed[:, 128:].reshape(8, CHANS, 128)


def fill_planes(coords, counts, y_bank, z_bank, work, outs):
    lane = lanes()
    work[...] = jnp.zeros_like(work)
    in_low = (lane & 32) == 0
    in_back = lane >= 64

    def one(j, carry):
        live = j < counts[0]
        z, y, x = coords[0, j] & 3, coords[1, j] & 3, coords[2, j]
        odd = (x & 1) == 1
        y_row, z_row = (z * 4 + x) >> 1, (y * 4 + x) >> 1
        face = y_bank[j]
        turned = pltpu.roll(face, 32, 1)
        value = jnp.where(odd, turned, face)
        for plane, edge, low in ((0, 0, True), (1, 3, False)):
            row = jnp.where(live & (y == edge), y_row, 8)
            mask = jnp.logical_xor(in_low if low else jnp.logical_not(in_low), odd)
            work[plane, row] = jnp.where(mask, value, work[plane, row])
        face = z_bank[j]
        turned = pltpu.roll(face, 64, 1)
        value = jnp.where(odd, turned, face)
        for plane, edge, low in ((2, 0, True), (3, 3, False)):
            row = jnp.where(live & (z == edge), z_row, 8)
            mask = jnp.logical_xor(in_back if low else jnp.logical_not(in_back), odd)
            work[plane, row] = jnp.where(mask, value, work[plane, row])
        return carry

    lax.fori_loop(0, BLOCKS, one, 0, unroll=4)
    for plane, out in enumerate(outs):
        out[...] = work[plane, :8]


def received(plane_ref, p, back):
    row = plane_ref[p // 2]
    return pltpu.roll(row, back, 1) if p % 2 else row


def bank_received(planes, y_bank, z_bank):
    zero = jnp.zeros((CHANS, 128), bf16)
    y_bank[BLOCKS] = zero
    z_bank[BLOCKS] = zero
    for p in range(16):
        y_bank[33 + p] = received(planes[0], p, 96)
        y_bank[49 + p] = received(planes[1], p, 96)
        z_bank[33 + p] = received(planes[2], p, 64)
        z_bank[49 + p] = received(planes[3], p, 64)


def convolve(coords, links, signal, y_bank, z_bank, weight, taps, finish):
    lane = lanes()
    along_x = lane & 7
    along_yx = lane & 63
    front = lane < 64

    def build(j, slot):
        z, y, x = coords[0, j] & 3, coords[1, j] & 3, coords[2, j]
        y_pos, z_pos = z * 4 + x, y * 4 + x

        def near(direction, inside, remote):
            link = links[direction, j]
            here = link & (BLOCKS - 1)
            if inside is not None:
                here = jnp.where(inside, here, remote)
            return jnp.where(link < 0, BLOCKS, here)

        x_up, x_down = near(0, None, None), near(1, None, None)
        y_up = y_bank[near(2, y < 3, 33 + y_pos)]
        y_down = y_bank[near(3, y > 0, 49 + y_pos)]
        z_up = z_bank[near(4, z < 3, 33 + z_pos)]
        z_down = z_bank[near(5, z > 0, 49 + z_pos)]
        own = [signal[j, :, tile(k)] for k in range(4)]
        half = [z_down] + [pltpu.roll(own[k], 64, 1) for k in range(4)] + [z_up]
        for k in range(4):
            to = tile(k)
            taps[slot, 0:32, to] = own[k]
            taps[slot, 32:64, to] = jnp.where(
                along_x == 7,
                pltpu.roll(signal[x_up, :, to], 7, 1),
                pltpu.roll(own[k], 127, 1),
            )
            taps[slot, 64:96, to] = jnp.where(
                along_x == 0,
                pltpu.roll(signal[x_down, :, to], 121, 1),
                pltpu.roll(own[k], 1, 1),
            )
            taps[slot, 96:128, to] = jnp.where(
                along_yx >= 56, pltpu.roll(y_up, 56 - 8 * k, 1), pltpu.roll(own[k], 120, 1)
            )
            taps[slot, 128:160, to] = jnp.where(
                along_yx < 8, pltpu.roll(y_down, 96 - 8 * k, 1), pltpu.roll(own[k], 8, 1)
            )
            taps[slot, 160:192, to] = jnp.where(front, half[k + 1], half[k + 2])
            taps[slot, 192:224, to] = jnp.where(front, half[k], half[k + 1])

    def some(i, carry):
        for u in range(4):
            build(i * 4 + u, u)
        for u in range(4):
            result = jnp.dot(weight[...], taps[u], preferred_element_type=f32)
            finish(i * 4 + u, result)
        return carry

    lax.fori_loop(0, BLOCKS // 4, some, 0)


def first_faces(coords, counts, features, faces, signal, y_own, z_own, p0, p1, p2, p3, work):
    def one(j, carry):
        signal[j] = silu(features[j].astype(f32)).astype(bf16)
        return carry

    lax.fori_loop(0, BLOCKS, one, 0, unroll=4)
    take_faces(signal, faces, y_own, z_own)
    fill_planes(coords, counts, y_own, z_own, work, (p0, p1, p2, p3))


def first_conv(
    coords, counts, links, features, signal_in, y_own, z_own, r0, r1, r2, r3,
    weight, faces, pool, down,
    level, p0, p1, p2, p3, message,
    signal, y_bank, z_bank, taps, work, gathered,
):
    signal[0:BLOCKS] = signal_in[...]
    signal[BLOCKS] = jnp.zeros((CHANS, VOXELS), bf16)
    y_bank[0:BLOCKS] = y_own[...]
    z_bank[0:BLOCKS] = z_own[...]
    bank_received((r0, r1, r2, r3), y_bank, z_bank)

    def finish(j, result):
        level[j] = (features[j].astype(f32) + result).astype(bf16)

    convolve(coords, links, signal, y_bank, z_bank, weight, taps, finish)
    take_faces(level, faces, y_bank, z_bank)
    fill_planes(coords, counts, y_bank, z_bank, work, (p0, p1, p2, p3))
    gathered[...] = jnp.zeros_like(gathered)
    diagonal = channel_diagonal()
    for i in range(0, BLOCKS, 8):
        block = level[i : i + 8].reshape(8 * CHANS, VOXELS)
        means = jnp.dot(block, pool[...], preferred_element_type=f32)
        for u in range(8):
            j = i + u
            part = jnp.where(diagonal, means[u * CHANS : (u + 1) * CHANS], 0.0)
            cell, pos = place(coords, j)
            pos = jnp.where(j < counts[0], pos, 8)
            gathered[pos, pl.ds(cell, 1), :] = jnp.sum(part, axis=0, keepdims=True)
    total = jnp.zeros((16, COARSE), f32)
    for pos in range(8):
        total += jnp.dot(
            gathered[pos].astype(bf16), down[pos * 256 : pos * 256 + 256], preferred_element_type=f32
        )
    total = total[:8]
    mean = jnp.mean(total, axis=0, keepdims=True)
    spread = jnp.sum((total - mean) * (total - mean), axis=0, keepdims=True)
    row = lax.broadcasted_iota(jnp.int32, (8, COARSE), 0)
    extra = jnp.where(row == 0, mean, jnp.where(row == 1, spread, 0.0))
    for i in range(16):
        message[i, 0:8] = total
        message[i, 8:16] = extra


def channel_diagonal():
    channel = lax.broadcasted_iota(jnp.int32, (CHANS, 256), 0)
    return channel == (lax.broadcasted_iota(jnp.int32, (CHANS, 256), 1) & 31)


def place(coords, j):
    z, y, x = coords[0, j] & 3, coords[1, j] & 3, coords[2, j]
    cell = (z >> 1) * 4 + (y >> 1) * 2 + (x >> 1)
    return cell, (z & 1) * 4 + (y & 1) * 2 + (x & 1)


def merged_sums(means, spreads, entries):
    mean = jnp.mean(means, axis=0, keepdims=True)
    away = means - mean
    return mean, jnp.sum(spreads + entries * away * away, axis=0, keepdims=True)


def row_sums(where, message, partial, strip):
    mean, spread = merged_sums(message[:, 8, :], message[:, 9, :], 8.0)
    row = lax.broadcasted_iota(jnp.int32, (8, COARSE), 0)
    both = jnp.where(row == 0, mean, jnp.where(row == 1, spread, 0.0))
    for i in range(16):
        partial[i] = both
    minor = where[1]
    for step in range(3):
        strip[step] = message[jnp.clip(minor + step - 1, 0, 15), 0:8]


def group_total(x):
    lane = lax.broadcasted_iota(jnp.int32, x.shape, 1)
    for width in (1, 2, 4):
        x = x + jnp.where(
            (lane & width) == 0, pltpu.roll(x, COARSE - width, 1), pltpu.roll(x, width, 1)
        )
    return x


def second_conv(
    coords, counts, links, where, level, r0, r1, r2, r3, partial, s_low, s_own, s_high,
    near_half, far_half, gain, bias, up, weight, faces, spread, y_spread, z_spread, patch, plain,
    second, signal2, y_own, z_own, p0, p1, p2, p3, coarse,
    joined, signal, y_bank, z_bank, taps, work, active, raw, patches, lifted, rows,
):
    major, minor = where[0], where[1]
    mean, spread_sum = merged_sums(partial[:, 0, :], partial[:, 1, :], 128.0)
    group_mean = group_total(mean) * (1.0 / GROUP)
    away = mean - group_mean
    variance = group_total(spread_sum + 2048.0 * away * away) * (1.0 / (2048 * GROUP))
    scale = gain[...] / jnp.sqrt(variance + NORM_EPS)
    active[...] = jnp.zeros_like(active)
    raw[...] = jnp.zeros_like(raw)
    for dz, strip in enumerate((s_low, s_own, s_high)):
        inside_z = (major + dz >= 1) & (major + dz <= 16)
        for dy in range(3):
            inside = inside_z & (minor + dy >= 1) & (minor + dy <= 16)
            value = strip[dy]
            at = (dz * 3 + dy) * 8
            raw[at : at + 8] = value
            normed = silu((value - group_mean) * scale + bias[...])
            active[at : at + 8] = jnp.where(inside, normed, 0.0)
    grid = active[...].astype(bf16)
    cells = jnp.dot(patch[...], grid, preferred_element_type=f32).astype(bf16)
    for t in range(TAPS):
        patches[2 * t] = cells[t * 32 : t * 32 + 32, :128]
        patches[2 * t + 1] = cells[t * 32 : t * 32 + 32, 128:]
    rest = raw[...]
    total = jnp.zeros((32, COARSE), f32)
    for _ in range(3):
        high = rest.astype(bf16)
        rest = rest - high.astype(f32)
        total += jnp.dot(plain[...], high, preferred_element_type=f32)
    core = major & 1
    contract = (((1,), (1,)), ((), ()))
    for half, base in ((near_half, core * TAPS), (far_half, (1 - core) * TAPS)):
        for t in range(TAPS):
            total += lax.dot_general(
                patches[base + t], half[:, tile(t)], contract, preferred_element_type=f32
            )
    result = total.astype(bf16)
    coarse[...] = result[0:8]
    for pos in range(8):
        lifted[pos] = jnp.dot(
            result, up[:, pos * 256 : pos * 256 + 256], preferred_element_type=f32
        )
    diagonal = channel_diagonal()

    def row_block(pos, cell):
        return jnp.where(diagonal, lifted[pos, pl.ds(cell, 1), :], 0.0).astype(bf16)

    for i in range(0, BLOCKS, 8):
        for u in range(8):
            cell, pos = place(coords, i + u)
            rows[u * CHANS : (u + 1) * CHANS] = row_block(pos, cell)
        term = jnp.dot(rows[...], spread[...], preferred_element_type=f32)
        base = level[i : i + 8].reshape(8 * CHANS, VOXELS).astype(f32)
        merged = (base + term).astype(bf16)
        joined[i : i + 8] = merged.reshape(8, CHANS, VOXELS)
        signal[i : i + 8] = silu(merged.astype(f32)).astype(bf16).reshape(8, CHANS, VOXELS)
    signal[BLOCKS] = jnp.zeros((CHANS, VOXELS), bf16)
    take_faces(signal, faces, y_bank, z_bank)
    zero = jnp.zeros((CHANS, 128), bf16)
    y_bank[BLOCKS] = zero
    z_bank[BLOCKS] = zero
    kinds = (
        (r0, y_bank, 33, 12, y_spread, 96, 4, 0, 2),
        (r1, y_bank, 49, 8, y_spread, 96, 4, 1, 2),
        (r2, z_bank, 33, 20, z_spread, 64, 2, 0, 4),
        (r3, z_bank, 49, 16, z_spread, 64, 2, 1, 4),
    )
    for plane, bank, entry, first, expand, back, stride, far, edge in kinds:
        for i in range(0, 16, 8):
            for u in range(8):
                p = i + u
                a, x = p // 4, p % 4
                pos = a % 2 * stride + far * edge + x % 2
                cell = first + a // 2 * 2 + x // 2
                rows[u * CHANS : (u + 1) * CHANS] = jnp.where(
                    diagonal, lifted[pos, cell : cell + 1, :], 0.0
                ).astype(bf16)
            term = jnp.dot(rows[...], expand[...], preferred_element_type=f32)
            for u in range(8):
                face = received(plane, i + u, back).astype(f32)
                merged = (face + term[u * CHANS : (u + 1) * CHANS]).astype(bf16)
                bank[entry + i + u] = silu(merged.astype(f32)).astype(bf16)

    def finish(j, value):
        out = (joined[j].astype(f32) + value).astype(bf16)
        second[j] = out
        signal2[j] = silu(out.astype(f32)).astype(bf16)

    convolve(coords, links, signal, y_bank, z_bank, weight, taps, finish)
    take_faces(signal2, faces, y_own, z_own)
    fill_planes(coords, counts, y_own, z_own, work, (p0, p1, p2, p3))


def third_conv(
    coords, counts, links, second, signal_in, y_own, z_own, r0, r1, r2, r3, weight,
    out, signal, y_bank, z_bank, taps,
):
    signal[0:BLOCKS] = signal_in[...]
    signal[BLOCKS] = jnp.zeros((CHANS, VOXELS), bf16)
    y_bank[0:BLOCKS] = y_own[...]
    z_bank[0:BLOCKS] = z_own[...]
    bank_received((r0, r1, r2, r3), y_bank, z_bank)

    def finish(j, result):
        value = second[j].astype(f32) + result
        out[j] = jnp.where(j < counts[0], value, 0.0).astype(bf16)

    convolve(coords, links, signal, y_bank, z_bank, weight, taps, finish)


def call(kernel, scalars, arrays, outs, scratch, mebibytes):
    smem = pl.BlockSpec(memory_space=pltpu.SMEM)
    vmem = pl.BlockSpec(memory_space=pltpu.VMEM)
    return pl.pallas_call(
        kernel,
        in_specs=[smem] * len(scalars) + [vmem] * len(arrays),
        out_specs=[vmem] * len(outs),
        out_shape=[jax.ShapeDtypeStruct(s, d) for s, d in outs],
        scratch_shapes=[pltpu.VMEM(s, d) for s, d in scratch],
        compiler_params=pltpu.CompilerParams(vmem_limit_bytes=mebibytes << 20),
    )(*scalars, *arrays)


FIELD = ((BLOCKS, CHANS, VOXELS), bf16)
FACES = ((BLOCKS, CHANS, 128), bf16)
PLANE = ((8, CHANS, 128), bf16)
SIGNAL = ((BLOCKS + 1, CHANS, VOXELS), bf16)
BANK = ((BLOCKS + 33, CHANS, 128), bf16)
TAP_STACK = ((4, 7 * CHANS, VOXELS), bf16)
WORK = ((4, 9, CHANS, 128), bf16)


def shifted(x, axes, step):
    count = lax.axis_size(axes)
    return lax.ppermute(x, axes, [(i, (i + step) % count) for i in range(count)])


def swap_planes(planes):
    y_low, y_high, z_low, z_high = planes
    return (
        shifted(y_low, MY, -1),
        shifted(y_high, MY, 1),
        shifted(z_low, MX, -1),
        shifted(z_high, MX, 1),
    )


def local(
    features, coords, counts, neighbours, fine_weights, down_weight, up_weight, norm_gain, norm_bias,
    coarse_weight,
):
    faces, pool, spread, y_spread, z_spread, patch, plain = map(jnp.asarray, tables())
    major = lax.axis_index(MX)
    minor = lax.axis_index(MY)
    where = jnp.stack([major, minor]).astype(jnp.int32)
    part = lax.dynamic_slice_in_dim(
        coarse_weight.T, lax.axis_index("mx_1") * HALF_ROWS, HALF_ROWS, 1
    )
    near_half = lax.all_gather(part, MY, axis=0, tiled=True)
    far_half = lax.ppermute(near_half, "mx_1", [(0, 1), (1, 0)])

    signal, y_own, z_own, *planes = call(
        first_faces, (coords, counts), (features, faces),
        (FIELD, FACES, FACES) + (PLANE,) * 4, (WORK,), 16,
    )
    planes = swap_planes(planes)
    level, *planes, message = call(
        first_conv, (coords, counts, neighbours),
        (features, signal, y_own, z_own, *planes, fine_weights[0], faces, pool, down_weight),
        (FIELD,) + (PLANE,) * 4 + (((16, 16, COARSE), f32),),
        (SIGNAL, BANK, BANK, TAP_STACK, WORK, ((9, 16, COARSE), f32)), 24,
    )
    message = lax.all_to_all(message, MY, 0, 0)
    partial, strip = call(
        row_sums, (where,), (message,),
        (((16, 8, COARSE), f32), ((3, 8, COARSE), f32)), (), 8,
    )
    strip_low = shifted(strip, MX, 1)
    strip_high = shifted(strip, MX, -1)
    planes = swap_planes(planes)
    partial = lax.all_to_all(partial, MX, 0, 0)
    second, signal, y_own, z_own, *planes, coarse = call(
        second_conv, (coords, counts, neighbours, where),
        (level, *planes, partial, strip_low, strip, strip_high, near_half, far_half,
         norm_gain.reshape(1, COARSE), norm_bias.reshape(1, COARSE), up_weight, fine_weights[1],
         faces, spread, y_spread, z_spread, patch, plain),
        (FIELD, FIELD, FACES, FACES) + (PLANE,) * 4 + (((8, COARSE), bf16),),
        (FIELD, SIGNAL, BANK, BANK, TAP_STACK, WORK, ((128, COARSE), f32), ((128, COARSE), f32),
         ((2 * TAPS, 32, 128), bf16), ((8, 32, COARSE), f32), ((256, 256), bf16)), 32,
    )
    planes = swap_planes(planes)
    (fine_out,) = call(
        third_conv, (coords, counts, neighbours),
        (second, signal, y_own, z_own, *planes, fine_weights[2]),
        (FIELD,), (SIGNAL, BANK, BANK, TAP_STACK), 24,
    )
    return fine_out, coarse.reshape(2, 2, 2, COARSE)


def solution(mesh):
    split = Mesh(mesh.devices.reshape(8, 2, 4, 4), ("mx_0", "mx_1", "my_0", "my_1"))
    placed = (
        P(MX_MY, None, None), P(None, MX_MY), P(MX_MY), P(None, MX_MY),
        P(), P(), P(), P(), P(), P(None, MY),
    )
    return jax.shard_map(
        local,
        mesh=split,
        in_specs=placed,
        out_specs=(P(MX_MY, None, None), P(MX, MY, None, None)),
        check_vma=False,
    )
```

```python
import functools

import jax
import jax.numpy as jnp
import ml_dtypes
import numpy as np
from jax import lax
from jax.experimental import pallas as pl
from jax.experimental.pallas import tpu as pltpu
from jax.sharding import Mesh
from jax.sharding import PartitionSpec as P

MX = ("mx_0", "mx_1")
MY = ("my_0", "my_1")
MX_MY = MX + MY
BLOCKS = 32
CHANS = 32
VOXELS = 512
COARSE = 256
GROUP = 8
TAPS = 27
HALF_ROWS = TAPS * COARSE // 2
NORM_EPS = 1e-05
bf16 = jnp.bfloat16
f32 = jnp.float32


def octant(z, y, x):
    return z // 4 * 4 + y // 4 * 2 + x // 4


def voxel_zyx():
    voxel = np.arange(VOXELS)
    return voxel // 64, voxel // 8 % 8, voxel % 8


@functools.cache
def tables():
    z, y, x = voxel_zyx()
    voxel = np.arange(VOXELS)
    faces = np.zeros((VOXELS, 256), np.float32)
    y_lane = z % 2 * 64 + z // 2 * 8 + x
    faces[voxel[y == 0], y_lane[y == 0]] = 1
    faces[voxel[y == 7], y_lane[y == 7] + 32] = 1
    z_lane = y * 8 + x
    faces[voxel[z == 0], 128 + 64 + z_lane[z == 0]] = 1
    faces[voxel[z == 7], 128 + z_lane[z == 7]] = 1
    own = np.arange(256) // 32
    pool = (octant(z, y, x)[:, None] == own[None, :]).astype(np.float32) / 64
    spread = (own[:, None] == octant(z, y, x)[None, :]).astype(np.float32)
    lane = np.arange(128)
    y_octant = octant(lane % 32 // 8 * 2 + lane // 64, lane // 32 % 2 * 4, lane % 8)
    z_octant = octant((lane < 64) * 4, lane % 64 // 8, lane % 8)
    y_spread = (own[:, None] == y_octant[None, :]).astype(np.float32)
    z_spread = (own[:, None] == z_octant[None, :]).astype(np.float32)
    cells = [(a, b, c) for a in range(2) for b in range(2) for c in range(2)]
    cells += [(a, b, c) for b in (-1, 2) for a in range(2) for c in range(2)]
    cells += [(a, b, c) for a in (-1, 2) for b in range(2) for c in range(2)]

    def row_of(a, b, c):
        part = (a // 2 + 1) * 3 + b // 2 + 1
        return part * 8 + a % 2 * 4 + b % 2 * 2 + c

    patch = np.zeros((TAPS, 32, 128), np.float32)
    plain = np.zeros((32, 128), np.float32)
    for i, (a, b, c) in enumerate(cells):
        plain[i, row_of(a, b, c)] = 1
        for t in range(TAPS):
            near = (a + t // 9 - 1, b + t // 3 % 3 - 1, c + t % 3 - 1)
            if 0 <= near[2] < 2:
                patch[t, i, row_of(*near)] = 1
    kinds = (faces, pool, spread, y_spread, z_spread, patch.reshape(TAPS * 32, 128), plain)
    return tuple(k.astype(ml_dtypes.bfloat16) for k in kinds)


def lanes():
    return lax.broadcasted_iota(jnp.int32, (CHANS, 128), 1)


def silu(x):
    return x * (1.0 / (1.0 + jnp.exp(-x)))


def tile(k):
    return slice(k * 128, k * 128 + 128)


def take_faces(signal, faces_ref, y_bank, z_bank):
    for i in range(0, BLOCKS, 8):
        block = signal[i : i + 8].reshape(8 * CHANS, VOXELS)
        packed = jnp.dot(block, faces_ref[...], preferred_element_type=f32).astype(bf16)
        y_bank[i : i + 8] = packed[:, :128].reshape(8, CHANS, 128)
        z_bank[i : i + 8] = packed[:, 128:].reshape(8, CHANS, 128)


def fill_planes(coords, counts, y_bank, z_bank, work, outs):
    lane = lanes()
    work[...] = jnp.zeros_like(work)
    in_low = (lane & 32) == 0
    in_back = lane >= 64

    def one(j, carry):
        live = j < counts[0]
        z, y, x = coords[0, j] & 3, coords[1, j] & 3, coords[2, j]
        odd = (x & 1) == 1
        y_row, z_row = (z * 4 + x) >> 1, (y * 4 + x) >> 1
        face = y_bank[j]
        turned = pltpu.roll(face, 32, 1)
        value = jnp.where(odd, turned, face)
        for plane, edge, low in ((0, 0, True), (1, 3, False)):
            row = jnp.where(live & (y == edge), y_row, 8)
            mask = jnp.logical_xor(in_low if low else jnp.logical_not(in_low), odd)
            work[plane, row] = jnp.where(mask, value, work[plane, row])
        face = z_bank[j]
        turned = pltpu.roll(face, 64, 1)
        value = jnp.where(odd, turned, face)
        for plane, edge, low in ((2, 0, True), (3, 3, False)):
            row = jnp.where(live & (z == edge), z_row, 8)
            mask = jnp.logical_xor(in_back if low else jnp.logical_not(in_back), odd)
            work[plane, row] = jnp.where(mask, value, work[plane, row])
        return carry

    lax.fori_loop(0, BLOCKS, one, 0, unroll=4)
    for plane, out in enumerate(outs):
        out[...] = work[plane, :8]


def received(plane_ref, p, back):
    row = plane_ref[p // 2]
    return pltpu.roll(row, back, 1) if p % 2 else row


def bank_received(planes, y_bank, z_bank):
    zero = jnp.zeros((CHANS, 128), bf16)
    y_bank[BLOCKS] = zero
    z_bank[BLOCKS] = zero
    for p in range(16):
        y_bank[33 + p] = received(planes[0], p, 96)
        y_bank[49 + p] = received(planes[1], p, 96)
        z_bank[33 + p] = received(planes[2], p, 64)
        z_bank[49 + p] = received(planes[3], p, 64)


def convolve(coords, links, signal, y_bank, z_bank, weight, taps, finish):
    lane = lanes()
    along_x = lane & 7
    along_yx = lane & 63
    front = lane < 64

    def build(j, slot):
        z, y, x = coords[0, j] & 3, coords[1, j] & 3, coords[2, j]
        y_pos, z_pos = z * 4 + x, y * 4 + x

        def near(direction, inside, remote):
            link = links[direction, j]
            here = link & (BLOCKS - 1)
            if inside is not None:
                here = jnp.where(inside, here, remote)
            return jnp.where(link < 0, BLOCKS, here)

        x_up, x_down = near(0, None, None), near(1, None, None)
        y_up = y_bank[near(2, y < 3, 33 + y_pos)]
        y_down = y_bank[near(3, y > 0, 49 + y_pos)]
        z_up = z_bank[near(4, z < 3, 33 + z_pos)]
        z_down = z_bank[near(5, z > 0, 49 + z_pos)]
        own = [signal[j, :, tile(k)] for k in range(4)]
        half = [z_down] + [pltpu.roll(own[k], 64, 1) for k in range(4)] + [z_up]
        for k in range(4):
            to = tile(k)
            taps[slot, 0:32, to] = own[k]
            taps[slot, 32:64, to] = jnp.where(
                along_x == 7,
                pltpu.roll(signal[x_up, :, to], 7, 1),
                pltpu.roll(own[k], 127, 1),
            )
            taps[slot, 64:96, to] = jnp.where(
                along_x == 0,
                pltpu.roll(signal[x_down, :, to], 121, 1),
                pltpu.roll(own[k], 1, 1),
            )
            taps[slot, 96:128, to] = jnp.where(
                along_yx >= 56, pltpu.roll(y_up, 56 - 8 * k, 1), pltpu.roll(own[k], 120, 1)
            )
            taps[slot, 128:160, to] = jnp.where(
                along_yx < 8, pltpu.roll(y_down, 96 - 8 * k, 1), pltpu.roll(own[k], 8, 1)
            )
            taps[slot, 160:192, to] = jnp.where(front, half[k + 1], half[k + 2])
            taps[slot, 192:224, to] = jnp.where(front, half[k], half[k + 1])

    def some(i, carry):
        for u in range(4):
            build(i * 4 + u, u)
        for u in range(4):
            result = jnp.dot(weight[...], taps[u], preferred_element_type=f32)
            finish(i * 4 + u, result)
        return carry

    lax.fori_loop(0, BLOCKS // 4, some, 0)


def first_faces(ins, outs, work):
    features, faces, coords, counts = ins
    signal, y_own, z_own, *planes = outs
    base = features.get()

    def one(j, carry):
        signal.ref[j] = silu(base[j].astype(f32)).astype(bf16)
        return carry

    lax.fori_loop(0, BLOCKS, one, 0, unroll=4)
    signal.send()
    take_faces(signal.ref, faces.get(), y_own.ref, z_own.ref)
    y_own.send()
    z_own.send()
    fill_planes(coords.get(), counts.get(), y_own.ref, z_own.ref, work, [p.ref for p in planes])


def first_conv(ins, outs, signal, y_bank, z_bank, taps, work, gathered):
    (coords, counts, links, weights, signal_in, y_own, z_own, *planes, features, faces, pool, down) = ins
    level, *sent, message = outs
    coords, counts, links, weight = coords.get(), counts.get(), links.get(), weights.get().at[0]
    signal[BLOCKS] = jnp.zeros((CHANS, VOXELS), bf16)
    bank_received([p.get() for p in planes], y_bank, z_bank)
    for one in (signal_in, y_own, z_own):
        one.get()
    base = features.get()
    level_ref = level.ref

    def finish(j, result):
        level_ref[j] = (base[j].astype(f32) + result).astype(bf16)

    convolve(coords, links, signal, y_bank, z_bank, weight, taps, finish)
    level.send()
    gathered[...] = jnp.zeros_like(gathered)
    diagonal = channel_diagonal()
    mean_of = pool.get()
    for i in range(0, BLOCKS, 8):
        block = level_ref[i : i + 8].reshape(8 * CHANS, VOXELS)
        means = jnp.dot(block, mean_of[...], preferred_element_type=f32)
        for u in range(8):
            j = i + u
            part = jnp.where(diagonal, means[u * CHANS : (u + 1) * CHANS], 0.0)
            cell, pos = place(coords, j)
            pos = jnp.where(j < counts[0], pos, 8)
            gathered[pos, pl.ds(cell, 1), :] = jnp.sum(part, axis=0, keepdims=True)
    total = jnp.zeros((16, COARSE), f32)
    rows = down.get()
    for pos in range(8):
        total += jnp.dot(
            gathered[pos].astype(bf16), rows[pos * 256 : pos * 256 + 256], preferred_element_type=f32
        )
    total = total[:8]
    mean = jnp.mean(total, axis=0, keepdims=True)
    spread = jnp.sum((total - mean) * (total - mean), axis=0, keepdims=True)
    row = lax.broadcasted_iota(jnp.int32, (8, COARSE), 0)
    extra = jnp.where(row == 0, mean, jnp.where(row == 1, spread, 0.0))
    for i in range(16):
        message.ref[i, 0:8] = total
        message.ref[i, 8:16] = extra
    message.send()
    take_faces(level_ref, faces.get(), y_bank, z_bank)
    fill_planes(coords, counts, y_bank, z_bank, work, [p.ref for p in sent])


def channel_diagonal():
    channel = lax.broadcasted_iota(jnp.int32, (CHANS, 256), 0)
    return channel == (lax.broadcasted_iota(jnp.int32, (CHANS, 256), 1) & 31)


def place(coords, j):
    z, y, x = coords[0, j] & 3, coords[1, j] & 3, coords[2, j]
    cell = (z >> 1) * 4 + (y >> 1) * 2 + (x >> 1)
    return cell, (z & 1) * 4 + (y & 1) * 2 + (x & 1)


def merged_sums(means, spreads, entries):
    mean = jnp.mean(means, axis=0, keepdims=True)
    away = means - mean
    return mean, jnp.sum(spreads + entries * away * away, axis=0, keepdims=True)


def row_sums(ins, outs):
    where, message = (one.get() for one in ins)
    partial, strip = (one.ref for one in outs)
    mean, spread = merged_sums(message[:, 8, :], message[:, 9, :], 8.0)
    row = lax.broadcasted_iota(jnp.int32, (8, COARSE), 0)
    both = jnp.where(row == 0, mean, jnp.where(row == 1, spread, 0.0))
    for i in range(16):
        partial[i] = both
    minor = where[1]
    for step in range(3):
        strip[step] = message[jnp.clip(minor + step - 1, 0, 15), 0:8]


def group_total(x):
    lane = lax.broadcasted_iota(jnp.int32, x.shape, 1)
    for width in (1, 2, 4):
        x = x + jnp.where(
            (lane & width) == 0, pltpu.roll(x, COARSE - width, 1), pltpu.roll(x, width, 1)
        )
    return x


def second_conv(
    ins, outs, joined, signal, y_bank, z_bank, taps, work, active, raw, patches, lifted, rows
):
    (where, partial, s_low, s_own, s_high, gain, bias, patch, plain, near_half, far_half, up, coords,
     counts, links, weights, spread, level, faces, y_spread, z_spread, *planes) = ins
    second, signal2, y_own, z_own, *sent, coarse = outs
    where, partial = where.get(), partial.get()
    major, minor = where[0], where[1]
    mean, spread_sum = merged_sums(partial[:, 0, :], partial[:, 1, :], 128.0)
    group_mean = group_total(mean) * (1.0 / GROUP)
    away = mean - group_mean
    variance = group_total(spread_sum + 2048.0 * away * away) * (1.0 / (2048 * GROUP))
    gain, bias = gain.get(), bias.get()
    scale = gain[...] / jnp.sqrt(variance + NORM_EPS)
    active[...] = jnp.zeros_like(active)
    raw[...] = jnp.zeros_like(raw)
    for dz, strip in enumerate((s_low.get(), s_own.get(), s_high.get())):
        inside_z = (major + dz >= 1) & (major + dz <= 16)
        for dy in range(3):
            inside = inside_z & (minor + dy >= 1) & (minor + dy <= 16)
            value = strip[dy]
            at = (dz * 3 + dy) * 8
            raw[at : at + 8] = value
            normed = silu((value - group_mean) * scale + bias[...])
            active[at : at + 8] = jnp.where(inside, normed, 0.0)
    grid = active[...].astype(bf16)
    cells = jnp.dot(patch.get()[...], grid, preferred_element_type=f32).astype(bf16)
    for t in range(TAPS):
        patches[2 * t] = cells[t * 32 : t * 32 + 32, :128]
        patches[2 * t + 1] = cells[t * 32 : t * 32 + 32, 128:]
    rest = raw[...]
    plain = plain.get()
    total = jnp.zeros((32, COARSE), f32)
    for _ in range(3):
        high = rest.astype(bf16)
        rest = rest - high.astype(f32)
        total += jnp.dot(plain[...], high, preferred_element_type=f32)
    core = major & 1
    contract = (((1,), (1,)), ((), ()))
    for half, base in ((near_half, core * TAPS), (far_half, (1 - core) * TAPS)):
        half = half.get()
        for t in range(TAPS):
            total += lax.dot_general(
                patches[base + t], half[:, tile(t)], contract, preferred_element_type=f32
            )
    result = total.astype(bf16)
    coarse.ref[...] = result[0:8]
    up = up.get()
    for pos in range(8):
        lifted[pos] = jnp.dot(
            result, up[:, pos * 256 : pos * 256 + 256], preferred_element_type=f32
        )
    diagonal = channel_diagonal()
    coords, counts, links, weight = coords.get(), counts.get(), links.get(), weights.get().at[1]
    spread, level, faces = spread.get(), level.get(), faces.get()
    y_spread, z_spread = y_spread.get(), z_spread.get()
    r0, r1, r2, r3 = (p.get() for p in planes)

    def row_block(pos, cell):
        return jnp.where(diagonal, lifted[pos, pl.ds(cell, 1), :], 0.0).astype(bf16)

    for i in range(0, BLOCKS, 8):
        for u in range(8):
            cell, pos = place(coords, i + u)
            rows[u * CHANS : (u + 1) * CHANS] = row_block(pos, cell)
        term = jnp.dot(rows[...], spread[...], preferred_element_type=f32)
        base = level[i : i + 8].reshape(8 * CHANS, VOXELS).astype(f32)
        merged = (base + term).astype(bf16)
        joined[i : i + 8] = merged.reshape(8, CHANS, VOXELS)
        signal[i : i + 8] = silu(merged.astype(f32)).astype(bf16).reshape(8, CHANS, VOXELS)
    signal[BLOCKS] = jnp.zeros((CHANS, VOXELS), bf16)
    take_faces(signal, faces, y_bank, z_bank)
    zero = jnp.zeros((CHANS, 128), bf16)
    y_bank[BLOCKS] = zero
    z_bank[BLOCKS] = zero
    kinds = (
        (r0, y_bank, 33, 12, y_spread, 96, 4, 0, 2),
        (r1, y_bank, 49, 8, y_spread, 96, 4, 1, 2),
        (r2, z_bank, 33, 20, z_spread, 64, 2, 0, 4),
        (r3, z_bank, 49, 16, z_spread, 64, 2, 1, 4),
    )
    for plane, bank, entry, first, expand, back, stride, far, edge in kinds:
        for i in range(0, 16, 8):
            for u in range(8):
                p = i + u
                a, x = p // 4, p % 4
                pos = a % 2 * stride + far * edge + x % 2
                cell = first + a // 2 * 2 + x // 2
                rows[u * CHANS : (u + 1) * CHANS] = jnp.where(
                    diagonal, lifted[pos, cell : cell + 1, :], 0.0
                ).astype(bf16)
            term = jnp.dot(rows[...], expand[...], preferred_element_type=f32)
            for u in range(8):
                face = received(plane, i + u, back).astype(f32)
                merged = (face + term[u * CHANS : (u + 1) * CHANS]).astype(bf16)
                bank[entry + i + u] = silu(merged.astype(f32)).astype(bf16)

    second_ref, signal2_ref = second.ref, signal2.ref

    def finish(j, value):
        out = (joined[j].astype(f32) + value).astype(bf16)
        second_ref[j] = out
        signal2_ref[j] = silu(out.astype(f32)).astype(bf16)

    convolve(coords, links, signal, y_bank, z_bank, weight, taps, finish)
    second.send()
    signal2.send()
    take_faces(signal2_ref, faces, y_own.ref, z_own.ref)
    y_own.send()
    z_own.send()
    fill_planes(coords, counts, y_own.ref, z_own.ref, work, [p.ref for p in sent])


def third_conv(ins, outs, signal, y_bank, z_bank, taps):
    (coords, counts, links, weights, signal_in, y_own, z_own, *planes, second) = ins
    coords, counts, links, weight = coords.get(), counts.get(), links.get(), weights.get().at[2]
    signal[BLOCKS] = jnp.zeros((CHANS, VOXELS), bf16)
    bank_received([p.get() for p in planes], y_bank, z_bank)
    for one in (signal_in, y_own, z_own):
        one.get()
    base = second.get()
    out = outs[0].ref

    def finish(j, result):
        value = base[j].astype(f32) + result
        out[j] = jnp.where(j < counts[0], value, 0.0).astype(bf16)

    convolve(coords, links, signal, y_bank, z_bank, weight, taps, finish)


class Arriving:
    def __init__(self, copy, ref):
        self.copy, self.ref = copy, ref
        copy.start()

    def get(self):
        if self.copy is not None:
            self.copy.wait()
            self.copy = None
        return self.ref


class Leaving:
    def __init__(self, copy, ref):
        self.copy, self.ref, self.sent = copy, ref, False

    def send(self):
        self.copy.start()
        self.sent = True


def call(kernel, arrays, outs, scratch, microseconds, spare=()):
    own = [(i, to) for i, (_, to) in enumerate(arrays) if to is None or to == "smem"]
    count, total = len(arrays), len(arrays) + len(spare)

    def body(*refs):
        ins, results = refs[:count], refs[total : total + len(outs)]
        rest = refs[total + len(outs) :]
        buffers, rest = rest[: len(own)], rest[len(own) :]
        staged, rest = rest[: len(outs)], rest[len(outs) :]
        work, (in_sem, out_sem) = rest[:-2], rest[-2:]
        placed = {i: buffer for (i, _), buffer in zip(own, buffers)}
        arriving = []
        for i, (_, to) in enumerate(arrays):
            ref = placed[i] if i in placed else to(*work)
            arriving.append(Arriving(pltpu.make_async_copy(ins[i], ref, in_sem.at[i]), ref))
        leaving = [
            Leaving(pltpu.make_async_copy(staged[i], results[i], out_sem.at[i]), staged[i])
            for i in range(len(outs))
        ]
        kernel(arriving, leaving, *work)
        for one in arriving:
            one.get()
        for one in leaving:
            if not one.sent:
                one.send()
        for one in leaving:
            one.copy.wait()

    hbm = pl.BlockSpec(memory_space=pltpu.HBM)
    spaces = {None: pltpu.VMEM, "smem": pltpu.SMEM}
    buffers = [spaces[to](arrays[i][0].shape, arrays[i][0].dtype) for i, to in own]
    buffers += [pltpu.VMEM(s, d) for s, d in (*outs, *scratch)]
    return pl.pallas_call(
        body,
        in_specs=[hbm] * total,
        out_specs=[hbm] * len(outs),
        out_shape=[jax.ShapeDtypeStruct(s, d) for s, d in outs],
        scratch_shapes=buffers
        + [pltpu.SemaphoreType.DMA((count,)), pltpu.SemaphoreType.DMA((len(outs),))],
        compiler_params=pltpu.CompilerParams(vmem_limit_bytes=60 << 20),
        cost_estimate=pl.CostEstimate(
            flops=microseconds * 1_000_000_000,
            bytes_accessed=microseconds * 3_000_000,
            transcendentals=0,
        ),
    )(*[a for a, _ in arrays], *spare)


FIELD = ((BLOCKS, CHANS, VOXELS), bf16)
FACES = ((BLOCKS, CHANS, 128), bf16)
PLANE = ((8, CHANS, 128), bf16)
SIGNAL = ((BLOCKS + 1, CHANS, VOXELS), bf16)
BANK = ((BLOCKS + 33, CHANS, 128), bf16)
TAP_STACK = ((4, 7 * CHANS, VOXELS), bf16)
WORK = ((4, 9, CHANS, 128), bf16)


def shifted(x, axes, step):
    count = lax.axis_size(axes)
    return lax.ppermute(x, axes, [(i, (i + step) % count) for i in range(count)])


def swap_planes(planes):
    y_low, y_high, z_low, z_high = planes
    return (
        shifted(y_low, MY, -1),
        shifted(y_high, MY, 1),
        shifted(z_low, MX, -1),
        shifted(z_high, MX, 1),
    )


def local(
    features, coords, counts, neighbours, fine_weights, down_weight, up_weight, norm_gain, norm_bias,
    coarse_weight,
):
    faces, pool, spread, y_spread, z_spread, patch, plain = map(jnp.asarray, tables())
    major = lax.axis_index(MX)
    minor = lax.axis_index(MY)
    where = jnp.stack([major, minor]).astype(jnp.int32)
    part = lax.dynamic_slice_in_dim(
        coarse_weight.T, lax.axis_index("mx_1") * HALF_ROWS, HALF_ROWS, 1
    )
    near_half = lax.all_gather(part, MY, axis=0, tiled=True)

    def plainly(*arrays):
        return tuple((x, None) for x in arrays)

    live = ((coords, "smem"), (counts, "smem"), (neighbours, "smem"))
    place_own = (
        lambda signal, *rest: signal.at[0:BLOCKS],
        lambda signal, y_bank, *rest: y_bank.at[0:BLOCKS],
        lambda signal, y_bank, z_bank, *rest: z_bank.at[0:BLOCKS],
    )
    *own, low_y, high_y, low_z, high_z = call(
        first_faces, (*plainly(features, faces), *live[:2]),
        (FIELD, FACES, FACES) + (PLANE,) * 4, (WORK,), 3,
    )
    planes = swap_planes((low_y, high_y, low_z, high_z))
    level, *planes, message = call(
        first_conv,
        (*live, (fine_weights, None), *zip(own, place_own), *plainly(*planes, features, faces, pool, down_weight)),
        (FIELD,) + (PLANE,) * 4 + (((16, 16, COARSE), f32),),
        (SIGNAL, BANK, BANK, TAP_STACK, WORK, ((9, 16, COARSE), f32)), 9,
    )
    message = lax.all_to_all(message, MY, 0, 0)
    planes = swap_planes(planes)
    partial, strip = call(
        row_sums, ((where, "smem"), (message, None)),
        (((16, 8, COARSE), f32), ((3, 8, COARSE), f32)), (), 1, planes,
    )
    partial = lax.all_to_all(partial, MX, 0, 0)
    strip_low = shifted(strip, MX, 1)
    strip_high = shifted(strip, MX, -1)
    near_half, strip_low = lax.optimization_barrier((near_half, strip_low))
    far_half = lax.ppermute(near_half, "mx_1", [(0, 1), (1, 0)])
    second, *own, low_y, high_y, low_z, high_z, coarse = call(
        second_conv,
        ((where, "smem"),
         *plainly(partial, strip_low, strip, strip_high, norm_gain.reshape(1, COARSE),
                  norm_bias.reshape(1, COARSE), patch, plain, near_half, far_half, up_weight),
         *live, *plainly(fine_weights, spread, level, faces, y_spread, z_spread, *planes)),
        (FIELD, FIELD, FACES, FACES) + (PLANE,) * 4 + (((8, COARSE), bf16),),
        (FIELD, SIGNAL, BANK, BANK, TAP_STACK, WORK, ((128, COARSE), f32), ((128, COARSE), f32),
         ((2 * TAPS, 32, 128), bf16), ((8, 32, COARSE), f32), ((256, 256), bf16)), 14,
    )
    planes = swap_planes((low_y, high_y, low_z, high_z))
    (fine_out,) = call(
        third_conv, (*live, (fine_weights, None), *zip(own, place_own), *plainly(*planes, second)),
        (FIELD,), (SIGNAL, BANK, BANK, TAP_STACK), 7,
    )
    return fine_out, coarse.reshape(2, 2, 2, COARSE)


def solution(mesh):
    split = Mesh(mesh.devices.reshape(8, 2, 4, 4), ("mx_0", "mx_1", "my_0", "my_1"))
    placed = (
        P(MX_MY, None, None), P(None, MX_MY), P(MX_MY), P(None, MX_MY),
        P(), P(), P(), P(), P(), P(None, MY),
    )
    return jax.shard_map(
        local,
        mesh=split,
        in_specs=placed,
        out_specs=(P(MX_MY, None, None), P(MX, MY, None, None)),
        check_vma=False,
    )
```

```python
import functools

import jax
import jax.numpy as jnp
import ml_dtypes
import numpy as np
from jax import lax
from jax.experimental import pallas as pl
from jax.experimental.pallas import tpu as pltpu
from jax.sharding import Mesh
from jax.sharding import PartitionSpec as P

MX = ("mx_0", "mx_1")
MY = ("my_0", "my_1")
MX_MY = MX + MY
BLOCKS = 32
CHANS = 32
VOXELS = 512
COARSE = 256
GROUP = 8
TAPS = 27
HALF_ROWS = TAPS * COARSE // 2
NORM_EPS = 1e-05
bf16 = jnp.bfloat16
f32 = jnp.float32


def octant(z, y, x):
    return z // 4 * 4 + y // 4 * 2 + x // 4


def voxel_zyx():
    voxel = np.arange(VOXELS)
    return voxel // 64, voxel // 8 % 8, voxel % 8


@functools.cache
def tables():
    z, y, x = voxel_zyx()
    voxel = np.arange(VOXELS)
    faces = np.zeros((VOXELS, 256), np.float32)
    y_lane = z % 2 * 64 + z // 2 * 8 + x
    faces[voxel[y == 0], y_lane[y == 0]] = 1
    faces[voxel[y == 7], y_lane[y == 7] + 32] = 1
    z_lane = y * 8 + x
    faces[voxel[z == 0], 128 + 64 + z_lane[z == 0]] = 1
    faces[voxel[z == 7], 128 + z_lane[z == 7]] = 1
    own = np.arange(256) // 32
    pool = (octant(z, y, x)[:, None] == own[None, :]).astype(np.float32) / 64
    spread = (own[:, None] == octant(z, y, x)[None, :]).astype(np.float32)
    lane = np.arange(128)
    y_octant = octant(lane % 32 // 8 * 2 + lane // 64, lane // 32 % 2 * 4, lane % 8)
    z_octant = octant((lane < 64) * 4, lane % 64 // 8, lane % 8)
    y_spread = (own[:, None] == y_octant[None, :]).astype(np.float32)
    z_spread = (own[:, None] == z_octant[None, :]).astype(np.float32)
    cells = [(a, b, c) for a in range(2) for b in range(2) for c in range(2)]
    cells += [(a, b, c) for b in (-1, 2) for a in range(2) for c in range(2)]
    cells += [(a, b, c) for a in (-1, 2) for b in range(2) for c in range(2)]

    def row_of(a, b, c):
        part = (a // 2 + 1) * 3 + b // 2 + 1
        return part * 8 + a % 2 * 4 + b % 2 * 2 + c

    patch = np.zeros((TAPS, 32, 128), np.float32)
    plain = np.zeros((32, 128), np.float32)
    for i, (a, b, c) in enumerate(cells):
        plain[i, row_of(a, b, c)] = 1
        for t in range(TAPS):
            near = (a + t // 9 - 1, b + t // 3 % 3 - 1, c + t % 3 - 1)
            if 0 <= near[2] < 2:
                patch[t, i, row_of(*near)] = 1
    kinds = (faces, pool, spread, y_spread, z_spread, patch.reshape(TAPS * 32, 128), plain)
    return tuple(k.astype(ml_dtypes.bfloat16) for k in kinds)


def lanes():
    return lax.broadcasted_iota(jnp.int32, (CHANS, 128), 1)


def silu(x):
    return x * (1.0 / (1.0 + jnp.exp(-x)))


def tile(k):
    return slice(k * 128, k * 128 + 128)


def take_faces(signal, faces_ref, y_bank, z_bank):
    for i in range(0, BLOCKS, 8):
        block = signal[i : i + 8].reshape(8 * CHANS, VOXELS)
        packed = jnp.dot(block, faces_ref[...], preferred_element_type=f32).astype(bf16)
        y_bank[i : i + 8] = packed[:, :128].reshape(8, CHANS, 128)
        z_bank[i : i + 8] = packed[:, 128:].reshape(8, CHANS, 128)


def fill_planes(coords, counts, y_bank, z_bank, work, outs):
    lane = lanes()
    work[...] = jnp.zeros_like(work)
    in_low = (lane & 32) == 0
    in_back = lane >= 64

    def one(j, carry):
        live = j < counts[0]
        z, y, x = coords[0, j] & 3, coords[1, j] & 3, coords[2, j]
        odd = (x & 1) == 1
        y_row, z_row = (z * 4 + x) >> 1, (y * 4 + x) >> 1
        face = y_bank[j]
        turned = pltpu.roll(face, 32, 1)
        value = jnp.where(odd, turned, face)
        for plane, edge, low in ((0, 0, True), (1, 3, False)):
            row = jnp.where(live & (y == edge), y_row, 8)
            mask = jnp.logical_xor(in_low if low else jnp.logical_not(in_low), odd)
            work[plane, row] = jnp.where(mask, value, work[plane, row])
        face = z_bank[j]
        turned = pltpu.roll(face, 64, 1)
        value = jnp.where(odd, turned, face)
        for plane, edge, low in ((2, 0, True), (3, 3, False)):
            row = jnp.where(live & (z == edge), z_row, 8)
            mask = jnp.logical_xor(in_back if low else jnp.logical_not(in_back), odd)
            work[plane, row] = jnp.where(mask, value, work[plane, row])
        return carry

    lax.fori_loop(0, BLOCKS, one, 0, unroll=4)
    for plane, out in enumerate(outs):
        out[0:8] = work[plane, :8]


def received(plane_ref, p, back):
    row = plane_ref[p // 2]
    return pltpu.roll(row, back, 1) if p % 2 else row


def bank_received(planes, y_bank, z_bank):
    zero = jnp.zeros((CHANS, 128), bf16)
    y_bank[BLOCKS] = zero
    z_bank[BLOCKS] = zero
    for p in range(16):
        y_bank[33 + p] = received(planes[0], p, 96)
        y_bank[49 + p] = received(planes[1], p, 96)
        z_bank[33 + p] = received(planes[2], p, 64)
        z_bank[49 + p] = received(planes[3], p, 64)


def convolve(coords, links, signal, y_bank, z_bank, weight, taps, finish):
    lane = lanes()
    along_x = lane & 7
    along_yx = lane & 63
    front = lane < 64

    def build(j, slot):
        z, y, x = coords[0, j] & 3, coords[1, j] & 3, coords[2, j]
        y_pos, z_pos = z * 4 + x, y * 4 + x

        def near(direction, inside, remote):
            link = links[direction, j]
            here = link & (BLOCKS - 1)
            if inside is not None:
                here = jnp.where(inside, here, remote)
            return jnp.where(link < 0, BLOCKS, here)

        x_up, x_down = near(0, None, None), near(1, None, None)
        y_up = y_bank[near(2, y < 3, 33 + y_pos)]
        y_down = y_bank[near(3, y > 0, 49 + y_pos)]
        z_up = z_bank[near(4, z < 3, 33 + z_pos)]
        z_down = z_bank[near(5, z > 0, 49 + z_pos)]
        own = [signal[j, :, tile(k)] for k in range(4)]
        half = [z_down] + [pltpu.roll(own[k], 64, 1) for k in range(4)] + [z_up]
        for k in range(4):
            to = tile(k)
            taps[slot, 0:32, to] = own[k]
            taps[slot, 32:64, to] = jnp.where(
                along_x == 7,
                pltpu.roll(signal[x_up, :, to], 7, 1),
                pltpu.roll(own[k], 127, 1),
            )
            taps[slot, 64:96, to] = jnp.where(
                along_x == 0,
                pltpu.roll(signal[x_down, :, to], 121, 1),
                pltpu.roll(own[k], 1, 1),
            )
            taps[slot, 96:128, to] = jnp.where(
                along_yx >= 56, pltpu.roll(y_up, 56 - 8 * k, 1), pltpu.roll(own[k], 120, 1)
            )
            taps[slot, 128:160, to] = jnp.where(
                along_yx < 8, pltpu.roll(y_down, 96 - 8 * k, 1), pltpu.roll(own[k], 8, 1)
            )
            taps[slot, 160:192, to] = jnp.where(front, half[k + 1], half[k + 2])
            taps[slot, 192:224, to] = jnp.where(front, half[k], half[k + 1])

    def some(i, carry):
        for u in range(4):
            build(i * 4 + u, u)
        for u in range(4):
            result = jnp.dot(weight[...], taps[u], preferred_element_type=f32)
            finish(i * 4 + u, result)
        return carry

    lax.fori_loop(0, BLOCKS // 4, some, 0)


def first_faces(ins, outs, work):
    features, faces, coords, counts = ins
    y_own, z_own, *planes = outs
    base, faces = features.get(), faces.get()
    for i in range(0, BLOCKS, 8):
        block = base[i : i + 8].reshape(8 * CHANS, VOXELS)
        packed = silu(jnp.dot(block, faces[...], preferred_element_type=f32)).astype(bf16)
        y_own.ref[i : i + 8] = packed[:, :128].reshape(8, CHANS, 128)
        z_own.ref[i : i + 8] = packed[:, 128:].reshape(8, CHANS, 128)
    y_own.send()
    z_own.send()
    fill_planes(coords.get(), counts.get(), y_own.ref, z_own.ref, work, [p.ref for p in planes])


def activate(ins, outs):
    base, signal = ins[0].get(), outs[0].ref

    def one(j, carry):
        signal[j] = silu(base[j].astype(f32)).astype(bf16)
        return carry

    lax.fori_loop(0, BLOCKS, one, 0, unroll=4)


def packed_tile(tile_rows):
    high = tile_rows.astype(bf16).astype(f32)
    low = tile_rows - high
    return jnp.concatenate([high[:, :128], high[:, 128:], low[:, :128], low[:, 128:]], axis=0).astype(bf16)


def unpacked_tile(rows):
    both = rows.astype(f32)
    both = both[0:16] + both[16:32]
    return jnp.concatenate([both[0:8], both[8:16]], axis=1)


def stat_rows(mean, spread):
    return jnp.concatenate([mean, spread, jnp.zeros((4, 128), f32)], axis=0)


def halves(row):
    return jnp.concatenate([row[:, :128], row[:, 128:]], axis=0)


def first_conv(ins, outs, signal, y_bank, z_bank, taps, gathered):
    (coords, counts, links, weights, signal_in, y_own, z_own, *planes, features, pool, down) = ins
    level, own_tile, message = outs
    coords, counts, links, weight = coords.get(), counts.get(), links.get(), weights.get().at[0]
    signal[BLOCKS] = jnp.zeros((CHANS, VOXELS), bf16)
    bank_received([p.get() for p in planes], y_bank, z_bank)
    for one in (signal_in, y_own, z_own):
        one.get()
    base = features.get()
    level_ref = level.ref

    def finish(j, result):
        level_ref[j] = (base[j].astype(f32) + result).astype(bf16)

    convolve(coords, links, signal, y_bank, z_bank, weight, taps, finish)
    level.send()
    gathered[...] = jnp.zeros_like(gathered)
    diagonal = channel_diagonal()
    mean_of = pool.get()
    for i in range(0, BLOCKS, 8):
        block = level_ref[i : i + 8].reshape(8 * CHANS, VOXELS)
        means = jnp.dot(block, mean_of[...], preferred_element_type=f32)
        for u in range(8):
            j = i + u
            part = jnp.where(diagonal, means[u * CHANS : (u + 1) * CHANS], 0.0)
            cell, pos = place(coords, j)
            pos = jnp.where(j < counts[0], pos, 8)
            gathered[pos, pl.ds(cell, 1), :] = jnp.sum(part, axis=0, keepdims=True)
    total = jnp.zeros((16, COARSE), f32)
    rows = down.get()
    for pos in range(8):
        total += jnp.dot(
            gathered[pos].astype(bf16), rows[pos * 256 : pos * 256 + 256], preferred_element_type=f32
        )
    total = total[:8]
    mean = jnp.mean(total, axis=0, keepdims=True)
    spread = jnp.sum((total - mean) * (total - mean), axis=0, keepdims=True)
    extra = stat_rows(halves(mean), halves(spread))
    for i in range(16):
        message.ref[i] = extra
    own_tile.ref[...] = total


def level_faces(ins, outs, y_bank, z_bank, work):
    coords, counts, level, faces, own_tile = (one.get() for one in ins)
    take_faces(level, faces, y_bank, z_bank)
    fill_planes(coords, counts, y_bank, z_bank, work, [p.ref for p in outs])
    packed = packed_tile(own_tile[...])
    outs[0].ref[8] = packed
    outs[1].ref[8] = packed


def channel_diagonal():
    channel = lax.broadcasted_iota(jnp.int32, (CHANS, 256), 0)
    return channel == (lax.broadcasted_iota(jnp.int32, (CHANS, 256), 1) & 31)


def place(coords, j):
    z, y, x = coords[0, j] & 3, coords[1, j] & 3, coords[2, j]
    cell = (z >> 1) * 4 + (y >> 1) * 2 + (x >> 1)
    return cell, (z & 1) * 4 + (y & 1) * 2 + (x & 1)


def merged_sums(means, spreads, entries):
    mean = jnp.mean(means, axis=0, keepdims=True)
    away = means - mean
    return mean, jnp.sum(spreads + entries * away * away, axis=0, keepdims=True)


def row_sums(ins, outs):
    message, own_tile, y_above, y_below, z_low, z_high = (one.get() for one in ins)
    partial, z_low_out, z_high_out = (one.ref for one in outs)
    mean, spread = merged_sums(message[:, 0:2, :], message[:, 2:4, :], 8.0)
    both = stat_rows(mean[0], spread[0])
    for i in range(16):
        partial[i] = both
    packed = packed_tile(own_tile[...])
    for out, plane in ((z_low_out, z_low), (z_high_out, z_high)):
        out[0:8] = plane[...]
        out[8] = y_below[8]
        out[9] = packed
        out[10] = y_above[8]


def group_total(x):
    lane = lax.broadcasted_iota(jnp.int32, x.shape, 1)
    for width in (1, 2, 4):
        x = x + jnp.where(
            (lane & width) == 0, pltpu.roll(x, 128 - width, 1), pltpu.roll(x, width, 1)
        )
    return x


def times_half(total, near, half):
    for t in range(TAPS):
        total += lax.dot_general(
            near(t), half[:, tile(t)], (((1,), (1,)), ((), ())), preferred_element_type=f32
        )
    return total


def coarse_front(ins, outs, active, raw, patches):
    where, partial, own_tile, gain, bias, patch, plain, near_half, *planes = ins
    where, partial = where.get(), partial.get()
    major, minor = where[0], where[1]
    mean, spread_sum = merged_sums(partial[:, 0:2, :], partial[:, 2:4, :], 128.0)
    mean, spread_sum = mean[0], spread_sum[0]
    group_mean = group_total(mean) * (1.0 / GROUP)
    away = mean - group_mean
    variance = group_total(spread_sum + 2048.0 * away * away) * (1.0 / (2048 * GROUP))
    gain, bias = gain.get(), bias.get()
    group_mean = jnp.concatenate([group_mean[0:1], group_mean[1:2]], axis=1)
    variance = jnp.concatenate([variance[0:1], variance[1:2]], axis=1)
    scale = gain[...] / jnp.sqrt(variance + NORM_EPS)
    r0, r1, r2, r3 = (p.get() for p in planes)
    tiles = [
        [unpacked_tile(r3[8]), unpacked_tile(r3[9]), unpacked_tile(r3[10])],
        [unpacked_tile(r1[8]), own_tile.get()[...], unpacked_tile(r0[8])],
        [unpacked_tile(r2[8]), unpacked_tile(r2[9]), unpacked_tile(r2[10])],
    ]
    active[...] = jnp.zeros_like(active)
    raw[...] = jnp.zeros_like(raw)
    for dz, strip in enumerate(tiles):
        inside_z = (major + dz >= 1) & (major + dz <= 16)
        for dy in range(3):
            inside = inside_z & (minor + dy >= 1) & (minor + dy <= 16)
            value = strip[dy]
            at = (dz * 3 + dy) * 8
            raw[at : at + 8] = value
            normed = silu((value - group_mean) * scale + bias[...])
            active[at : at + 8] = jnp.where(inside, normed, 0.0)
    grid = active[...].astype(bf16)
    cells = jnp.dot(patch.get()[...], grid, preferred_element_type=f32).astype(bf16)
    for t in range(TAPS):
        patches[2 * t] = cells[t * 32 : t * 32 + 32, :128]
        patches[2 * t + 1] = cells[t * 32 : t * 32 + 32, 128:]
    rest = raw[...]
    plain = plain.get()
    total = jnp.zeros((32, COARSE), f32)
    for _ in range(3):
        high = rest.astype(bf16)
        rest = rest - high.astype(f32)
        total += jnp.dot(plain[...], high, preferred_element_type=f32)
    base = (major & 1) * TAPS
    half = near_half.get()
    outs[0].ref[...] = times_half(total, lambda t: patches[base + t], half)
    for t in range(TAPS):
        outs[1].ref[t] = patches[TAPS - base + t]


def second_conv(ins, outs, joined, signal, y_bank, z_bank, taps, work, lifted, rows):
    (total, far_patches, far_half, up, coords, counts, links, weights, spread, level, faces,
     y_spread, z_spread, *planes) = ins
    second, signal2, y_own, z_own, *sent, coarse = outs
    far_patches = far_patches.get()
    total = times_half(total.get()[...], lambda t: far_patches[t], far_half.get())
    r0, r1, r2, r3 = (p.get() for p in planes)
    result = total.astype(bf16)
    coarse.ref[...] = result[0:8]
    up = up.get()
    for pos in range(8):
        lifted[pos] = jnp.dot(
            result, up[:, pos * 256 : pos * 256 + 256], preferred_element_type=f32
        )
    diagonal = channel_diagonal()
    coords, counts, links, weight = coords.get(), counts.get(), links.get(), weights.get().at[1]
    spread, level, faces = spread.get(), level.get(), faces.get()
    y_spread, z_spread = y_spread.get(), z_spread.get()

    def row_block(pos, cell):
        return jnp.where(diagonal, lifted[pos, pl.ds(cell, 1), :], 0.0).astype(bf16)

    for i in range(0, BLOCKS, 8):
        for u in range(8):
            cell, pos = place(coords, i + u)
            rows[u * CHANS : (u + 1) * CHANS] = row_block(pos, cell)
        term = jnp.dot(rows[...], spread[...], preferred_element_type=f32)
        base = level[i : i + 8].reshape(8 * CHANS, VOXELS).astype(f32)
        merged = (base + term).astype(bf16)
        joined[i : i + 8] = merged.reshape(8, CHANS, VOXELS)
        signal[i : i + 8] = silu(merged.astype(f32)).astype(bf16).reshape(8, CHANS, VOXELS)
    signal[BLOCKS] = jnp.zeros((CHANS, VOXELS), bf16)
    take_faces(signal, faces, y_bank, z_bank)
    zero = jnp.zeros((CHANS, 128), bf16)
    y_bank[BLOCKS] = zero
    z_bank[BLOCKS] = zero
    kinds = (
        (r0, y_bank, 33, 12, y_spread, 96, 4, 0, 2),
        (r1, y_bank, 49, 8, y_spread, 96, 4, 1, 2),
        (r2, z_bank, 33, 20, z_spread, 64, 2, 0, 4),
        (r3, z_bank, 49, 16, z_spread, 64, 2, 1, 4),
    )
    for plane, bank, entry, first, expand, back, stride, far, edge in kinds:
        for i in range(0, 16, 8):
            for u in range(8):
                p = i + u
                a, x = p // 4, p % 4
                pos = a % 2 * stride + far * edge + x % 2
                cell = first + a // 2 * 2 + x // 2
                rows[u * CHANS : (u + 1) * CHANS] = jnp.where(
                    diagonal, lifted[pos, cell : cell + 1, :], 0.0
                ).astype(bf16)
            term = jnp.dot(rows[...], expand[...], preferred_element_type=f32)
            for u in range(8):
                face = received(plane, i + u, back).astype(f32)
                merged = (face + term[u * CHANS : (u + 1) * CHANS]).astype(bf16)
                bank[entry + i + u] = silu(merged.astype(f32)).astype(bf16)

    second_ref, signal2_ref = second.ref, signal2.ref

    def finish(j, value):
        out = (joined[j].astype(f32) + value).astype(bf16)
        second_ref[j] = out
        signal2_ref[j] = silu(out.astype(f32)).astype(bf16)

    convolve(coords, links, signal, y_bank, z_bank, weight, taps, finish)
    second.send()
    signal2.send()
    take_faces(signal2_ref, faces, y_own.ref, z_own.ref)
    y_own.send()
    z_own.send()
    fill_planes(coords, counts, y_own.ref, z_own.ref, work, [p.ref for p in sent])


def third_conv(ins, outs, signal, y_bank, z_bank, taps):
    (coords, counts, links, weights, signal_in, y_own, z_own, *planes, second) = ins
    coords, counts, links, weight = coords.get(), counts.get(), links.get(), weights.get().at[2]
    signal[BLOCKS] = jnp.zeros((CHANS, VOXELS), bf16)
    bank_received([p.get() for p in planes], y_bank, z_bank)
    for one in (signal_in, y_own, z_own):
        one.get()
    base = second.get()
    out = outs[0].ref

    def finish(j, result):
        value = base[j].astype(f32) + result
        out[j] = jnp.where(j < counts[0], value, 0.0).astype(bf16)

    convolve(coords, links, signal, y_bank, z_bank, weight, taps, finish)


class Arriving:
    def __init__(self, copy, ref):
        self.copy, self.ref = copy, ref
        copy.start()

    def get(self):
        if self.copy is not None:
            self.copy.wait()
            self.copy = None
        return self.ref


class Leaving:
    def __init__(self, copy, ref):
        self.copy, self.ref, self.sent = copy, ref, False

    def send(self):
        self.copy.start()
        self.sent = True


def call(kernel, arrays, outs, scratch, microseconds, spare=()):
    own = [(i, to) for i, (_, to) in enumerate(arrays) if to is None or to == "smem"]
    count, total = len(arrays), len(arrays) + len(spare)

    def body(*refs):
        ins, results = refs[:count], refs[total : total + len(outs)]
        rest = refs[total + len(outs) :]
        buffers, rest = rest[: len(own)], rest[len(own) :]
        staged, rest = rest[: len(outs)], rest[len(outs) :]
        work, (in_sem, out_sem) = rest[:-2], rest[-2:]
        placed = {i: buffer for (i, _), buffer in zip(own, buffers)}
        arriving = []
        for i, (_, to) in enumerate(arrays):
            ref = placed[i] if i in placed else to(*work)
            arriving.append(Arriving(pltpu.make_async_copy(ins[i], ref, in_sem.at[i]), ref))
        leaving = [
            Leaving(pltpu.make_async_copy(staged[i], results[i], out_sem.at[i]), staged[i])
            for i in range(len(outs))
        ]
        kernel(arriving, leaving, *work)
        for one in arriving:
            one.get()
        for one in leaving:
            if not one.sent:
                one.send()
        for one in leaving:
            one.copy.wait()

    hbm = pl.BlockSpec(memory_space=pltpu.HBM)
    spaces = {None: pltpu.VMEM, "smem": pltpu.SMEM}
    buffers = [spaces[to](arrays[i][0].shape, arrays[i][0].dtype) for i, to in own]
    buffers += [pltpu.VMEM(s, d) for s, d in (*outs, *scratch)]
    return pl.pallas_call(
        body,
        in_specs=[hbm] * total,
        out_specs=[hbm] * len(outs),
        out_shape=[jax.ShapeDtypeStruct(s, d) for s, d in outs],
        scratch_shapes=buffers
        + [pltpu.SemaphoreType.DMA((count,)), pltpu.SemaphoreType.DMA((len(outs),))],
        compiler_params=pltpu.CompilerParams(vmem_limit_bytes=60 << 20),
        cost_estimate=pl.CostEstimate(
            flops=microseconds * 1_000_000_000,
            bytes_accessed=microseconds * 3_000_000,
            transcendentals=0,
        ),
    )(*[a for a, _ in arrays], *spare)


FIELD = ((BLOCKS, CHANS, VOXELS), bf16)
FACES = ((BLOCKS, CHANS, 128), bf16)
PLANE = ((8, CHANS, 128), bf16)
SIGNAL = ((BLOCKS + 1, CHANS, VOXELS), bf16)
BANK = ((BLOCKS + 33, CHANS, 128), bf16)
TAP_STACK = ((4, 7 * CHANS, VOXELS), bf16)
SUMS = ((16, 8, 128), f32)
WORK = ((4, 9, CHANS, 128), bf16)


def shifted(x, axes, step):
    count = lax.axis_size(axes)
    return lax.ppermute(x, axes, [(i, (i + step) % count) for i in range(count)])


def swap_planes(planes):
    y_low, y_high, z_low, z_high = planes
    return (
        shifted(y_low, MY, -1),
        shifted(y_high, MY, 1),
        shifted(z_low, MX, -1),
        shifted(z_high, MX, 1),
    )


def local(
    features, coords, counts, neighbours, fine_weights, down_weight, up_weight, norm_gain, norm_bias,
    coarse_weight,
):
    faces, pool, spread, y_spread, z_spread, patch, plain = map(jnp.asarray, tables())
    major = lax.axis_index(MX)
    minor = lax.axis_index(MY)
    where = jnp.stack([major, minor]).astype(jnp.int32)
    part = lax.dynamic_slice_in_dim(
        coarse_weight.T, lax.axis_index("mx_1") * HALF_ROWS, HALF_ROWS, 1
    )
    near_half = lax.all_gather(part, MY, axis=0, tiled=True)

    def plainly(*arrays):
        return tuple((x, None) for x in arrays)

    live = ((coords, "smem"), (counts, "smem"), (neighbours, "smem"))
    place_own = (
        lambda signal, *rest: signal.at[0:BLOCKS],
        lambda signal, y_bank, *rest: y_bank.at[0:BLOCKS],
        lambda signal, y_bank, z_bank, *rest: z_bank.at[0:BLOCKS],
    )
    *own, low_y, high_y, low_z, high_z = call(
        first_faces, (*plainly(features, faces), *live[:2]),
        (FACES, FACES) + (PLANE,) * 4, (WORK,), 3,
    )
    planes = swap_planes((low_y, high_y, low_z, high_z))
    (signal,) = call(activate, plainly(features), (FIELD,), (), 3)
    level, own_tile, message = call(
        first_conv,
        (*live, (fine_weights, None), *zip((signal, *own), place_own),
         *plainly(*planes, features, pool, down_weight)),
        (FIELD, ((8, COARSE), f32), SUMS),
        (SIGNAL, BANK, BANK, TAP_STACK, ((9, 16, COARSE), f32)), 8,
    )
    message = lax.all_to_all(message, MY, 0, 0)
    low_y, high_y, low_z, high_z = call(
        level_faces, (*live[:2], *plainly(level, faces, own_tile)),
        (((9, CHANS, 128), bf16),) * 2 + (PLANE,) * 2, (FACES, FACES, WORK), 3,
    )
    y_above, y_below = shifted(low_y, MY, -1), shifted(high_y, MY, 1)
    partial, low_z, high_z = call(
        row_sums, plainly(message, own_tile, y_above, y_below, low_z, high_z),
        (SUMS,) + (((11, CHANS, 128), bf16),) * 2, (), 1,
    )
    partial = lax.all_to_all(partial, MX, 0, 0)
    z_above, z_below = shifted(low_z, MX, -1), shifted(high_z, MX, 1)
    near_half, partial, z_above, z_below = lax.optimization_barrier(
        (near_half, partial, z_above, z_below)
    )
    far_half = lax.ppermute(near_half, "mx_1", [(0, 1), (1, 0)])
    planes = (y_above, y_below, z_above, z_below)
    front = call(
        coarse_front,
        ((where, "smem"),
         *plainly(partial, own_tile, norm_gain.reshape(1, COARSE), norm_bias.reshape(1, COARSE),
                  patch, plain, near_half, *planes)),
        (((32, COARSE), f32), ((TAPS, 32, 128), bf16)),
        (((128, COARSE), f32), ((128, COARSE), f32), ((2 * TAPS, 32, 128), bf16)), 4,
    )
    second, *own, low_y, high_y, low_z, high_z, coarse = call(
        second_conv,
        (*plainly(*front, far_half, up_weight), *live,
         *plainly(fine_weights, spread, level, faces, y_spread, z_spread, *planes)),
        (FIELD, FIELD, FACES, FACES) + (PLANE,) * 4 + (((8, COARSE), bf16),),
        (FIELD, SIGNAL, BANK, BANK, TAP_STACK, WORK, ((8, 32, COARSE), f32), ((256, 256), bf16)), 12,
    )
    planes = swap_planes((low_y, high_y, low_z, high_z))
    (fine_out,) = call(
        third_conv, (*live, (fine_weights, None), *zip(own, place_own), *plainly(*planes, second)),
        (FIELD,), (SIGNAL, BANK, BANK, TAP_STACK), 7,
    )
    return fine_out, coarse.reshape(2, 2, 2, COARSE)


def solution(mesh):
    split = Mesh(mesh.devices.reshape(8, 2, 4, 4), ("mx_0", "mx_1", "my_0", "my_1"))
    placed = (
        P(MX_MY, None, None), P(None, MX_MY), P(MX_MY), P(None, MX_MY),
        P(), P(), P(), P(), P(), P(None, MY),
    )
    return jax.shard_map(
        local,
        mesh=split,
        in_specs=placed,
        out_specs=(P(MX_MY, None, None), P(MX, MY, None, None)),
        check_vma=False,
    )
```

```python
import functools

import jax
import jax.numpy as jnp
import ml_dtypes
import numpy as np
from jax import lax
from jax.experimental import pallas as pl
from jax.experimental.pallas import tpu as pltpu
from jax.sharding import Mesh
from jax.sharding import PartitionSpec as P

MX = ("mx_0", "mx_1")
MY = ("my_0", "my_1")
MX_MY = MX + MY
BLOCKS = 32
CHANS = 32
VOXELS = 512
COARSE = 256
GROUP = 8
TAPS = 27
HALF_ROWS = TAPS * COARSE // 2
NORM_EPS = 1e-05
bf16 = jnp.bfloat16
f32 = jnp.float32


def octant(z, y, x):
    return z // 4 * 4 + y // 4 * 2 + x // 4


def voxel_zyx():
    voxel = np.arange(VOXELS)
    return voxel // 64, voxel // 8 % 8, voxel % 8


@functools.cache
def tables():
    z, y, x = voxel_zyx()
    voxel = np.arange(VOXELS)
    faces = np.zeros((VOXELS, 256), np.float32)
    y_lane = z % 2 * 64 + z // 2 * 8 + x
    faces[voxel[y == 0], y_lane[y == 0]] = 1
    faces[voxel[y == 7], y_lane[y == 7] + 32] = 1
    z_lane = y * 8 + x
    faces[voxel[z == 0], 128 + 64 + z_lane[z == 0]] = 1
    faces[voxel[z == 7], 128 + z_lane[z == 7]] = 1
    own = np.arange(256) // 32
    pool = (octant(z, y, x)[:, None] == own[None, :]).astype(np.float32) / 64
    spread = (own[:, None] == octant(z, y, x)[None, :]).astype(np.float32)
    lane = np.arange(128)
    y_octant = octant(lane % 32 // 8 * 2 + lane // 64, lane // 32 % 2 * 4, lane % 8)
    z_octant = octant((lane < 64) * 4, lane % 64 // 8, lane % 8)
    y_spread = (own[:, None] == y_octant[None, :]).astype(np.float32)
    z_spread = (own[:, None] == z_octant[None, :]).astype(np.float32)
    cells = [(a, b, c) for a in range(2) for b in range(2) for c in range(2)]
    cells += [(a, b, c) for b in (-1, 2) for a in range(2) for c in range(2)]
    cells += [(a, b, c) for a in (-1, 2) for b in range(2) for c in range(2)]

    def row_of(a, b, c):
        part = (a // 2 + 1) * 3 + b // 2 + 1
        return part * 8 + a % 2 * 4 + b % 2 * 2 + c

    patch = np.zeros((TAPS, 32, 128), np.float32)
    plain = np.zeros((32, 128), np.float32)
    for i, (a, b, c) in enumerate(cells):
        plain[i, row_of(a, b, c)] = 1
        for t in range(TAPS):
            near = (a + t // 9 - 1, b + t // 3 % 3 - 1, c + t % 3 - 1)
            if 0 <= near[2] < 2:
                patch[t, i, row_of(*near)] = 1
    kinds = (faces, pool, spread, y_spread, z_spread, patch.reshape(TAPS * 32, 128), plain)
    return tuple(k.astype(ml_dtypes.bfloat16) for k in kinds)


def lanes():
    return lax.broadcasted_iota(jnp.int32, (CHANS, 128), 1)


def silu(x):
    return x * (1.0 / (1.0 + jnp.exp(-x)))


def tile(k):
    return slice(k * 128, k * 128 + 128)


def take_faces(signal, faces_ref, y_bank, z_bank):
    for i in range(0, BLOCKS, 8):
        block = signal[i : i + 8].reshape(8 * CHANS, VOXELS)
        packed = jnp.dot(block, faces_ref[...], preferred_element_type=f32).astype(bf16)
        y_bank[i : i + 8] = packed[:, :128].reshape(8, CHANS, 128)
        z_bank[i : i + 8] = packed[:, 128:].reshape(8, CHANS, 128)


def fill_planes(coords, counts, y_bank, z_bank, work, outs):
    lane = lanes()
    work[...] = jnp.zeros_like(work)
    in_low = (lane & 32) == 0
    in_back = lane >= 64

    def one(j, carry):
        live = j < counts[0]
        z, y, x = coords[0, j] & 3, coords[1, j] & 3, coords[2, j]
        odd = (x & 1) == 1
        y_row, z_row = (z * 4 + x) >> 1, (y * 4 + x) >> 1
        face = y_bank[j]
        turned = pltpu.roll(face, 32, 1)
        value = jnp.where(odd, turned, face)
        for plane, edge, low in ((0, 0, True), (1, 3, False)):
            row = jnp.where(live & (y == edge), y_row, 8)
            mask = jnp.logical_xor(in_low if low else jnp.logical_not(in_low), odd)
            work[plane, row] = jnp.where(mask, value, work[plane, row])
        face = z_bank[j]
        turned = pltpu.roll(face, 64, 1)
        value = jnp.where(odd, turned, face)
        for plane, edge, low in ((2, 0, True), (3, 3, False)):
            row = jnp.where(live & (z == edge), z_row, 8)
            mask = jnp.logical_xor(in_back if low else jnp.logical_not(in_back), odd)
            work[plane, row] = jnp.where(mask, value, work[plane, row])
        return carry

    lax.fori_loop(0, BLOCKS, one, 0, unroll=4)
    for plane, out in enumerate(outs):
        out[0:8] = work[plane, :8]


def received(plane_ref, p, back):
    row = plane_ref[p // 2]
    return pltpu.roll(row, back, 1) if p % 2 else row


def bank_received(planes, y_bank, z_bank):
    zero = jnp.zeros((CHANS, 128), bf16)
    y_bank[BLOCKS] = zero
    z_bank[BLOCKS] = zero
    for p in range(16):
        y_bank[33 + p] = received(planes[0], p, 96)
        y_bank[49 + p] = received(planes[1], p, 96)
        z_bank[33 + p] = received(planes[2], p, 64)
        z_bank[49 + p] = received(planes[3], p, 64)


def convolve(coords, links, signal, y_bank, z_bank, weight, taps, finish):
    lane = lanes()
    along_x = lane & 7
    along_yx = lane & 63
    front = lane < 64

    def build(j, slot):
        z, y, x = coords[0, j] & 3, coords[1, j] & 3, coords[2, j]
        y_pos, z_pos = z * 4 + x, y * 4 + x

        def near(direction, inside, remote):
            link = links[direction, j]
            here = link & (BLOCKS - 1)
            if inside is not None:
                here = jnp.where(inside, here, remote)
            return jnp.where(link < 0, BLOCKS, here)

        x_up, x_down = near(0, None, None), near(1, None, None)
        y_up = y_bank[near(2, y < 3, 33 + y_pos)]
        y_down = y_bank[near(3, y > 0, 49 + y_pos)]
        z_up = z_bank[near(4, z < 3, 33 + z_pos)]
        z_down = z_bank[near(5, z > 0, 49 + z_pos)]
        own = [signal[j, :, tile(k)] for k in range(4)]
        half = [z_down] + [pltpu.roll(own[k], 64, 1) for k in range(4)] + [z_up]
        for k in range(4):
            to = tile(k)
            taps[slot, 0:32, to] = own[k]
            taps[slot, 32:64, to] = jnp.where(
                along_x == 7,
                pltpu.roll(signal[x_up, :, to], 7, 1),
                pltpu.roll(own[k], 127, 1),
            )
            taps[slot, 64:96, to] = jnp.where(
                along_x == 0,
                pltpu.roll(signal[x_down, :, to], 121, 1),
                pltpu.roll(own[k], 1, 1),
            )
            taps[slot, 96:128, to] = jnp.where(
                along_yx >= 56, pltpu.roll(y_up, 56 - 8 * k, 1), pltpu.roll(own[k], 120, 1)
            )
            taps[slot, 128:160, to] = jnp.where(
                along_yx < 8, pltpu.roll(y_down, 96 - 8 * k, 1), pltpu.roll(own[k], 8, 1)
            )
            taps[slot, 160:192, to] = jnp.where(front, half[k + 1], half[k + 2])
            taps[slot, 192:224, to] = jnp.where(front, half[k], half[k + 1])

    def some(i, carry):
        for u in range(4):
            build(i * 4 + u, u)
        for u in range(4):
            result = jnp.dot(weight[...], taps[u], preferred_element_type=f32)
            finish(i * 4 + u, result)
        return carry

    lax.fori_loop(0, BLOCKS // 4, some, 0)


def first_faces(ins, outs, work):
    features, faces, coords, counts = ins
    y_own, z_own, *planes = outs
    base, faces = features.get(), faces.get()
    for i in range(0, BLOCKS, 8):
        block = base[i : i + 8].reshape(8 * CHANS, VOXELS)
        packed = silu(jnp.dot(block, faces[...], preferred_element_type=f32)).astype(bf16)
        y_own.ref[i : i + 8] = packed[:, :128].reshape(8, CHANS, 128)
        z_own.ref[i : i + 8] = packed[:, 128:].reshape(8, CHANS, 128)
    y_own.send()
    z_own.send()
    fill_planes(coords.get(), counts.get(), y_own.ref, z_own.ref, work, [p.ref for p in planes])


def activate(ins, outs):
    base, signal = ins[0].get(), outs[0].ref

    def one(j, carry):
        signal[j] = silu(base[j].astype(f32)).astype(bf16)
        return carry

    lax.fori_loop(0, BLOCKS, one, 0, unroll=4)


def packed_tile(tile_rows):
    high = tile_rows.astype(bf16).astype(f32)
    low = tile_rows - high
    return jnp.concatenate([high[:, :128], high[:, 128:], low[:, :128], low[:, 128:]], axis=0).astype(bf16)


def unpacked_tile(rows):
    both = rows.astype(f32)
    both = both[0:16] + both[16:32]
    return jnp.concatenate([both[0:8], both[8:16]], axis=1)


def exact_parts(x):
    parts = []
    for _ in range(3):
        part = x.astype(bf16).astype(f32)
        parts.append(part)
        x = x - part
    return jnp.concatenate([*parts, jnp.zeros((4, 128), f32)], axis=0).astype(bf16)


def stat_rows(mean, spread):
    return jnp.concatenate([mean, spread, jnp.zeros((4, 128), f32)], axis=0)


def halves(row):
    return jnp.concatenate([row[:, :128], row[:, 128:]], axis=0)


def first_conv(ins, outs, signal, y_bank, z_bank, taps, gathered):
    (coords, counts, links, weights, signal_in, y_own, z_own, *planes, features, pool, down, where, weight_columns) = ins
    level, own_tile, message = outs
    coords, counts, links, weight = coords.get(), counts.get(), links.get(), weights.get().at[0]
    signal[BLOCKS] = jnp.zeros((CHANS, VOXELS), bf16)
    bank_received([p.get() for p in planes], y_bank, z_bank)
    for one in (signal_in, y_own, z_own):
        one.get()
    base = features.get()
    level_ref = level.ref
    start = pl.multiple_of((where.get()[0] & 1) * HALF_ROWS, 128)
    half = weight_columns.get()[:, pl.ds(start, HALF_ROWS)]
    for i in range(16):
        message.ref[i, :, :HALF_ROWS] = half

    def finish(j, result):
        level_ref[j] = (base[j].astype(f32) + result).astype(bf16)

    convolve(coords, links, signal, y_bank, z_bank, weight, taps, finish)
    level.send()
    gathered[...] = jnp.zeros_like(gathered)
    diagonal = channel_diagonal()
    mean_of = pool.get()
    for i in range(0, BLOCKS, 8):
        block = level_ref[i : i + 8].reshape(8 * CHANS, VOXELS)
        means = jnp.dot(block, mean_of[...], preferred_element_type=f32)
        for u in range(8):
            j = i + u
            part = jnp.where(diagonal, means[u * CHANS : (u + 1) * CHANS], 0.0)
            cell, pos = place(coords, j)
            pos = jnp.where(j < counts[0], pos, 8)
            gathered[pos, pl.ds(cell, 1), :] = jnp.sum(part, axis=0, keepdims=True)
    total = jnp.zeros((16, COARSE), f32)
    rows = down.get()
    for pos in range(8):
        total += jnp.dot(
            gathered[pos].astype(bf16), rows[pos * 256 : pos * 256 + 256], preferred_element_type=f32
        )
    total = total[:8]
    mean = jnp.mean(total, axis=0, keepdims=True)
    spread = jnp.sum((total - mean) * (total - mean), axis=0, keepdims=True)
    extra = exact_parts(jnp.concatenate([halves(mean), halves(spread)], axis=0))
    for i in range(16):
        message.ref[i, :, HALF_ROWS:] = extra
    own_tile.ref[...] = total


def level_faces(ins, outs, y_bank, z_bank, work):
    coords, counts, level, faces, own_tile = (one.get() for one in ins)
    take_faces(level, faces, y_bank, z_bank)
    fill_planes(coords, counts, y_bank, z_bank, work, [p.ref for p in outs])
    packed = packed_tile(own_tile[...])
    outs[0].ref[8] = packed
    outs[1].ref[8] = packed


def channel_diagonal():
    channel = lax.broadcasted_iota(jnp.int32, (CHANS, 256), 0)
    return channel == (lax.broadcasted_iota(jnp.int32, (CHANS, 256), 1) & 31)


def place(coords, j):
    z, y, x = coords[0, j] & 3, coords[1, j] & 3, coords[2, j]
    cell = (z >> 1) * 4 + (y >> 1) * 2 + (x >> 1)
    return cell, (z & 1) * 4 + (y & 1) * 2 + (x & 1)


def merged_sums(means, spreads, entries):
    mean = jnp.mean(means, axis=0, keepdims=True)
    away = means - mean
    return mean, jnp.sum(spreads + entries * away * away, axis=0, keepdims=True)


def row_sums(ins, outs):
    message, own_tile, y_above, y_below, z_low, z_high = (one.get() for one in ins)
    partial, z_low_out, z_high_out = (one.ref for one in outs)
    sums = message[...].astype(f32)
    sums = sums[:, 0:4] + sums[:, 4:8] + sums[:, 8:12]
    mean, spread = merged_sums(sums[:, 0:2], sums[:, 2:4], 8.0)
    both = stat_rows(mean[0], spread[0])
    for i in range(16):
        partial[i] = both
    packed = packed_tile(own_tile[...])
    for out, plane in ((z_low_out, z_low), (z_high_out, z_high)):
        out[0:8] = plane[...]
        out[8] = y_below[8]
        out[9] = packed
        out[10] = y_above[8]


def group_total(x):
    lane = lax.broadcasted_iota(jnp.int32, x.shape, 1)
    for width in (1, 2, 4):
        x = x + jnp.where(
            (lane & width) == 0, pltpu.roll(x, 128 - width, 1), pltpu.roll(x, width, 1)
        )
    return x


def times_half(total, near, half):
    for t in range(TAPS):
        total += lax.dot_general(
            near(t), half[:, tile(t)], (((1,), (1,)), ((), ())), preferred_element_type=f32
        )
    return total


def coarse_front(ins, outs, active, raw, patches):
    where, partial, own_tile, gain, bias, patch, plain, near_half, *planes = ins
    where, partial = where.get(), partial.get()
    major, minor = where[0], where[1]
    mean, spread_sum = merged_sums(partial[:, 0:2, :], partial[:, 2:4, :], 128.0)
    mean, spread_sum = mean[0], spread_sum[0]
    group_mean = group_total(mean) * (1.0 / GROUP)
    away = mean - group_mean
    variance = group_total(spread_sum + 2048.0 * away * away) * (1.0 / (2048 * GROUP))
    gain, bias = gain.get(), bias.get()
    group_mean = jnp.concatenate([group_mean[0:1], group_mean[1:2]], axis=1)
    variance = jnp.concatenate([variance[0:1], variance[1:2]], axis=1)
    scale = gain[...] / jnp.sqrt(variance + NORM_EPS)
    r0, r1, r2, r3 = (p.get() for p in planes)
    tiles = [
        [unpacked_tile(r3[8]), unpacked_tile(r3[9]), unpacked_tile(r3[10])],
        [unpacked_tile(r1[8]), own_tile.get()[...], unpacked_tile(r0[8])],
        [unpacked_tile(r2[8]), unpacked_tile(r2[9]), unpacked_tile(r2[10])],
    ]
    active[...] = jnp.zeros_like(active)
    raw[...] = jnp.zeros_like(raw)
    for dz, strip in enumerate(tiles):
        inside_z = (major + dz >= 1) & (major + dz <= 16)
        for dy in range(3):
            inside = inside_z & (minor + dy >= 1) & (minor + dy <= 16)
            value = strip[dy]
            at = (dz * 3 + dy) * 8
            raw[at : at + 8] = value
            normed = silu((value - group_mean) * scale + bias[...])
            active[at : at + 8] = jnp.where(inside, normed, 0.0)
    grid = active[...].astype(bf16)
    cells = jnp.dot(patch.get()[...], grid, preferred_element_type=f32).astype(bf16)
    for t in range(TAPS):
        patches[2 * t] = cells[t * 32 : t * 32 + 32, :128]
        patches[2 * t + 1] = cells[t * 32 : t * 32 + 32, 128:]
    rest = raw[...]
    plain = plain.get()
    total = jnp.zeros((32, COARSE), f32)
    for _ in range(3):
        high = rest.astype(bf16)
        rest = rest - high.astype(f32)
        total += jnp.dot(plain[...], high, preferred_element_type=f32)
    base = (major & 1) * TAPS
    half = near_half.get()
    outs[0].ref[...] = times_half(total, lambda t: patches[base + t], half)
    for t in range(TAPS):
        outs[1].ref[t] = patches[TAPS - base + t]


def second_conv(ins, outs, joined, signal, y_bank, z_bank, taps, work, lifted, rows):
    (total, far_patches, far_half, up, coords, counts, links, weights, spread, level, faces,
     y_spread, z_spread, *planes) = ins
    second, signal2, y_own, z_own, *sent, coarse = outs
    far_patches = far_patches.get()
    total = times_half(total.get()[...], lambda t: far_patches[t], far_half.get())
    r0, r1, r2, r3 = (p.get() for p in planes)
    result = total.astype(bf16)
    coarse.ref[...] = result[0:8]
    up = up.get()
    for pos in range(8):
        lifted[pos] = jnp.dot(
            result, up[:, pos * 256 : pos * 256 + 256], preferred_element_type=f32
        )
    diagonal = channel_diagonal()
    coords, counts, links, weight = coords.get(), counts.get(), links.get(), weights.get().at[1]
    spread, level, faces = spread.get(), level.get(), faces.get()
    y_spread, z_spread = y_spread.get(), z_spread.get()

    def row_block(pos, cell):
        return jnp.where(diagonal, lifted[pos, pl.ds(cell, 1), :], 0.0).astype(bf16)

    for i in range(0, BLOCKS, 8):
        for u in range(8):
            cell, pos = place(coords, i + u)
            rows[u * CHANS : (u + 1) * CHANS] = row_block(pos, cell)
        term = jnp.dot(rows[...], spread[...], preferred_element_type=f32)
        base = level[i : i + 8].reshape(8 * CHANS, VOXELS).astype(f32)
        merged = (base + term).astype(bf16)
        joined[i : i + 8] = merged.reshape(8, CHANS, VOXELS)
        signal[i : i + 8] = silu(merged.astype(f32)).astype(bf16).reshape(8, CHANS, VOXELS)
    signal[BLOCKS] = jnp.zeros((CHANS, VOXELS), bf16)
    take_faces(signal, faces, y_bank, z_bank)
    zero = jnp.zeros((CHANS, 128), bf16)
    y_bank[BLOCKS] = zero
    z_bank[BLOCKS] = zero
    kinds = (
        (r0, y_bank, 33, 12, y_spread, 96, 4, 0, 2),
        (r1, y_bank, 49, 8, y_spread, 96, 4, 1, 2),
        (r2, z_bank, 33, 20, z_spread, 64, 2, 0, 4),
        (r3, z_bank, 49, 16, z_spread, 64, 2, 1, 4),
    )
    for plane, bank, entry, first, expand, back, stride, far, edge in kinds:
        for i in range(0, 16, 8):
            for u in range(8):
                p = i + u
                a, x = p // 4, p % 4
                pos = a % 2 * stride + far * edge + x % 2
                cell = first + a // 2 * 2 + x // 2
                rows[u * CHANS : (u + 1) * CHANS] = jnp.where(
                    diagonal, lifted[pos, cell : cell + 1, :], 0.0
                ).astype(bf16)
            term = jnp.dot(rows[...], expand[...], preferred_element_type=f32)
            for u in range(8):
                face = received(plane, i + u, back).astype(f32)
                merged = (face + term[u * CHANS : (u + 1) * CHANS]).astype(bf16)
                bank[entry + i + u] = silu(merged.astype(f32)).astype(bf16)

    second_ref, signal2_ref = second.ref, signal2.ref

    def finish(j, value):
        out = (joined[j].astype(f32) + value).astype(bf16)
        second_ref[j] = out
        signal2_ref[j] = silu(out.astype(f32)).astype(bf16)

    convolve(coords, links, signal, y_bank, z_bank, weight, taps, finish)
    second.send()
    signal2.send()
    take_faces(signal2_ref, faces, y_own.ref, z_own.ref)
    y_own.send()
    z_own.send()
    fill_planes(coords, counts, y_own.ref, z_own.ref, work, [p.ref for p in sent])


def third_conv(ins, outs, signal, y_bank, z_bank, taps):
    (coords, counts, links, weights, signal_in, y_own, z_own, *planes, second) = ins
    coords, counts, links, weight = coords.get(), counts.get(), links.get(), weights.get().at[2]
    signal[BLOCKS] = jnp.zeros((CHANS, VOXELS), bf16)
    bank_received([p.get() for p in planes], y_bank, z_bank)
    for one in (signal_in, y_own, z_own):
        one.get()
    base = second.get()
    out = outs[0].ref

    def finish(j, result):
        value = base[j].astype(f32) + result
        out[j] = jnp.where(j < counts[0], value, 0.0).astype(bf16)

    convolve(coords, links, signal, y_bank, z_bank, weight, taps, finish)


class Arriving:
    def __init__(self, copy, ref):
        self.copy, self.ref = copy, ref
        copy.start()

    def get(self):
        if self.copy is not None:
            self.copy.wait()
            self.copy = None
        return self.ref


class Leaving:
    def __init__(self, copy, ref):
        self.copy, self.ref, self.sent = copy, ref, False

    def send(self):
        self.copy.start()
        self.sent = True


def call(kernel, arrays, outs, scratch, microseconds, spare=()):
    own = [(i, to) for i, (_, to) in enumerate(arrays) if not callable(to)]
    count, total = len(arrays), len(arrays) + len(spare)

    def body(*refs):
        ins, results = refs[:count], refs[total : total + len(outs)]
        rest = refs[total + len(outs) :]
        buffers, rest = rest[: len(own)], rest[len(own) :]
        staged, rest = rest[: len(outs)], rest[len(outs) :]
        work, (in_sem, out_sem) = rest[:-2], rest[-2:]
        placed = {i: buffer for (i, _), buffer in zip(own, buffers)}
        arriving = []
        for i, (_, to) in enumerate(arrays):
            ref = placed[i] if i in placed else to(*work)
            source = ins[i].at[:, :, to] if isinstance(to, slice) else ins[i]
            arriving.append(Arriving(pltpu.make_async_copy(source, ref, in_sem.at[i]), ref))
        leaving = [
            Leaving(pltpu.make_async_copy(staged[i], results[i], out_sem.at[i]), staged[i])
            for i in range(len(outs))
        ]
        kernel(arriving, leaving, *work)
        for one in arriving:
            one.get()
        for one in leaving:
            if not one.sent:
                one.send()
        for one in leaving:
            one.copy.wait()

    hbm = pl.BlockSpec(memory_space=pltpu.HBM)
    buffers = []
    for i, to in own:
        shape = arrays[i][0].shape
        if isinstance(to, slice):
            shape = (*shape[:-1], to.stop - to.start)
        space = pltpu.SMEM if to == "smem" else pltpu.VMEM
        buffers.append(space(shape, arrays[i][0].dtype))
    buffers += [pltpu.VMEM(s, d) for s, d in (*outs, *scratch)]
    return pl.pallas_call(
        body,
        in_specs=[hbm] * total,
        out_specs=[hbm] * len(outs),
        out_shape=[jax.ShapeDtypeStruct(s, d) for s, d in outs],
        scratch_shapes=buffers
        + [pltpu.SemaphoreType.DMA((count,)), pltpu.SemaphoreType.DMA((len(outs),))],
        compiler_params=pltpu.CompilerParams(vmem_limit_bytes=60 << 20),
        cost_estimate=pl.CostEstimate(
            flops=microseconds * 1_000_000_000,
            bytes_accessed=microseconds * 3_000_000,
            transcendentals=0,
        ),
    )(*[a for a, _ in arrays], *spare)


FIELD = ((BLOCKS, CHANS, VOXELS), bf16)
FACES = ((BLOCKS, CHANS, 128), bf16)
PLANE = ((8, CHANS, 128), bf16)
SIGNAL = ((BLOCKS + 1, CHANS, VOXELS), bf16)
BANK = ((BLOCKS + 33, CHANS, 128), bf16)
TAP_STACK = ((4, 7 * CHANS, VOXELS), bf16)
SUMS = ((16, 8, 128), f32)
WORK = ((4, 9, CHANS, 128), bf16)


def shifted(x, axes, step):
    count = lax.axis_size(axes)
    return lax.ppermute(x, axes, [(i, (i + step) % count) for i in range(count)])


def swap_planes(planes):
    y_low, y_high, z_low, z_high = planes
    return (
        shifted(y_low, MY, -1),
        shifted(y_high, MY, 1),
        shifted(z_low, MX, -1),
        shifted(z_high, MX, 1),
    )


def local(
    features, coords, counts, neighbours, fine_weights, down_weight, up_weight, norm_gain, norm_bias,
    coarse_weight,
):
    faces, pool, spread, y_spread, z_spread, patch, plain = map(jnp.asarray, tables())
    major = lax.axis_index(MX)
    minor = lax.axis_index(MY)
    where = jnp.stack([major, minor]).astype(jnp.int32)
    def plainly(*arrays):
        return tuple((x, None) for x in arrays)

    live = ((coords, "smem"), (counts, "smem"), (neighbours, "smem"))
    place_own = (
        lambda signal, *rest: signal.at[0:BLOCKS],
        lambda signal, y_bank, *rest: y_bank.at[0:BLOCKS],
        lambda signal, y_bank, z_bank, *rest: z_bank.at[0:BLOCKS],
    )
    *own, low_y, high_y, low_z, high_z = call(
        first_faces, (*plainly(features, faces), *live[:2]),
        (FACES, FACES) + (PLANE,) * 4, (WORK,), 3,
    )
    planes = swap_planes((low_y, high_y, low_z, high_z))
    (signal,) = call(activate, plainly(features), (FIELD,), (), 3)
    level, own_tile, message = call(
        first_conv,
        (*live, (fine_weights, None), *zip((signal, *own), place_own),
         *plainly(*planes, features, pool, down_weight), (where, "smem"), (coarse_weight.T, None)),
        (FIELD, ((8, COARSE), f32), ((16, 16, HALF_ROWS + 128), bf16)),
        (SIGNAL, BANK, BANK, TAP_STACK, ((9, 16, COARSE), f32)), 8,
    )
    message = lax.all_to_all(message, MY, 0, 0)
    low_y, high_y, low_z, high_z = call(
        level_faces, (*live[:2], *plainly(level, faces, own_tile)),
        (((9, CHANS, 128), bf16),) * 2 + (PLANE,) * 2, (FACES, FACES, WORK), 3,
    )
    y_above, y_below = shifted(low_y, MY, -1), shifted(high_y, MY, 1)
    partial, low_z, high_z = call(
        row_sums,
        ((message, slice(HALF_ROWS, HALF_ROWS + 128)), *plainly(own_tile, y_above, y_below, low_z, high_z)),
        (SUMS,) + (((11, CHANS, 128), bf16),) * 2, (), 1,
    )
    partial = lax.all_to_all(partial, MX, 0, 0)
    z_above, z_below = shifted(low_z, MX, -1), shifted(high_z, MX, 1)
    near_half = message.reshape(COARSE, HALF_ROWS + 128)
    near_half, partial, z_above, z_below = lax.optimization_barrier(
        (near_half, partial, z_above, z_below)
    )
    far_half = lax.ppermute(near_half, "mx_1", [(0, 1), (1, 0)])
    planes = (y_above, y_below, z_above, z_below)
    front = call(
        coarse_front,
        ((where, "smem"),
         *plainly(partial, own_tile, norm_gain.reshape(1, COARSE), norm_bias.reshape(1, COARSE),
                  patch, plain, near_half, *planes)),
        (((32, COARSE), f32), ((TAPS, 32, 128), bf16)),
        (((128, COARSE), f32), ((128, COARSE), f32), ((2 * TAPS, 32, 128), bf16)), 4,
    )
    second, *own, low_y, high_y, low_z, high_z, coarse = call(
        second_conv,
        (*plainly(*front, far_half, up_weight), *live,
         *plainly(fine_weights, spread, level, faces, y_spread, z_spread, *planes)),
        (FIELD, FIELD, FACES, FACES) + (PLANE,) * 4 + (((8, COARSE), bf16),),
        (FIELD, SIGNAL, BANK, BANK, TAP_STACK, WORK, ((8, 32, COARSE), f32), ((256, 256), bf16)), 12,
    )
    planes = swap_planes((low_y, high_y, low_z, high_z))
    (fine_out,) = call(
        third_conv, (*live, (fine_weights, None), *zip(own, place_own), *plainly(*planes, second)),
        (FIELD,), (SIGNAL, BANK, BANK, TAP_STACK), 7,
    )
    return fine_out, coarse.reshape(2, 2, 2, COARSE)


def solution(mesh):
    split = Mesh(mesh.devices.reshape(8, 2, 4, 4), ("mx_0", "mx_1", "my_0", "my_1"))
    placed = (
        P(MX_MY, None, None), P(None, MX_MY), P(MX_MY), P(None, MX_MY),
        P(), P(), P(), P(), P(), P(None, MY),
    )
    return jax.shard_map(
        local,
        mesh=split,
        in_specs=placed,
        out_specs=(P(MX_MY, None, None), P(MX, MY, None, None)),
        check_vma=False,
    )
```

```python
import functools

import jax
import jax.numpy as jnp
import ml_dtypes
import numpy as np
from jax import lax
from jax.experimental import pallas as pl
from jax.experimental.pallas import tpu as pltpu
from jax.sharding import Mesh
from jax.sharding import PartitionSpec as P

MX = ("mx_0", "mx_1")
MY = ("my_0", "my_1")
MX_MY = MX + MY
BLOCKS = 32
CHANS = 32
VOXELS = 512
COARSE = 256
GROUP = 8
TAPS = 27
HALF_ROWS = TAPS * COARSE // 2
NORM_EPS = 1e-05
bf16 = jnp.bfloat16
f32 = jnp.float32


def octant(z, y, x):
    return z // 4 * 4 + y // 4 * 2 + x // 4


def voxel_zyx():
    voxel = np.arange(VOXELS)
    return voxel // 64, voxel // 8 % 8, voxel % 8


@functools.cache
def tables():
    z, y, x = voxel_zyx()
    voxel = np.arange(VOXELS)
    faces = np.zeros((VOXELS, 256), np.float32)
    y_lane = z % 2 * 64 + z // 2 * 8 + x
    faces[voxel[y == 0], y_lane[y == 0]] = 1
    faces[voxel[y == 7], y_lane[y == 7] + 32] = 1
    z_lane = y * 8 + x
    faces[voxel[z == 0], 128 + 64 + z_lane[z == 0]] = 1
    faces[voxel[z == 7], 128 + z_lane[z == 7]] = 1
    own = np.arange(256) // 32
    pool = (octant(z, y, x)[:, None] == own[None, :]).astype(np.float32) / 64
    spread = (own[:, None] == octant(z, y, x)[None, :]).astype(np.float32)
    lane = np.arange(128)
    y_octant = octant(lane % 32 // 8 * 2 + lane // 64, lane // 32 % 2 * 4, lane % 8)
    z_octant = octant((lane < 64) * 4, lane % 64 // 8, lane % 8)
    y_spread = (own[:, None] == y_octant[None, :]).astype(np.float32)
    z_spread = (own[:, None] == z_octant[None, :]).astype(np.float32)
    cells = [(a, b, c) for a in range(2) for b in range(2) for c in range(2)]
    cells += [(a, b, c) for b in (-1, 2) for a in range(2) for c in range(2)]
    cells += [(a, b, c) for a in (-1, 2) for b in range(2) for c in range(2)]

    def row_of(a, b, c):
        part = (a // 2 + 1) * 3 + b // 2 + 1
        return part * 8 + a % 2 * 4 + b % 2 * 2 + c

    patch = np.zeros((TAPS, 32, 128), np.float32)
    plain = np.zeros((32, 128), np.float32)
    for i, (a, b, c) in enumerate(cells):
        plain[i, row_of(a, b, c)] = 1
        for t in range(TAPS):
            near = (a + t // 9 - 1, b + t // 3 % 3 - 1, c + t % 3 - 1)
            if 0 <= near[2] < 2:
                patch[t, i, row_of(*near)] = 1
    kinds = (faces, pool, spread, y_spread, z_spread, patch.reshape(TAPS * 32, 128), plain)
    return tuple(k.astype(ml_dtypes.bfloat16) for k in kinds)


def lanes():
    return lax.broadcasted_iota(jnp.int32, (CHANS, 128), 1)


def silu(x):
    return x * (1.0 / (1.0 + jnp.exp(-x)))


def tile(k):
    return slice(k * 128, k * 128 + 128)


def take_faces(signal, faces_ref, y_bank, z_bank):
    for i in range(0, BLOCKS, 8):
        block = signal[i : i + 8].reshape(8 * CHANS, VOXELS)
        packed = jnp.dot(block, faces_ref[...], preferred_element_type=f32).astype(bf16)
        y_bank[i : i + 8] = packed[:, :128].reshape(8, CHANS, 128)
        z_bank[i : i + 8] = packed[:, 128:].reshape(8, CHANS, 128)


def fill_planes(coords, counts, y_bank, z_bank, work, outs):
    lane = lanes()
    for plane in work:
        plane[...] = jnp.zeros_like(plane)
    in_low = (lane & 32) == 0
    in_back = lane >= 64

    def one(j, carry):
        live = j < counts[0]
        z, y, x = coords[0, j] & 3, coords[1, j] & 3, coords[2, j]
        odd = (x & 1) == 1
        y_row, z_row = (z * 4 + x) >> 1, (y * 4 + x) >> 1
        face = y_bank[j]
        turned = pltpu.roll(face, 32, 1)
        value = jnp.where(odd, turned, face)
        for plane, edge, low in ((0, 0, True), (1, 3, False)):
            row = jnp.where(live & (y == edge), y_row, 8)
            mask = jnp.logical_xor(in_low if low else jnp.logical_not(in_low), odd)
            work[plane][row] = jnp.where(mask, value, work[plane][row])
        face = z_bank[j]
        turned = pltpu.roll(face, 64, 1)
        value = jnp.where(odd, turned, face)
        for plane, edge, low in ((2, 0, True), (3, 3, False)):
            row = jnp.where(live & (z == edge), z_row, 8)
            mask = jnp.logical_xor(in_back if low else jnp.logical_not(in_back), odd)
            work[plane][row] = jnp.where(mask, value, work[plane][row])
        return carry

    lax.fori_loop(0, BLOCKS, one, 0, unroll=4)
    for plane, out in enumerate(outs):
        out[0:8] = work[plane][0:8]


def received(plane_ref, p, back):
    row = plane_ref[p // 2]
    return pltpu.roll(row, back, 1) if p % 2 else row


def bank_received(planes, y_bank, z_bank):
    zero = jnp.zeros((CHANS, 128), bf16)
    y_bank[BLOCKS] = zero
    z_bank[BLOCKS] = zero
    for p in range(16):
        y_bank[33 + p] = received(planes[0], p, 96)
        y_bank[49 + p] = received(planes[1], p, 96)
        z_bank[33 + p] = received(planes[2], p, 64)
        z_bank[49 + p] = received(planes[3], p, 64)


def convolve(coords, links, signal, y_bank, z_bank, weight, taps, finish):
    lane = lanes()
    along_x = lane & 7
    along_yx = lane & 63
    front = lane < 64

    def build(j, slot):
        z, y, x = coords[0, j] & 3, coords[1, j] & 3, coords[2, j]
        y_pos, z_pos = z * 4 + x, y * 4 + x

        def near(direction, inside, remote):
            link = links[direction, j]
            here = link & (BLOCKS - 1)
            if inside is not None:
                here = jnp.where(inside, here, remote)
            return jnp.where(link < 0, BLOCKS, here)

        x_up, x_down = near(0, None, None), near(1, None, None)
        y_up = y_bank[near(2, y < 3, 33 + y_pos)]
        y_down = y_bank[near(3, y > 0, 49 + y_pos)]
        z_up = z_bank[near(4, z < 3, 33 + z_pos)]
        z_down = z_bank[near(5, z > 0, 49 + z_pos)]
        own = [signal[j, :, tile(k)] for k in range(4)]
        half = [z_down] + [pltpu.roll(own[k], 64, 1) for k in range(4)] + [z_up]
        for k in range(4):
            to = tile(k)
            taps[slot][0:32, to] = own[k]
            taps[slot][32:64, to] = jnp.where(
                along_x == 7,
                pltpu.roll(signal[x_up, :, to], 7, 1),
                pltpu.roll(own[k], 127, 1),
            )
            taps[slot][64:96, to] = jnp.where(
                along_x == 0,
                pltpu.roll(signal[x_down, :, to], 121, 1),
                pltpu.roll(own[k], 1, 1),
            )
            taps[slot][96:128, to] = jnp.where(
                along_yx >= 56, pltpu.roll(y_up, 56 - 8 * k, 1), pltpu.roll(own[k], 120, 1)
            )
            taps[slot][128:160, to] = jnp.where(
                along_yx < 8, pltpu.roll(y_down, 96 - 8 * k, 1), pltpu.roll(own[k], 8, 1)
            )
            taps[slot][160:192, to] = jnp.where(front, half[k + 1], half[k + 2])
            taps[slot][192:224, to] = jnp.where(front, half[k], half[k + 1])

    def product(j, slot):
        finish(j, jnp.dot(weight[...], taps[slot][...], preferred_element_type=f32))

    build(0, 0)
    build(1, 1)

    def some(i, carry):
        j = i * 4
        build(j + 2, 2)
        product(j, 0)
        build(j + 3, 3)
        product(j + 1, 1)
        after = jnp.minimum(j + 4, BLOCKS - 2)
        build(after, 0)
        product(j + 2, 2)
        build(after + 1, 1)
        product(j + 3, 3)
        return carry

    lax.fori_loop(0, BLOCKS // 4, some, 0)


def first_faces(ins, outs, *work):
    features, faces, coords, counts = ins
    y_own, z_own, *planes = outs
    base, faces = features.get(), faces.get()
    for i in range(0, BLOCKS, 8):
        block = base[i : i + 8].reshape(8 * CHANS, VOXELS)
        packed = silu(jnp.dot(block, faces[...], preferred_element_type=f32)).astype(bf16)
        y_own.ref[i : i + 8] = packed[:, :128].reshape(8, CHANS, 128)
        z_own.ref[i : i + 8] = packed[:, 128:].reshape(8, CHANS, 128)
    y_own.send()
    z_own.send()
    fill_planes(coords.get(), counts.get(), y_own.ref, z_own.ref, work, [p.ref for p in planes])


def activate(ins, outs):
    base, signal = ins[0].get(), outs[0].ref

    def one(j, carry):
        signal[j] = silu(base[j].astype(f32)).astype(bf16)
        return carry

    lax.fori_loop(0, BLOCKS, one, 0, unroll=4)


def packed_tile(tile_rows):
    high = tile_rows.astype(bf16).astype(f32)
    low = tile_rows - high
    return jnp.concatenate([high[:, :128], high[:, 128:], low[:, :128], low[:, 128:]], axis=0).astype(bf16)


def unpacked_tile(rows):
    both = rows.astype(f32)
    both = both[0:16] + both[16:32]
    return jnp.concatenate([both[0:8], both[8:16]], axis=1)


def exact_parts(x):
    parts = []
    for _ in range(3):
        part = x.astype(bf16).astype(f32)
        parts.append(part)
        x = x - part
    return jnp.concatenate([*parts, jnp.zeros((4, 128), f32)], axis=0).astype(bf16)


def stat_rows(mean, spread):
    return jnp.concatenate([mean, spread, jnp.zeros((4, 128), f32)], axis=0)


def halves(row):
    return jnp.concatenate([row[:, :128], row[:, 128:]], axis=0)


def first_conv(ins, outs, signal, y_bank, z_bank, *taps_gathered):
    (coords, counts, links, weights, signal_in, y_own, z_own, *planes, features, pool, down, where, weight_columns) = ins
    level, own_tile, message = outs
    *taps, gathered = taps_gathered
    coords, counts, links, weight = coords.get(), counts.get(), links.get(), weights.get().at[0]
    signal[BLOCKS] = jnp.zeros((CHANS, VOXELS), bf16)
    bank_received([p.get() for p in planes], y_bank, z_bank)
    for one in (signal_in, y_own, z_own):
        one.get()
    base = features.get()
    level_ref = level.ref
    start = pl.multiple_of((where.get()[0] & 1) * HALF_ROWS, 128)
    half = weight_columns.get()[:, pl.ds(start, HALF_ROWS)]
    for i in range(16):
        message.ref[i, :, :HALF_ROWS] = half
    message.send(0)

    def finish(j, result):
        level_ref[j] = (base[j].astype(f32) + result).astype(bf16)

    convolve(coords, links, signal, y_bank, z_bank, weight, taps, finish)
    level.send()
    gathered[...] = jnp.zeros_like(gathered)
    diagonal = channel_diagonal()
    mean_of = pool.get()
    for i in range(0, BLOCKS, 8):
        block = level_ref[i : i + 8].reshape(8 * CHANS, VOXELS)
        means = jnp.dot(block, mean_of[...], preferred_element_type=f32)
        for u in range(8):
            j = i + u
            part = jnp.where(diagonal, means[u * CHANS : (u + 1) * CHANS], 0.0)
            cell, pos = place(coords, j)
            pos = jnp.where(j < counts[0], pos, 8)
            gathered[pos, pl.ds(cell, 1), :] = jnp.sum(part, axis=0, keepdims=True)
    total = jnp.zeros((16, COARSE), f32)
    rows = down.get()
    for pos in range(8):
        total += jnp.dot(
            gathered[pos].astype(bf16), rows[pos * 256 : pos * 256 + 256], preferred_element_type=f32
        )
    total = total[:8]
    mean = jnp.mean(total, axis=0, keepdims=True)
    spread = jnp.sum((total - mean) * (total - mean), axis=0, keepdims=True)
    extra = exact_parts(jnp.concatenate([halves(mean), halves(spread)], axis=0))
    for i in range(16):
        message.ref[i, :, HALF_ROWS:] = extra
    own_tile.ref[...] = total


def level_faces(ins, outs, y_bank, z_bank, *work):
    coords, counts, level, faces, own_tile = (one.get() for one in ins)
    take_faces(level, faces, y_bank, z_bank)
    fill_planes(coords, counts, y_bank, z_bank, work, [p.ref for p in outs])
    packed = packed_tile(own_tile[...])
    outs[0].ref[8] = packed
    outs[1].ref[8] = packed


def channel_diagonal():
    channel = lax.broadcasted_iota(jnp.int32, (CHANS, 256), 0)
    return channel == (lax.broadcasted_iota(jnp.int32, (CHANS, 256), 1) & 31)


def place(coords, j):
    z, y, x = coords[0, j] & 3, coords[1, j] & 3, coords[2, j]
    cell = (z >> 1) * 4 + (y >> 1) * 2 + (x >> 1)
    return cell, (z & 1) * 4 + (y & 1) * 2 + (x & 1)


def merged_sums(means, spreads, entries):
    mean = jnp.mean(means, axis=0, keepdims=True)
    away = means - mean
    return mean, jnp.sum(spreads + entries * away * away, axis=0, keepdims=True)


def row_sums(ins, outs):
    message, own_tile, y_above, y_below, z_low, z_high = (one.get() for one in ins)
    partial, z_low_out, z_high_out = (one.ref for one in outs)
    sums = message[...].astype(f32)
    sums = sums[:, 0:4] + sums[:, 4:8] + sums[:, 8:12]
    mean, spread = merged_sums(sums[:, 0:2], sums[:, 2:4], 8.0)
    both = stat_rows(mean[0], spread[0])
    for i in range(16):
        partial[i] = both
    packed = packed_tile(own_tile[...])
    for out, plane in ((z_low_out, z_low), (z_high_out, z_high)):
        out[0:8] = plane[...]
        out[8] = y_below[8]
        out[9] = packed
        out[10] = y_above[8]


def group_total(x):
    lane = lax.broadcasted_iota(jnp.int32, x.shape, 1)
    for width in (1, 2, 4):
        x = x + jnp.where(
            (lane & width) == 0, pltpu.roll(x, 128 - width, 1), pltpu.roll(x, width, 1)
        )
    return x


def times_half(total, near, half):
    for t in range(TAPS):
        total += lax.dot_general(
            near(t), half[:, tile(t)], (((1,), (1,)), ((), ())), preferred_element_type=f32
        )
    return total


def coarse_front(ins, outs, active, raw, patches):
    where, partial, own_tile, gain, bias, patch, plain, near_half, *planes = ins
    where, partial = where.get(), partial.get()
    major, minor = where[0], where[1]
    mean, spread_sum = merged_sums(partial[:, 0:2, :], partial[:, 2:4, :], 128.0)
    mean, spread_sum = mean[0], spread_sum[0]
    group_mean = group_total(mean) * (1.0 / GROUP)
    away = mean - group_mean
    variance = group_total(spread_sum + 2048.0 * away * away) * (1.0 / (2048 * GROUP))
    gain, bias = gain.get(), bias.get()
    group_mean = jnp.concatenate([group_mean[0:1], group_mean[1:2]], axis=1)
    variance = jnp.concatenate([variance[0:1], variance[1:2]], axis=1)
    scale = gain[...] / jnp.sqrt(variance + NORM_EPS)
    r0, r1, r2, r3 = (p.get() for p in planes)
    tiles = [
        [unpacked_tile(r3[8]), unpacked_tile(r3[9]), unpacked_tile(r3[10])],
        [unpacked_tile(r1[8]), own_tile.get()[...], unpacked_tile(r0[8])],
        [unpacked_tile(r2[8]), unpacked_tile(r2[9]), unpacked_tile(r2[10])],
    ]
    active[...] = jnp.zeros_like(active)
    raw[...] = jnp.zeros_like(raw)
    for dz, strip in enumerate(tiles):
        inside_z = (major + dz >= 1) & (major + dz <= 16)
        for dy in range(3):
            inside = inside_z & (minor + dy >= 1) & (minor + dy <= 16)
            value = strip[dy]
            at = (dz * 3 + dy) * 8
            raw[at : at + 8] = value
            normed = silu((value - group_mean) * scale + bias[...])
            active[at : at + 8] = jnp.where(inside, normed, 0.0)
    grid = active[...].astype(bf16)
    cells = jnp.dot(patch.get()[...], grid, preferred_element_type=f32).astype(bf16)
    for t in range(TAPS):
        patches[2 * t] = cells[t * 32 : t * 32 + 32, :128]
        patches[2 * t + 1] = cells[t * 32 : t * 32 + 32, 128:]
    rest = raw[...]
    plain = plain.get()
    total = jnp.zeros((32, COARSE), f32)
    for _ in range(3):
        high = rest.astype(bf16)
        rest = rest - high.astype(f32)
        total += jnp.dot(plain[...], high, preferred_element_type=f32)
    base = (major & 1) * TAPS
    half = near_half.get()
    outs[0].ref[...] = times_half(total, lambda t: patches[base + t], half)
    for t in range(TAPS):
        outs[1].ref[t] = patches[TAPS - base + t]


def second_conv(ins, outs, joined, signal, y_bank, z_bank, *rest):
    (total, far_patches, far_half, up, coords, counts, links, weights, spread, level, faces,
     y_spread, z_spread, *planes) = ins
    second, signal2, y_own, z_own, *sent, coarse = outs
    taps, work, (lifted, rows) = rest[:4], rest[4:8], rest[8:]
    far_patches = far_patches.get()
    total = times_half(total.get()[...], lambda t: far_patches[t], far_half.get())
    r0, r1, r2, r3 = (p.get() for p in planes)
    result = total.astype(bf16)
    coarse.ref[...] = result[0:8]
    up = up.get()
    for pos in range(8):
        lifted[pos] = jnp.dot(
            result, up[:, pos * 256 : pos * 256 + 256], preferred_element_type=f32
        )
    diagonal = channel_diagonal()
    coords, counts, links, weight = coords.get(), counts.get(), links.get(), weights.get().at[1]
    spread, level, faces = spread.get(), level.get(), faces.get()
    y_spread, z_spread = y_spread.get(), z_spread.get()

    def row_block(pos, cell):
        return jnp.where(diagonal, lifted[pos, pl.ds(cell, 1), :], 0.0).astype(bf16)

    for i in range(0, BLOCKS, 8):
        for u in range(8):
            cell, pos = place(coords, i + u)
            rows[u * CHANS : (u + 1) * CHANS] = row_block(pos, cell)
        term = jnp.dot(rows[...], spread[...], preferred_element_type=f32)
        base = level[i : i + 8].reshape(8 * CHANS, VOXELS).astype(f32)
        merged = (base + term).astype(bf16)
        joined[i : i + 8] = merged.reshape(8, CHANS, VOXELS)
        signal[i : i + 8] = silu(merged.astype(f32)).astype(bf16).reshape(8, CHANS, VOXELS)
    signal[BLOCKS] = jnp.zeros((CHANS, VOXELS), bf16)
    take_faces(signal, faces, y_bank, z_bank)
    zero = jnp.zeros((CHANS, 128), bf16)
    y_bank[BLOCKS] = zero
    z_bank[BLOCKS] = zero
    kinds = (
        (r0, y_bank, 33, 12, y_spread, 96, 4, 0, 2),
        (r1, y_bank, 49, 8, y_spread, 96, 4, 1, 2),
        (r2, z_bank, 33, 20, z_spread, 64, 2, 0, 4),
        (r3, z_bank, 49, 16, z_spread, 64, 2, 1, 4),
    )
    for plane, bank, entry, first, expand, back, stride, far, edge in kinds:
        for i in range(0, 16, 8):
            for u in range(8):
                p = i + u
                a, x = p // 4, p % 4
                pos = a % 2 * stride + far * edge + x % 2
                cell = first + a // 2 * 2 + x // 2
                rows[u * CHANS : (u + 1) * CHANS] = jnp.where(
                    diagonal, lifted[pos, cell : cell + 1, :], 0.0
                ).astype(bf16)
            term = jnp.dot(rows[...], expand[...], preferred_element_type=f32)
            for u in range(8):
                face = received(plane, i + u, back).astype(f32)
                merged = (face + term[u * CHANS : (u + 1) * CHANS]).astype(bf16)
                bank[entry + i + u] = silu(merged.astype(f32)).astype(bf16)

    second_ref, signal2_ref = second.ref, signal2.ref

    def finish(j, value):
        out = (joined[j].astype(f32) + value).astype(bf16)
        second_ref[j] = out
        signal2_ref[j] = silu(out.astype(f32)).astype(bf16)

    convolve(coords, links, signal, y_bank, z_bank, weight, taps, finish)
    second.send()
    signal2.send()
    take_faces(signal2_ref, faces, y_own.ref, z_own.ref)
    y_own.send()
    z_own.send()
    fill_planes(coords, counts, y_own.ref, z_own.ref, work, [p.ref for p in sent])


def third_conv(ins, outs, signal, y_bank, z_bank, *taps):
    (coords, counts, links, weights, signal_in, y_own, z_own, *planes, second) = ins
    coords, counts, links, weight = coords.get(), counts.get(), links.get(), weights.get().at[2]
    signal[BLOCKS] = jnp.zeros((CHANS, VOXELS), bf16)
    bank_received([p.get() for p in planes], y_bank, z_bank)
    for one in (signal_in, y_own, z_own):
        one.get()
    base = second.get()
    out = outs[0].ref

    def finish(j, result):
        value = base[j].astype(f32) + result
        out[j] = jnp.where(j < counts[0], value, 0.0).astype(bf16)

    convolve(coords, links, signal, y_bank, z_bank, weight, taps, finish)


class Arriving:
    def __init__(self, copy, ref):
        self.copy, self.ref = copy, ref
        copy.start()

    def get(self):
        if self.copy is not None:
            self.copy.wait()
            self.copy = None
        return self.ref


class Leaving:
    def __init__(self, copies, ref):
        self.copies, self.ref, self.sent = copies, ref, set()

    def send(self, *which):
        for i in which or range(len(self.copies)):
            if i not in self.sent:
                self.copies[i].start()
                self.sent.add(i)


def call(kernel, arrays, outs, scratch, microseconds, spare=()):
    own = [(i, to) for i, (_, to) in enumerate(arrays) if not callable(to)]
    count, total = len(arrays), len(arrays) + len(spare)

    def body(*refs):
        ins, results = refs[:count], refs[total : total + len(outs)]
        rest = refs[total + len(outs) :]
        buffers, rest = rest[: len(own)], rest[len(own) :]
        staged, rest = rest[: len(outs)], rest[len(outs) :]
        work, (in_sem, out_sem) = rest[:-2], rest[-2:]
        placed = {i: buffer for (i, _), buffer in zip(own, buffers)}
        arriving = []
        for i, (_, to) in enumerate(arrays):
            ref = placed[i] if i in placed else to(*work)
            source = ins[i].at[:, :, to] if isinstance(to, slice) else ins[i]
            arriving.append(Arriving(pltpu.make_async_copy(source, ref, in_sem.at[i]), ref))
        leaving = []
        for i, (_, _, *cut) in enumerate(outs):
            pairs = [(staged[i], results[i])]
            if cut:
                pairs = [(a.at[:, :, to], b.at[:, :, to]) for a, b in pairs for to in cut]
            leaving.append(
                Leaving(
                    [pltpu.make_async_copy(a, b, out_sem.at[2 * i + k]) for k, (a, b) in enumerate(pairs)],
                    staged[i],
                )
            )
        kernel(arriving, leaving, *work)
        for one in arriving:
            one.get()
        for one in leaving:
            one.send()
        for one in leaving:
            for copy in one.copies:
                copy.wait()

    hbm = pl.BlockSpec(memory_space=pltpu.HBM)
    buffers = []
    for i, to in own:
        shape = arrays[i][0].shape
        if isinstance(to, slice):
            shape = (*shape[:-1], to.stop - to.start)
        space = pltpu.SMEM if to == "smem" else pltpu.VMEM
        buffers.append(space(shape, arrays[i][0].dtype))
    buffers += [pltpu.VMEM(s, d) for s, d, *_ in (*outs, *scratch)]
    return pl.pallas_call(
        body,
        in_specs=[hbm] * total,
        out_specs=[hbm] * len(outs),
        out_shape=[jax.ShapeDtypeStruct(s, d) for s, d, *_ in outs],
        scratch_shapes=buffers
        + [pltpu.SemaphoreType.DMA((count,)), pltpu.SemaphoreType.DMA((2 * len(outs),))],
        compiler_params=pltpu.CompilerParams(vmem_limit_bytes=60 << 20),
        cost_estimate=pl.CostEstimate(
            flops=microseconds * 1_000_000_000,
            bytes_accessed=microseconds * 3_000_000,
            transcendentals=0,
        ),
    )(*[a for a, _ in arrays], *spare)


FIELD = ((BLOCKS, CHANS, VOXELS), bf16)
FACES = ((BLOCKS, CHANS, 128), bf16)
PLANE = ((8, CHANS, 128), bf16)
SIGNAL = ((BLOCKS + 1, CHANS, VOXELS), bf16)
BANK = ((BLOCKS + 33, CHANS, 128), bf16)
TAP_STACK = (((7 * CHANS, VOXELS), bf16),) * 4
SUMS = ((16, 8, 128), f32)
WORK = (((9, CHANS, 128), bf16),) * 4


def shifted(x, axes, step):
    count = lax.axis_size(axes)
    return lax.ppermute(x, axes, [(i, (i + step) % count) for i in range(count)])


def swap_planes(planes):
    y_low, y_high, z_low, z_high = planes
    return (
        shifted(y_low, MY, -1),
        shifted(y_high, MY, 1),
        shifted(z_low, MX, -1),
        shifted(z_high, MX, 1),
    )


def local(
    features, coords, counts, neighbours, fine_weights, down_weight, up_weight, norm_gain, norm_bias,
    coarse_weight,
):
    faces, pool, spread, y_spread, z_spread, patch, plain = map(jnp.asarray, tables())
    major = lax.axis_index(MX)
    minor = lax.axis_index(MY)
    where = jnp.stack([major, minor]).astype(jnp.int32)
    def plainly(*arrays):
        return tuple((x, None) for x in arrays)

    live = ((coords, "smem"), (counts, "smem"), (neighbours, "smem"))
    place_own = (
        lambda signal, *rest: signal.at[0:BLOCKS],
        lambda signal, y_bank, *rest: y_bank.at[0:BLOCKS],
        lambda signal, y_bank, z_bank, *rest: z_bank.at[0:BLOCKS],
    )
    *own, low_y, high_y, low_z, high_z = call(
        first_faces, (*plainly(features, faces), *live[:2]),
        (FACES, FACES) + (PLANE,) * 4, WORK, 3,
    )
    planes = swap_planes((low_y, high_y, low_z, high_z))
    (signal,) = call(activate, plainly(features), (FIELD,), (), 3)
    level, own_tile, message = call(
        first_conv,
        (*live, (fine_weights, None), *zip((signal, *own), place_own),
         *plainly(*planes, features, pool, down_weight), (where, "smem"), (coarse_weight.T, None)),
        (FIELD, ((8, COARSE), f32), ((16, 16, HALF_ROWS + 128), bf16, slice(0, HALF_ROWS), slice(HALF_ROWS, HALF_ROWS + 128))),
        (SIGNAL, BANK, BANK, *TAP_STACK, ((9, 16, COARSE), f32)), 8,
    )
    message = lax.all_to_all(message, MY, 0, 0)
    low_y, high_y, low_z, high_z = call(
        level_faces, (*live[:2], *plainly(level, faces, own_tile)),
        (((9, CHANS, 128), bf16),) * 2 + (PLANE,) * 2, (FACES, FACES, *WORK), 3,
    )
    y_above, y_below = shifted(low_y, MY, -1), shifted(high_y, MY, 1)
    partial, low_z, high_z = call(
        row_sums,
        ((message, slice(HALF_ROWS, HALF_ROWS + 128)), *plainly(own_tile, y_above, y_below, low_z, high_z)),
        (SUMS,) + (((11, CHANS, 128), bf16),) * 2, (), 1,
    )
    partial = lax.all_to_all(partial, MX, 0, 0)
    z_above, z_below = shifted(low_z, MX, -1), shifted(high_z, MX, 1)
    near_half = message.reshape(COARSE, HALF_ROWS + 128)
    near_half, partial, z_above, z_below = lax.optimization_barrier(
        (near_half, partial, z_above, z_below)
    )
    far_half = lax.ppermute(near_half, "mx_1", [(0, 1), (1, 0)])
    planes = (y_above, y_below, z_above, z_below)
    front = call(
        coarse_front,
        ((where, "smem"),
         *plainly(partial, own_tile, norm_gain.reshape(1, COARSE), norm_bias.reshape(1, COARSE),
                  patch, plain, near_half, *planes)),
        (((32, COARSE), f32), ((TAPS, 32, 128), bf16)),
        (((128, COARSE), f32), ((128, COARSE), f32), ((2 * TAPS, 32, 128), bf16)), 4,
    )
    second, *own, low_y, high_y, low_z, high_z, coarse = call(
        second_conv,
        (*plainly(*front, far_half, up_weight), *live,
         *plainly(fine_weights, spread, level, faces, y_spread, z_spread, *planes)),
        (FIELD, FIELD, FACES, FACES) + (PLANE,) * 4 + (((8, COARSE), bf16),),
        (FIELD, SIGNAL, BANK, BANK, *TAP_STACK, *WORK, ((8, 32, COARSE), f32), ((256, 256), bf16)), 12,
    )
    planes = swap_planes((low_y, high_y, low_z, high_z))
    (fine_out,) = call(
        third_conv, (*live, (fine_weights, None), *zip(own, place_own), *plainly(*planes, second)),
        (FIELD,), (SIGNAL, BANK, BANK, *TAP_STACK), 7,
    )
    return fine_out, coarse.reshape(2, 2, 2, COARSE)


def solution(mesh):
    split = Mesh(mesh.devices.reshape(8, 2, 4, 4), ("mx_0", "mx_1", "my_0", "my_1"))
    placed = (
        P(MX_MY, None, None), P(None, MX_MY), P(MX_MY), P(None, MX_MY),
        P(), P(), P(), P(), P(), P(None, MY),
    )
    return jax.shard_map(
        local,
        mesh=split,
        in_specs=placed,
        out_specs=(P(MX_MY, None, None), P(MX, MY, None, None)),
        check_vma=False,
    )
```

```python
import functools

import jax
import jax.numpy as jnp
import ml_dtypes
import numpy as np
from jax import lax
from jax.experimental import pallas as pl
from jax.experimental.pallas import tpu as pltpu
from jax.sharding import Mesh
from jax.sharding import PartitionSpec as P

MX = ("mx_0", "mx_1")
MY = ("my_0", "my_1")
MX_MY = MX + MY
BLOCKS = 32
CHANS = 32
VOXELS = 512
COARSE = 256
GROUP = 8
TAPS = 27
HALF_ROWS = TAPS * COARSE // 2
NORM_EPS = 1e-05
bf16 = jnp.bfloat16
f32 = jnp.float32


def octant(z, y, x):
    return z // 4 * 4 + y // 4 * 2 + x // 4


def voxel_zyx():
    voxel = np.arange(VOXELS)
    return voxel // 64, voxel // 8 % 8, voxel % 8


@functools.cache
def tables():
    z, y, x = voxel_zyx()
    voxel = np.arange(VOXELS)
    faces = np.zeros((VOXELS, 256), np.float32)
    y_lane = z % 2 * 64 + z // 2 * 8 + x
    faces[voxel[y == 0], y_lane[y == 0]] = 1
    faces[voxel[y == 7], y_lane[y == 7] + 32] = 1
    z_lane = y * 8 + x
    faces[voxel[z == 0], 128 + 64 + z_lane[z == 0]] = 1
    faces[voxel[z == 7], 128 + z_lane[z == 7]] = 1
    own = np.arange(256) // 32
    pool = (octant(z, y, x)[:, None] == own[None, :]).astype(np.float32) / 64
    spread = (own[:, None] == octant(z, y, x)[None, :]).astype(np.float32)
    lane = np.arange(128)
    y_octant = octant(lane % 32 // 8 * 2 + lane // 64, lane // 32 % 2 * 4, lane % 8)
    z_octant = octant((lane < 64) * 4, lane % 64 // 8, lane % 8)
    y_spread = (own[:, None] == y_octant[None, :]).astype(np.float32)
    z_spread = (own[:, None] == z_octant[None, :]).astype(np.float32)
    cells = [(a, b, c) for a in range(2) for b in range(2) for c in range(2)]
    cells += [(a, b, c) for b in (-1, 2) for a in range(2) for c in range(2)]
    cells += [(a, b, c) for a in (-1, 2) for b in range(2) for c in range(2)]

    def row_of(a, b, c):
        part = (a // 2 + 1) * 3 + b // 2 + 1
        return part * 8 + a % 2 * 4 + b % 2 * 2 + c

    patch = np.zeros((TAPS, 32, 128), np.float32)
    plain = np.zeros((32, 128), np.float32)
    for i, (a, b, c) in enumerate(cells):
        plain[i, row_of(a, b, c)] = 1
        for t in range(TAPS):
            near = (a + t // 9 - 1, b + t // 3 % 3 - 1, c + t % 3 - 1)
            if 0 <= near[2] < 2:
                patch[t, i, row_of(*near)] = 1
    kinds = (faces, pool, spread, y_spread, z_spread, patch.reshape(TAPS * 32, 128), plain)
    return tuple(k.astype(ml_dtypes.bfloat16) for k in kinds)


def lanes():
    return lax.broadcasted_iota(jnp.int32, (CHANS, 128), 1)


def silu(x):
    return x * (1.0 / (1.0 + jnp.exp(-x)))


def tile(k):
    return slice(k * 128, k * 128 + 128)


def take_faces(signal, faces_ref, y_bank, z_bank):
    for i in range(0, BLOCKS, 8):
        block = signal[i : i + 8].reshape(8 * CHANS, VOXELS)
        packed = jnp.dot(block, faces_ref[...], preferred_element_type=f32).astype(bf16)
        y_bank[i : i + 8] = packed[:, :128].reshape(8, CHANS, 128)
        z_bank[i : i + 8] = packed[:, 128:].reshape(8, CHANS, 128)


def fill_planes(coords, counts, y_bank, z_bank, work, outs):
    lane = lanes()
    for plane in work:
        plane[...] = jnp.zeros_like(plane)
    in_low = (lane & 32) == 0
    in_back = lane >= 64

    def one(j, carry):
        live = j < counts[0]
        z, y, x = coords[0, j] & 3, coords[1, j] & 3, coords[2, j]
        odd = (x & 1) == 1
        y_row, z_row = (z * 4 + x) >> 1, (y * 4 + x) >> 1
        face = y_bank[j]
        turned = pltpu.roll(face, 32, 1)
        value = jnp.where(odd, turned, face)
        for plane, edge, low in ((0, 0, True), (1, 3, False)):
            row = jnp.where(live & (y == edge), y_row, 8)
            mask = jnp.logical_xor(in_low if low else jnp.logical_not(in_low), odd)
            work[plane][row] = jnp.where(mask, value, work[plane][row])
        face = z_bank[j]
        turned = pltpu.roll(face, 64, 1)
        value = jnp.where(odd, turned, face)
        for plane, edge, low in ((2, 0, True), (3, 3, False)):
            row = jnp.where(live & (z == edge), z_row, 8)
            mask = jnp.logical_xor(in_back if low else jnp.logical_not(in_back), odd)
            work[plane][row] = jnp.where(mask, value, work[plane][row])
        return carry

    lax.fori_loop(0, BLOCKS, one, 0, unroll=4)
    for plane, out in enumerate(outs):
        out[0:8] = work[plane][0:8]


def received(plane_ref, p, back):
    row = plane_ref[p // 2]
    return pltpu.roll(row, back, 1) if p % 2 else row


def bank_received(planes, y_bank, z_bank):
    zero = jnp.zeros((CHANS, 128), bf16)
    y_bank[BLOCKS] = zero
    z_bank[BLOCKS] = zero
    for p in range(16):
        y_bank[33 + p] = received(planes[0], p, 96)
        y_bank[49 + p] = received(planes[1], p, 96)
        z_bank[33 + p] = received(planes[2], p, 64)
        z_bank[49 + p] = received(planes[3], p, 64)


def convolve(coords, links, signal, y_bank, z_bank, weight, taps, finish):
    lane = lanes()
    along_x = lane & 7
    along_yx = lane & 63
    front = lane < 64

    def build(j, slot):
        z, y, x = coords[0, j] & 3, coords[1, j] & 3, coords[2, j]
        y_pos, z_pos = z * 4 + x, y * 4 + x

        def near(direction, inside, remote):
            link = links[direction, j]
            here = link & (BLOCKS - 1)
            if inside is not None:
                here = jnp.where(inside, here, remote)
            return jnp.where(link < 0, BLOCKS, here)

        x_up, x_down = near(0, None, None), near(1, None, None)
        y_up = y_bank[near(2, y < 3, 33 + y_pos)]
        y_down = y_bank[near(3, y > 0, 49 + y_pos)]
        z_up = z_bank[near(4, z < 3, 33 + z_pos)]
        z_down = z_bank[near(5, z > 0, 49 + z_pos)]
        own = [signal[j, :, tile(k)] for k in range(4)]
        half = [z_down] + [pltpu.roll(own[k], 64, 1) for k in range(4)] + [z_up]
        for k in range(4):
            to = tile(k)
            taps[slot][0:32, to] = own[k]
            taps[slot][32:64, to] = jnp.where(
                along_x == 7,
                pltpu.roll(signal[x_up, :, to], 7, 1),
                pltpu.roll(own[k], 127, 1),
            )
            taps[slot][64:96, to] = jnp.where(
                along_x == 0,
                pltpu.roll(signal[x_down, :, to], 121, 1),
                pltpu.roll(own[k], 1, 1),
            )
            taps[slot][96:128, to] = jnp.where(
                along_yx >= 56, pltpu.roll(y_up, 56 - 8 * k, 1), pltpu.roll(own[k], 120, 1)
            )
            taps[slot][128:160, to] = jnp.where(
                along_yx < 8, pltpu.roll(y_down, 96 - 8 * k, 1), pltpu.roll(own[k], 8, 1)
            )
            taps[slot][160:192, to] = jnp.where(front, half[k + 1], half[k + 2])
            taps[slot][192:224, to] = jnp.where(front, half[k], half[k + 1])

    def product(j, slot):
        finish(j, jnp.dot(weight[...], taps[slot][...], preferred_element_type=f32))

    build(0, 0)
    build(1, 1)

    def some(i, carry):
        j = i * 4
        build(j + 2, 2)
        product(j, 0)
        build(j + 3, 3)
        product(j + 1, 1)
        after = jnp.minimum(j + 4, BLOCKS - 2)
        build(after, 0)
        product(j + 2, 2)
        build(after + 1, 1)
        product(j + 3, 3)
        return carry

    lax.fori_loop(0, BLOCKS // 4, some, 0)


def first_faces(ins, outs, *work):
    features, faces, coords, counts = ins
    y_own, z_own, *planes = outs
    base, faces = features.get(), faces.get()
    for i in range(0, BLOCKS, 8):
        block = base[i : i + 8].reshape(8 * CHANS, VOXELS)
        packed = silu(jnp.dot(block, faces[...], preferred_element_type=f32)).astype(bf16)
        y_own.ref[i : i + 8] = packed[:, :128].reshape(8, CHANS, 128)
        z_own.ref[i : i + 8] = packed[:, 128:].reshape(8, CHANS, 128)
    y_own.send()
    z_own.send()
    fill_planes(coords.get(), counts.get(), y_own.ref, z_own.ref, work, [p.ref for p in planes])


def activate(ins, outs):
    base, signal = ins[0].get(), outs[0].ref

    def one(j, carry):
        signal[j] = silu(base[j].astype(f32)).astype(bf16)
        return carry

    lax.fori_loop(0, BLOCKS, one, 0, unroll=4)


def packed_tile(tile_rows):
    high = tile_rows.astype(bf16).astype(f32)
    low = tile_rows - high
    return jnp.concatenate([high[:, :128], high[:, 128:], low[:, :128], low[:, 128:]], axis=0).astype(bf16)


def unpacked_tile(rows):
    both = rows.astype(f32)
    both = both[0:16] + both[16:32]
    return jnp.concatenate([both[0:8], both[8:16]], axis=1)


def exact_parts(x):
    parts = []
    for _ in range(3):
        part = x.astype(bf16).astype(f32)
        parts.append(part)
        x = x - part
    return jnp.concatenate([*parts, jnp.zeros((4, 128), f32)], axis=0).astype(bf16)


def stat_rows(mean, spread):
    return jnp.concatenate([mean, spread, jnp.zeros((4, 128), f32)], axis=0)


def halves(row):
    return jnp.concatenate([row[:, :128], row[:, 128:]], axis=0)


def first_conv(ins, outs, signal, y_bank, z_bank, *taps_gathered):
    (coords, counts, links, weights, signal_in, y_own, z_own, *planes, features, pool, down, where, weight_columns) = ins
    level, own_tile, message = outs
    *taps, gathered = taps_gathered
    coords, counts, links, weight = coords.get(), counts.get(), links.get(), weights.get().at[0]
    signal[BLOCKS] = jnp.zeros((CHANS, VOXELS), bf16)
    bank_received([p.get() for p in planes], y_bank, z_bank)
    for one in (signal_in, y_own, z_own):
        one.get()
    base = features.get()
    level_ref = level.ref
    start = pl.multiple_of((where.get()[0] & 1) * HALF_ROWS, 128)
    half = weight_columns.get()[:, pl.ds(start, HALF_ROWS)]
    for i in range(16):
        message.ref[i, :, :HALF_ROWS] = half
    message.send(0)

    def finish(j, result):
        level_ref[j] = (base[j].astype(f32) + result).astype(bf16)

    convolve(coords, links, signal, y_bank, z_bank, weight, taps, finish)
    level.send()
    gathered[...] = jnp.zeros_like(gathered)
    diagonal = channel_diagonal()
    mean_of = pool.get()
    for i in range(0, BLOCKS, 8):
        block = level_ref[i : i + 8].reshape(8 * CHANS, VOXELS)
        means = jnp.dot(block, mean_of[...], preferred_element_type=f32)
        for u in range(8):
            j = i + u
            part = jnp.where(diagonal, means[u * CHANS : (u + 1) * CHANS], 0.0)
            cell, pos = place(coords, j)
            pos = jnp.where(j < counts[0], pos, 8)
            gathered[pos, pl.ds(cell, 1), :] = jnp.sum(part, axis=0, keepdims=True)
    total = jnp.zeros((16, COARSE), f32)
    rows = down.get()
    for pos in range(8):
        total += jnp.dot(
            gathered[pos].astype(bf16), rows[pos * 256 : pos * 256 + 256], preferred_element_type=f32
        )
    total = total[:8]
    mean = jnp.mean(total, axis=0, keepdims=True)
    spread = jnp.sum((total - mean) * (total - mean), axis=0, keepdims=True)
    extra = exact_parts(jnp.concatenate([halves(mean), halves(spread)], axis=0))
    for i in range(16):
        message.ref[i, :, HALF_ROWS:] = extra
    own_tile.ref[...] = total


def level_faces(ins, outs, y_bank, z_bank, *work):
    coords, counts, level, faces, own_tile = (one.get() for one in ins)
    take_faces(level, faces, y_bank, z_bank)
    fill_planes(coords, counts, y_bank, z_bank, work, [p.ref for p in outs])
    packed = packed_tile(own_tile[...])
    outs[0].ref[8] = packed
    outs[1].ref[8] = packed


def channel_diagonal():
    channel = lax.broadcasted_iota(jnp.int32, (CHANS, 256), 0)
    return channel == (lax.broadcasted_iota(jnp.int32, (CHANS, 256), 1) & 31)


def place(coords, j):
    z, y, x = coords[0, j] & 3, coords[1, j] & 3, coords[2, j]
    cell = (z >> 1) * 4 + (y >> 1) * 2 + (x >> 1)
    return cell, (z & 1) * 4 + (y & 1) * 2 + (x & 1)


def merged_sums(means, spreads, entries):
    mean = jnp.mean(means, axis=0, keepdims=True)
    away = means - mean
    return mean, jnp.sum(spreads + entries * away * away, axis=0, keepdims=True)


def row_sums(ins, outs):
    message, own_tile, y_above, y_below, z_low, z_high = (one.get() for one in ins)
    partial, z_low_out, z_high_out = (one.ref for one in outs)
    sums = message[...].astype(f32)
    sums = sums[:, 0:4] + sums[:, 4:8] + sums[:, 8:12]
    mean, spread = merged_sums(sums[:, 0:2], sums[:, 2:4], 8.0)
    both = stat_rows(mean[0], spread[0])
    for i in range(16):
        partial[i] = both
    packed = packed_tile(own_tile[...])
    for out, plane in ((z_low_out, z_low), (z_high_out, z_high)):
        out[0:8] = plane[...]
        out[8] = y_below[8]
        out[9] = packed
        out[10] = y_above[8]


def group_total(x):
    lane = lax.broadcasted_iota(jnp.int32, x.shape, 1)
    for width in (1, 2, 4):
        x = x + jnp.where(
            (lane & width) == 0, pltpu.roll(x, 128 - width, 1), pltpu.roll(x, width, 1)
        )
    return x


def times_half(total, near, half):
    for t in range(TAPS):
        total += lax.dot_general(
            near(t), half[:, tile(t)], (((1,), (1,)), ((), ())), preferred_element_type=f32
        )
    return total


def coarse_sums(ins, active, raw, patches):
    where, partial, own_tile, gain, bias, patch, plain, near_half, far_half, *planes = ins
    where, partial = where.get(), partial.get()
    major, minor = where[0], where[1]
    mean, spread_sum = merged_sums(partial[:, 0:2, :], partial[:, 2:4, :], 128.0)
    mean, spread_sum = mean[0], spread_sum[0]
    group_mean = group_total(mean) * (1.0 / GROUP)
    away = mean - group_mean
    variance = group_total(spread_sum + 2048.0 * away * away) * (1.0 / (2048 * GROUP))
    gain, bias = gain.get(), bias.get()
    group_mean = jnp.concatenate([group_mean[0:1], group_mean[1:2]], axis=1)
    variance = jnp.concatenate([variance[0:1], variance[1:2]], axis=1)
    scale = gain[...] / jnp.sqrt(variance + NORM_EPS)
    r0, r1, r2, r3 = (p.get() for p in planes)
    tiles = [
        [unpacked_tile(r3[8]), unpacked_tile(r3[9]), unpacked_tile(r3[10])],
        [unpacked_tile(r1[8]), own_tile.get()[...], unpacked_tile(r0[8])],
        [unpacked_tile(r2[8]), unpacked_tile(r2[9]), unpacked_tile(r2[10])],
    ]
    active[...] = jnp.zeros_like(active)
    raw[...] = jnp.zeros_like(raw)
    for dz, strip in enumerate(tiles):
        inside_z = (major + dz >= 1) & (major + dz <= 16)
        for dy in range(3):
            inside = inside_z & (minor + dy >= 1) & (minor + dy <= 16)
            value = strip[dy]
            at = (dz * 3 + dy) * 8
            raw[at : at + 8] = value
            normed = silu((value - group_mean) * scale + bias[...])
            active[at : at + 8] = jnp.where(inside, normed, 0.0)
    grid = active[...].astype(bf16)
    cells = jnp.dot(patch.get()[...], grid, preferred_element_type=f32).astype(bf16)
    for t in range(TAPS):
        patches[2 * t] = cells[t * 32 : t * 32 + 32, :128]
        patches[2 * t + 1] = cells[t * 32 : t * 32 + 32, 128:]
    rest = raw[...]
    plain = plain.get()
    total = jnp.zeros((32, COARSE), f32)
    for _ in range(3):
        high = rest.astype(bf16)
        rest = rest - high.astype(f32)
        total += jnp.dot(plain[...], high, preferred_element_type=f32)
    base = (major & 1) * TAPS
    total = times_half(total, lambda t: patches[base + t], near_half.get())
    return times_half(total, lambda t: patches[TAPS - base + t], far_half.get())


def second_conv(ins, outs, joined, signal, y_bank, z_bank, *rest):
    first, planes = ins[:9], ins[9:13]
    (up, coords, counts, links, weights, spread, level, faces, y_spread, z_spread) = ins[13:]
    second, signal2, y_own, z_own, *sent, coarse = outs
    taps, work, (lifted, rows, *coarse_work) = rest[:4], rest[4:8], rest[8:]
    total = coarse_sums((*first, *planes), *coarse_work)
    r0, r1, r2, r3 = (p.get() for p in planes)
    result = total.astype(bf16)
    coarse.ref[...] = result[0:8]
    up = up.get()
    for pos in range(8):
        lifted[pos] = jnp.dot(
            result, up[:, pos * 256 : pos * 256 + 256], preferred_element_type=f32
        )
    diagonal = channel_diagonal()
    coords, counts, links, weight = coords.get(), counts.get(), links.get(), weights.get().at[1]
    spread, level, faces = spread.get(), level.get(), faces.get()
    y_spread, z_spread = y_spread.get(), z_spread.get()

    def row_block(pos, cell):
        return jnp.where(diagonal, lifted[pos, pl.ds(cell, 1), :], 0.0).astype(bf16)

    for i in range(0, BLOCKS, 8):
        for u in range(8):
            cell, pos = place(coords, i + u)
            rows[u * CHANS : (u + 1) * CHANS] = row_block(pos, cell)
        term = jnp.dot(rows[...], spread[...], preferred_element_type=f32)
        base = level[i : i + 8].reshape(8 * CHANS, VOXELS).astype(f32)
        merged = (base + term).astype(bf16)
        joined[i : i + 8] = merged.reshape(8, CHANS, VOXELS)
        signal[i : i + 8] = silu(merged.astype(f32)).astype(bf16).reshape(8, CHANS, VOXELS)
    signal[BLOCKS] = jnp.zeros((CHANS, VOXELS), bf16)
    take_faces(signal, faces, y_bank, z_bank)
    zero = jnp.zeros((CHANS, 128), bf16)
    y_bank[BLOCKS] = zero
    z_bank[BLOCKS] = zero
    kinds = (
        (r0, y_bank, 33, 12, y_spread, 96, 4, 0, 2),
        (r1, y_bank, 49, 8, y_spread, 96, 4, 1, 2),
        (r2, z_bank, 33, 20, z_spread, 64, 2, 0, 4),
        (r3, z_bank, 49, 16, z_spread, 64, 2, 1, 4),
    )
    for plane, bank, entry, first, expand, back, stride, far, edge in kinds:
        for i in range(0, 16, 8):
            for u in range(8):
                p = i + u
                a, x = p // 4, p % 4
                pos = a % 2 * stride + far * edge + x % 2
                cell = first + a // 2 * 2 + x // 2
                rows[u * CHANS : (u + 1) * CHANS] = jnp.where(
                    diagonal, lifted[pos, cell : cell + 1, :], 0.0
                ).astype(bf16)
            term = jnp.dot(rows[...], expand[...], preferred_element_type=f32)
            for u in range(8):
                face = received(plane, i + u, back).astype(f32)
                merged = (face + term[u * CHANS : (u + 1) * CHANS]).astype(bf16)
                bank[entry + i + u] = silu(merged.astype(f32)).astype(bf16)

    second_ref, signal2_ref = second.ref, signal2.ref

    def finish(j, value):
        out = (joined[j].astype(f32) + value).astype(bf16)
        second_ref[j] = out
        signal2_ref[j] = silu(out.astype(f32)).astype(bf16)

    convolve(coords, links, signal, y_bank, z_bank, weight, taps, finish)
    second.send()
    signal2.send()
    take_faces(signal2_ref, faces, y_own.ref, z_own.ref)
    y_own.send()
    z_own.send()
    fill_planes(coords, counts, y_own.ref, z_own.ref, work, [p.ref for p in sent])


def third_conv(ins, outs, signal, y_bank, z_bank, *taps):
    (coords, counts, links, weights, signal_in, y_own, z_own, *planes, second) = ins
    coords, counts, links, weight = coords.get(), counts.get(), links.get(), weights.get().at[2]
    signal[BLOCKS] = jnp.zeros((CHANS, VOXELS), bf16)
    bank_received([p.get() for p in planes], y_bank, z_bank)
    for one in (signal_in, y_own, z_own):
        one.get()
    base = second.get()
    out = outs[0].ref

    def finish(j, result):
        value = base[j].astype(f32) + result
        out[j] = jnp.where(j < counts[0], value, 0.0).astype(bf16)

    convolve(coords, links, signal, y_bank, z_bank, weight, taps, finish)


class Arriving:
    def __init__(self, copy, ref):
        self.copy, self.ref = copy, ref
        copy.start()

    def get(self):
        if self.copy is not None:
            self.copy.wait()
            self.copy = None
        return self.ref


class Leaving:
    def __init__(self, copies, ref):
        self.copies, self.ref, self.sent = copies, ref, set()

    def send(self, *which):
        for i in which or range(len(self.copies)):
            if i not in self.sent:
                self.copies[i].start()
                self.sent.add(i)


def call(kernel, arrays, outs, scratch, microseconds, spare=()):
    own = [(i, to) for i, (_, to) in enumerate(arrays) if not callable(to)]
    count, total = len(arrays), len(arrays) + len(spare)

    def body(*refs):
        ins, results = refs[:count], refs[total : total + len(outs)]
        rest = refs[total + len(outs) :]
        buffers, rest = rest[: len(own)], rest[len(own) :]
        staged, rest = rest[: len(outs)], rest[len(outs) :]
        work, (in_sem, out_sem) = rest[:-2], rest[-2:]
        placed = {i: buffer for (i, _), buffer in zip(own, buffers)}
        arriving = []
        for i, (_, to) in enumerate(arrays):
            ref = placed[i] if i in placed else to(*work)
            source = ins[i].at[:, :, to] if isinstance(to, slice) else ins[i]
            arriving.append(Arriving(pltpu.make_async_copy(source, ref, in_sem.at[i]), ref))
        leaving = []
        for i, (_, _, *cut) in enumerate(outs):
            pairs = [(staged[i], results[i])]
            if cut:
                pairs = [(a.at[:, :, to], b.at[:, :, to]) for a, b in pairs for to in cut]
            leaving.append(
                Leaving(
                    [pltpu.make_async_copy(a, b, out_sem.at[2 * i + k]) for k, (a, b) in enumerate(pairs)],
                    staged[i],
                )
            )
        kernel(arriving, leaving, *work)
        for one in arriving:
            one.get()
        for one in leaving:
            one.send()
        for one in leaving:
            for copy in one.copies:
                copy.wait()

    hbm = pl.BlockSpec(memory_space=pltpu.HBM)
    buffers = []
    for i, to in own:
        shape = arrays[i][0].shape
        if isinstance(to, slice):
            shape = (*shape[:-1], to.stop - to.start)
        space = pltpu.SMEM if to == "smem" else pltpu.VMEM
        buffers.append(space(shape, arrays[i][0].dtype))
    buffers += [pltpu.VMEM(s, d) for s, d, *_ in (*outs, *scratch)]
    return pl.pallas_call(
        body,
        in_specs=[hbm] * total,
        out_specs=[hbm] * len(outs),
        out_shape=[jax.ShapeDtypeStruct(s, d) for s, d, *_ in outs],
        scratch_shapes=buffers
        + [pltpu.SemaphoreType.DMA((count,)), pltpu.SemaphoreType.DMA((2 * len(outs),))],
        compiler_params=pltpu.CompilerParams(vmem_limit_bytes=60 << 20),
        cost_estimate=pl.CostEstimate(
            flops=microseconds * 1_000_000_000,
            bytes_accessed=microseconds * 3_000_000,
            transcendentals=0,
        ),
    )(*[a for a, _ in arrays], *spare)


FIELD = ((BLOCKS, CHANS, VOXELS), bf16)
FACES = ((BLOCKS, CHANS, 128), bf16)
PLANE = ((8, CHANS, 128), bf16)
SIGNAL = ((BLOCKS + 1, CHANS, VOXELS), bf16)
BANK = ((BLOCKS + 33, CHANS, 128), bf16)
TAP_STACK = (((7 * CHANS, VOXELS), bf16),) * 4
SUMS = ((16, 8, 128), f32)
WORK = (((9, CHANS, 128), bf16),) * 4


def shifted(x, axes, step):
    count = lax.axis_size(axes)
    return lax.ppermute(x, axes, [(i, (i + step) % count) for i in range(count)])


def swap_planes(planes):
    y_low, y_high, z_low, z_high = planes
    return (
        shifted(y_low, MY, -1),
        shifted(y_high, MY, 1),
        shifted(z_low, MX, -1),
        shifted(z_high, MX, 1),
    )


def local(
    features, coords, counts, neighbours, fine_weights, down_weight, up_weight, norm_gain, norm_bias,
    coarse_weight,
):
    faces, pool, spread, y_spread, z_spread, patch, plain = map(jnp.asarray, tables())
    major = lax.axis_index(MX)
    minor = lax.axis_index(MY)
    where = jnp.stack([major, minor]).astype(jnp.int32)
    def plainly(*arrays):
        return tuple((x, None) for x in arrays)

    live = ((coords, "smem"), (counts, "smem"), (neighbours, "smem"))
    place_own = (
        lambda signal, *rest: signal.at[0:BLOCKS],
        lambda signal, y_bank, *rest: y_bank.at[0:BLOCKS],
        lambda signal, y_bank, z_bank, *rest: z_bank.at[0:BLOCKS],
    )
    *own, low_y, high_y, low_z, high_z = call(
        first_faces, (*plainly(features, faces), *live[:2]),
        (FACES, FACES) + (PLANE,) * 4, WORK, 3,
    )
    planes = swap_planes((low_y, high_y, low_z, high_z))
    (signal,) = call(activate, plainly(features), (FIELD,), (), 3)
    level, own_tile, message = call(
        first_conv,
        (*live, (fine_weights, None), *zip((signal, *own), place_own),
         *plainly(*planes, features, pool, down_weight), (where, "smem"), (coarse_weight.T, None)),
        (FIELD, ((8, COARSE), f32), ((16, 16, HALF_ROWS + 128), bf16, slice(0, HALF_ROWS), slice(HALF_ROWS, HALF_ROWS + 128))),
        (SIGNAL, BANK, BANK, *TAP_STACK, ((9, 16, COARSE), f32)), 8,
    )
    message = lax.all_to_all(message, MY, 0, 0)
    low_y, high_y, low_z, high_z = call(
        level_faces, (*live[:2], *plainly(level, faces, own_tile)),
        (((9, CHANS, 128), bf16),) * 2 + (PLANE,) * 2, (FACES, FACES, *WORK), 3,
    )
    y_above, y_below = shifted(low_y, MY, -1), shifted(high_y, MY, 1)
    partial, low_z, high_z = call(
        row_sums,
        ((message, slice(HALF_ROWS, HALF_ROWS + 128)), *plainly(own_tile, y_above, y_below, low_z, high_z)),
        (SUMS,) + (((11, CHANS, 128), bf16),) * 2, (), 1,
    )
    near_half = message.reshape(COARSE, HALF_ROWS + 128)
    near_half, partial = lax.optimization_barrier((near_half, partial))
    partial = lax.all_to_all(partial, MX, 0, 0)
    far_half = lax.ppermute(near_half, "mx_1", [(0, 1), (1, 0)])
    z_above, z_below = shifted(low_z, MX, -1), shifted(high_z, MX, 1)
    second, *own, low_y, high_y, low_z, high_z, coarse = call(
        second_conv,
        ((where, "smem"),
         *plainly(partial, own_tile, norm_gain.reshape(1, COARSE), norm_bias.reshape(1, COARSE),
                  patch, plain, near_half, far_half, y_above, y_below, z_above, z_below, up_weight),
         *live, *plainly(fine_weights, spread, level, faces, y_spread, z_spread)),
        (FIELD, FIELD, FACES, FACES) + (PLANE,) * 4 + (((8, COARSE), bf16),),
        (FIELD, SIGNAL, BANK, BANK, *TAP_STACK, *WORK, ((8, 32, COARSE), f32), ((256, 256), bf16),
         ((128, COARSE), f32), ((128, COARSE), f32), ((2 * TAPS, 32, 128), bf16)), 14,
    )
    planes = swap_planes((low_y, high_y, low_z, high_z))
    (fine_out,) = call(
        third_conv, (*live, (fine_weights, None), *zip(own, place_own), *plainly(*planes, second)),
        (FIELD,), (SIGNAL, BANK, BANK, *TAP_STACK), 7,
    )
    return fine_out, coarse.reshape(2, 2, 2, COARSE)


def solution(mesh):
    split = Mesh(mesh.devices.reshape(8, 2, 4, 4), ("mx_0", "mx_1", "my_0", "my_1"))
    placed = (
        P(MX_MY, None, None), P(None, MX_MY), P(MX_MY), P(None, MX_MY),
        P(), P(), P(), P(), P(), P(None, MY),
    )
    return jax.shard_map(
        local,
        mesh=split,
        in_specs=placed,
        out_specs=(P(MX_MY, None, None), P(MX, MY, None, None)),
        check_vma=False,
    )
```

```python
import functools

import jax
import jax.numpy as jnp
import ml_dtypes
import numpy as np
from jax import lax
from jax.experimental import pallas as pl
from jax.experimental.pallas import tpu as pltpu
from jax.sharding import Mesh
from jax.sharding import PartitionSpec as P

MX = ("mx_0", "mx_1")
MY = ("my_0", "my_1")
MX_MY = MX + MY
BLOCKS = 32
CHANS = 32
VOXELS = 512
COARSE = 256
GROUP = 8
TAPS = 27
HALF_ROWS = TAPS * COARSE // 2
NORM_EPS = 1e-05
bf16 = jnp.bfloat16
f32 = jnp.float32


def octant(z, y, x):
    return z // 4 * 4 + y // 4 * 2 + x // 4


def voxel_zyx():
    voxel = np.arange(VOXELS)
    return voxel // 64, voxel // 8 % 8, voxel % 8


@functools.cache
def tables():
    z, y, x = voxel_zyx()
    voxel = np.arange(VOXELS)
    faces = np.zeros((VOXELS, 256), np.float32)
    y_lane = z % 2 * 64 + z // 2 * 8 + x
    faces[voxel[y == 0], y_lane[y == 0]] = 1
    faces[voxel[y == 7], y_lane[y == 7] + 32] = 1
    z_lane = y * 8 + x
    faces[voxel[z == 0], 128 + 64 + z_lane[z == 0]] = 1
    faces[voxel[z == 7], 128 + z_lane[z == 7]] = 1
    own = np.arange(256) // 32
    pool = (octant(z, y, x)[:, None] == own[None, :]).astype(np.float32) / 64
    spread = (own[:, None] == octant(z, y, x)[None, :]).astype(np.float32)
    lane = np.arange(128)
    y_octant = octant(lane % 32 // 8 * 2 + lane // 64, lane // 32 % 2 * 4, lane % 8)
    z_octant = octant((lane < 64) * 4, lane % 64 // 8, lane % 8)
    y_spread = (own[:, None] == y_octant[None, :]).astype(np.float32)
    z_spread = (own[:, None] == z_octant[None, :]).astype(np.float32)
    cells = [(a, b, c) for a in range(2) for b in range(2) for c in range(2)]
    cells += [(a, b, c) for b in (-1, 2) for a in range(2) for c in range(2)]
    cells += [(a, b, c) for a in (-1, 2) for b in range(2) for c in range(2)]

    def row_of(a, b, c):
        part = (a // 2 + 1) * 3 + b // 2 + 1
        return part * 8 + a % 2 * 4 + b % 2 * 2 + c

    patch = np.zeros((TAPS, 32, 128), np.float32)
    plain = np.zeros((32, 128), np.float32)
    for i, (a, b, c) in enumerate(cells):
        plain[i, row_of(a, b, c)] = 1
        for t in range(TAPS):
            near = (a + t // 9 - 1, b + t // 3 % 3 - 1, c + t % 3 - 1)
            if 0 <= near[2] < 2:
                patch[t, i, row_of(*near)] = 1
    kinds = (faces, pool, spread, y_spread, z_spread, patch.reshape(TAPS * 32, 128), plain)
    return tuple(k.astype(ml_dtypes.bfloat16) for k in kinds)


def lanes():
    return lax.broadcasted_iota(jnp.int32, (CHANS, 128), 1)


def silu(x):
    return x * (1.0 / (1.0 + jnp.exp(-x)))


def tile(k):
    return slice(k * 128, k * 128 + 128)


def take_faces(signal, faces_ref, y_bank, z_bank):
    for i in range(0, BLOCKS, 8):
        block = signal[i : i + 8].reshape(8 * CHANS, VOXELS)
        packed = jnp.dot(block, faces_ref[...], preferred_element_type=f32).astype(bf16)
        y_bank[i : i + 8] = packed[:, :128].reshape(8, CHANS, 128)
        z_bank[i : i + 8] = packed[:, 128:].reshape(8, CHANS, 128)


def fill_planes(coords, counts, y_bank, z_bank, work, outs):
    lane = lanes()
    for plane in work:
        plane[...] = jnp.zeros_like(plane)
    in_low = (lane & 32) == 0
    in_back = lane >= 64

    def one(j, carry):
        live = j < counts[0]
        z, y, x = coords[0, j] & 3, coords[1, j] & 3, coords[2, j]
        odd = (x & 1) == 1
        y_row, z_row = (z * 4 + x) >> 1, (y * 4 + x) >> 1
        face = y_bank[j]
        turned = pltpu.roll(face, 32, 1)
        value = jnp.where(odd, turned, face)
        for plane, edge, low in ((0, 0, True), (1, 3, False)):
            row = jnp.where(live & (y == edge), y_row, 8)
            mask = jnp.logical_xor(in_low if low else jnp.logical_not(in_low), odd)
            work[plane][row] = jnp.where(mask, value, work[plane][row])
        face = z_bank[j]
        turned = pltpu.roll(face, 64, 1)
        value = jnp.where(odd, turned, face)
        for plane, edge, low in ((2, 0, True), (3, 3, False)):
            row = jnp.where(live & (z == edge), z_row, 8)
            mask = jnp.logical_xor(in_back if low else jnp.logical_not(in_back), odd)
            work[plane][row] = jnp.where(mask, value, work[plane][row])
        return carry

    lax.fori_loop(0, BLOCKS, one, 0, unroll=4)
    for plane, out in enumerate(outs):
        out[0:8] = work[plane][0:8]


def received(plane_ref, p, back):
    row = plane_ref[p // 2]
    return pltpu.roll(row, back, 1) if p % 2 else row


def bank_received(planes, y_bank, z_bank):
    zero = jnp.zeros((CHANS, 128), bf16)
    y_bank[BLOCKS] = zero
    z_bank[BLOCKS] = zero
    for p in range(16):
        y_bank[33 + p] = received(planes[0], p, 96)
        y_bank[49 + p] = received(planes[1], p, 96)
        z_bank[33 + p] = received(planes[2], p, 64)
        z_bank[49 + p] = received(planes[3], p, 64)


def convolve(coords, links, signal, y_bank, z_bank, weight, taps, finish):
    lane = lanes()
    along_x = lane & 7
    along_yx = lane & 63
    front = lane < 64

    def build(j, slot):
        z, y, x = coords[0, j] & 3, coords[1, j] & 3, coords[2, j]
        y_pos, z_pos = z * 4 + x, y * 4 + x

        def near(direction, inside, remote):
            link = links[direction, j]
            here = link & (BLOCKS - 1)
            if inside is not None:
                here = jnp.where(inside, here, remote)
            return jnp.where(link < 0, BLOCKS, here)

        x_up, x_down = near(0, None, None), near(1, None, None)
        y_up = y_bank[near(2, y < 3, 33 + y_pos)]
        y_down = y_bank[near(3, y > 0, 49 + y_pos)]
        z_up = z_bank[near(4, z < 3, 33 + z_pos)]
        z_down = z_bank[near(5, z > 0, 49 + z_pos)]
        own = [signal[j, :, tile(k)] for k in range(4)]
        half = [z_down] + [pltpu.roll(own[k], 64, 1) for k in range(4)] + [z_up]
        for k in range(4):
            to = tile(k)
            taps[slot][0:32, to] = own[k]
            taps[slot][32:64, to] = jnp.where(
                along_x == 7,
                pltpu.roll(signal[x_up, :, to], 7, 1),
                pltpu.roll(own[k], 127, 1),
            )
            taps[slot][64:96, to] = jnp.where(
                along_x == 0,
                pltpu.roll(signal[x_down, :, to], 121, 1),
                pltpu.roll(own[k], 1, 1),
            )
            taps[slot][96:128, to] = jnp.where(
                along_yx >= 56, pltpu.roll(y_up, 56 - 8 * k, 1), pltpu.roll(own[k], 120, 1)
            )
            taps[slot][128:160, to] = jnp.where(
                along_yx < 8, pltpu.roll(y_down, 96 - 8 * k, 1), pltpu.roll(own[k], 8, 1)
            )
            taps[slot][160:192, to] = jnp.where(front, half[k + 1], half[k + 2])
            taps[slot][192:224, to] = jnp.where(front, half[k], half[k + 1])

    def product(j, slot):
        finish(j, jnp.dot(weight[...], taps[slot][...], preferred_element_type=f32))

    build(0, 0)
    build(1, 1)

    def some(i, carry):
        j = i * 4
        build(j + 2, 2)
        product(j, 0)
        build(j + 3, 3)
        product(j + 1, 1)
        after = jnp.minimum(j + 4, BLOCKS - 2)
        build(after, 0)
        product(j + 2, 2)
        build(after + 1, 1)
        product(j + 3, 3)
        return carry

    lax.fori_loop(0, BLOCKS // 4, some, 0)


def first_faces(ins, outs, *work):
    features, faces, coords, counts = ins
    y_own, z_own, *planes = outs
    base, faces = features.get(), faces.get()
    for i in range(0, BLOCKS, 8):
        block = base[i : i + 8].reshape(8 * CHANS, VOXELS)
        packed = silu(jnp.dot(block, faces[...], preferred_element_type=f32)).astype(bf16)
        y_own.ref[i : i + 8] = packed[:, :128].reshape(8, CHANS, 128)
        z_own.ref[i : i + 8] = packed[:, 128:].reshape(8, CHANS, 128)
    y_own.send()
    z_own.send()
    fill_planes(coords.get(), counts.get(), y_own.ref, z_own.ref, work, [p.ref for p in planes])


def activate(ins, outs):
    base, signal = ins[0].get(), outs[0].ref

    def one(j, carry):
        signal[j] = silu(base[j].astype(f32)).astype(bf16)
        return carry

    lax.fori_loop(0, BLOCKS, one, 0, unroll=4)


def packed_tile(tile_rows):
    high = tile_rows.astype(bf16).astype(f32)
    low = tile_rows - high
    return jnp.concatenate([high[:, :128], high[:, 128:], low[:, :128], low[:, 128:]], axis=0).astype(bf16)


def unpacked_tile(rows):
    both = rows.astype(f32)
    both = both[0:16] + both[16:32]
    return jnp.concatenate([both[0:8], both[8:16]], axis=1)


def exact_parts(x):
    parts = []
    for _ in range(3):
        part = x.astype(bf16).astype(f32)
        parts.append(part)
        x = x - part
    return jnp.concatenate([*parts, jnp.zeros((4, 128), f32)], axis=0).astype(bf16)


def stat_rows(mean, spread):
    return jnp.concatenate([mean, spread, jnp.zeros((4, 128), f32)], axis=0)


def halves(row):
    return jnp.concatenate([row[:, :128], row[:, 128:]], axis=0)


def first_conv(ins, outs, signal, y_bank, z_bank, *taps_gathered):
    (coords, counts, links, weights, signal_in, y_own, z_own, *planes, features, pool, down, where, weight_columns) = ins
    level, own_tile, message = outs
    *taps, gathered = taps_gathered
    coords, counts, links, weight = coords.get(), counts.get(), links.get(), weights.get().at[0]
    signal[BLOCKS] = jnp.zeros((CHANS, VOXELS), bf16)
    bank_received([p.get() for p in planes], y_bank, z_bank)
    for one in (signal_in, y_own, z_own):
        one.get()
    base = features.get()
    level_ref = level.ref
    start = pl.multiple_of((where.get()[0] & 1) * HALF_ROWS, 128)
    half = weight_columns.get()[:, pl.ds(start, HALF_ROWS)]
    for i in range(16):
        message.ref[i, :, :HALF_ROWS] = half
    message.send(0)

    def finish(j, result):
        level_ref[j] = (base[j].astype(f32) + result).astype(bf16)

    convolve(coords, links, signal, y_bank, z_bank, weight, taps, finish)
    level.send()
    gathered[...] = jnp.zeros_like(gathered)
    diagonal = channel_diagonal()
    mean_of = pool.get()
    for i in range(0, BLOCKS, 8):
        block = level_ref[i : i + 8].reshape(8 * CHANS, VOXELS)
        means = jnp.dot(block, mean_of[...], preferred_element_type=f32)
        for u in range(8):
            j = i + u
            part = jnp.where(diagonal, means[u * CHANS : (u + 1) * CHANS], 0.0)
            cell, pos = place(coords, j)
            pos = jnp.where(j < counts[0], pos, 8)
            gathered[pos, pl.ds(cell, 1), :] = jnp.sum(part, axis=0, keepdims=True)
    total = jnp.zeros((16, COARSE), f32)
    rows = down.get()
    for pos in range(8):
        total += jnp.dot(
            gathered[pos].astype(bf16), rows[pos * 256 : pos * 256 + 256], preferred_element_type=f32
        )
    total = total[:8]
    mean = jnp.mean(total, axis=0, keepdims=True)
    spread = jnp.sum((total - mean) * (total - mean), axis=0, keepdims=True)
    extra = exact_parts(jnp.concatenate([halves(mean), halves(spread)], axis=0))
    for i in range(16):
        message.ref[i, :, HALF_ROWS:] = extra
    own_tile.ref[...] = total


def level_faces(ins, outs, y_bank, z_bank, *work):
    coords, counts, level, faces, own_tile = (one.get() for one in ins)
    take_faces(level, faces, y_bank, z_bank)
    fill_planes(coords, counts, y_bank, z_bank, work, [p.ref for p in outs])
    packed = packed_tile(own_tile[...])
    outs[0].ref[8] = packed
    outs[1].ref[8] = packed


def channel_diagonal():
    channel = lax.broadcasted_iota(jnp.int32, (CHANS, 256), 0)
    return channel == (lax.broadcasted_iota(jnp.int32, (CHANS, 256), 1) & 31)


def place(coords, j):
    z, y, x = coords[0, j] & 3, coords[1, j] & 3, coords[2, j]
    cell = (z >> 1) * 4 + (y >> 1) * 2 + (x >> 1)
    return cell, (z & 1) * 4 + (y & 1) * 2 + (x & 1)


def merged_sums(means, spreads, entries):
    mean = jnp.mean(means, axis=0, keepdims=True)
    away = means - mean
    return mean, jnp.sum(spreads + entries * away * away, axis=0, keepdims=True)


def row_sums(ins, outs):
    message, own_tile, y_above, y_below = (one.get() for one in ins)
    partial, strip = (one.ref for one in outs)
    sums = message[...].astype(f32)
    sums = sums[:, 0:4] + sums[:, 4:8] + sums[:, 8:12]
    mean, spread = merged_sums(sums[:, 0:2], sums[:, 2:4], 8.0)
    both = stat_rows(mean[0], spread[0])
    for i in range(16):
        partial[i] = both
    strip[0] = y_below[8]
    strip[1] = packed_tile(own_tile[...])
    strip[2] = y_above[8]


def group_total(x):
    lane = lax.broadcasted_iota(jnp.int32, x.shape, 1)
    for width in (1, 2, 4):
        x = x + jnp.where(
            (lane & width) == 0, pltpu.roll(x, 128 - width, 1), pltpu.roll(x, width, 1)
        )
    return x


def times_half(total, near, half):
    for t in range(TAPS):
        total += lax.dot_general(
            near(t), half[:, tile(t)], (((1,), (1,)), ((), ())), preferred_element_type=f32
        )
    return total


def coarse_sums(ins, active, raw, patches):
    where, partial, own_tile, gain, bias, patch, plain, near_half, far_half, *planes = ins
    where, partial = where.get(), partial.get()
    major, minor = where[0], where[1]
    mean, spread_sum = merged_sums(partial[:, 0:2, :], partial[:, 2:4, :], 128.0)
    mean, spread_sum = mean[0], spread_sum[0]
    group_mean = group_total(mean) * (1.0 / GROUP)
    away = mean - group_mean
    variance = group_total(spread_sum + 2048.0 * away * away) * (1.0 / (2048 * GROUP))
    gain, bias = gain.get(), bias.get()
    group_mean = jnp.concatenate([group_mean[0:1], group_mean[1:2]], axis=1)
    variance = jnp.concatenate([variance[0:1], variance[1:2]], axis=1)
    scale = gain[...] / jnp.sqrt(variance + NORM_EPS)
    y_above, y_below, strip_above, strip_below = (p.get() for p in planes)
    tiles = [
        [unpacked_tile(strip_below[step]) for step in range(3)],
        [unpacked_tile(y_below[8]), own_tile.get()[...], unpacked_tile(y_above[8])],
        [unpacked_tile(strip_above[step]) for step in range(3)],
    ]
    active[...] = jnp.zeros_like(active)
    raw[...] = jnp.zeros_like(raw)
    for dz, strip in enumerate(tiles):
        inside_z = (major + dz >= 1) & (major + dz <= 16)
        for dy in range(3):
            inside = inside_z & (minor + dy >= 1) & (minor + dy <= 16)
            value = strip[dy]
            at = (dz * 3 + dy) * 8
            raw[at : at + 8] = value
            normed = silu((value - group_mean) * scale + bias[...])
            active[at : at + 8] = jnp.where(inside, normed, 0.0)
    grid = active[...].astype(bf16)
    cells = jnp.dot(patch.get()[...], grid, preferred_element_type=f32).astype(bf16)
    for t in range(TAPS):
        patches[2 * t] = cells[t * 32 : t * 32 + 32, :128]
        patches[2 * t + 1] = cells[t * 32 : t * 32 + 32, 128:]
    rest = raw[...]
    plain = plain.get()
    total = jnp.zeros((32, COARSE), f32)
    for _ in range(3):
        high = rest.astype(bf16)
        rest = rest - high.astype(f32)
        total += jnp.dot(plain[...], high, preferred_element_type=f32)
    base = (major & 1) * TAPS
    total = times_half(total, lambda t: patches[base + t], near_half.get())
    return times_half(total, lambda t: patches[TAPS - base + t], far_half.get())


def second_conv(ins, outs, joined, signal, y_bank, z_bank, *rest):
    first, strips, planes = ins[:9], ins[9:11], ins[11:15]
    (up, coords, counts, links, weights, spread, level, faces, y_spread, z_spread) = ins[15:]
    second, signal2, y_own, z_own, *sent, coarse = outs
    taps, work, (lifted, rows, *coarse_work) = rest[:4], rest[4:8], rest[8:]
    total = coarse_sums((*first, *planes[:2], *strips), *coarse_work)
    r0, r1, r2, r3 = (p.get() for p in planes)
    result = total.astype(bf16)
    coarse.ref[...] = result[0:8]
    up = up.get()
    for pos in range(8):
        lifted[pos] = jnp.dot(
            result, up[:, pos * 256 : pos * 256 + 256], preferred_element_type=f32
        )
    diagonal = channel_diagonal()
    coords, counts, links, weight = coords.get(), counts.get(), links.get(), weights.get().at[1]
    spread, level, faces = spread.get(), level.get(), faces.get()
    y_spread, z_spread = y_spread.get(), z_spread.get()

    def row_block(pos, cell):
        return jnp.where(diagonal, lifted[pos, pl.ds(cell, 1), :], 0.0).astype(bf16)

    for i in range(0, BLOCKS, 8):
        for u in range(8):
            cell, pos = place(coords, i + u)
            rows[u * CHANS : (u + 1) * CHANS] = row_block(pos, cell)
        term = jnp.dot(rows[...], spread[...], preferred_element_type=f32)
        base = level[i : i + 8].reshape(8 * CHANS, VOXELS).astype(f32)
        merged = (base + term).astype(bf16)
        joined[i : i + 8] = merged.reshape(8, CHANS, VOXELS)
        signal[i : i + 8] = silu(merged.astype(f32)).astype(bf16).reshape(8, CHANS, VOXELS)
    signal[BLOCKS] = jnp.zeros((CHANS, VOXELS), bf16)
    take_faces(signal, faces, y_bank, z_bank)
    zero = jnp.zeros((CHANS, 128), bf16)
    y_bank[BLOCKS] = zero
    z_bank[BLOCKS] = zero
    kinds = (
        (r0, y_bank, 33, 12, y_spread, 96, 4, 0, 2),
        (r1, y_bank, 49, 8, y_spread, 96, 4, 1, 2),
        (r2, z_bank, 33, 20, z_spread, 64, 2, 0, 4),
        (r3, z_bank, 49, 16, z_spread, 64, 2, 1, 4),
    )
    for plane, bank, entry, first, expand, back, stride, far, edge in kinds:
        for i in range(0, 16, 8):
            for u in range(8):
                p = i + u
                a, x = p // 4, p % 4
                pos = a % 2 * stride + far * edge + x % 2
                cell = first + a // 2 * 2 + x // 2
                rows[u * CHANS : (u + 1) * CHANS] = jnp.where(
                    diagonal, lifted[pos, cell : cell + 1, :], 0.0
                ).astype(bf16)
            term = jnp.dot(rows[...], expand[...], preferred_element_type=f32)
            for u in range(8):
                face = received(plane, i + u, back).astype(f32)
                merged = (face + term[u * CHANS : (u + 1) * CHANS]).astype(bf16)
                bank[entry + i + u] = silu(merged.astype(f32)).astype(bf16)

    second_ref, signal2_ref = second.ref, signal2.ref

    def finish(j, value):
        out = (joined[j].astype(f32) + value).astype(bf16)
        second_ref[j] = out
        signal2_ref[j] = silu(out.astype(f32)).astype(bf16)

    convolve(coords, links, signal, y_bank, z_bank, weight, taps, finish)
    second.send()
    signal2.send()
    take_faces(signal2_ref, faces, y_own.ref, z_own.ref)
    y_own.send()
    z_own.send()
    fill_planes(coords, counts, y_own.ref, z_own.ref, work, [p.ref for p in sent])


def third_conv(ins, outs, signal, y_bank, z_bank, *taps):
    (coords, counts, links, weights, signal_in, y_own, z_own, *planes, second) = ins
    coords, counts, links, weight = coords.get(), counts.get(), links.get(), weights.get().at[2]
    signal[BLOCKS] = jnp.zeros((CHANS, VOXELS), bf16)
    bank_received([p.get() for p in planes], y_bank, z_bank)
    for one in (signal_in, y_own, z_own):
        one.get()
    base = second.get()
    out = outs[0].ref

    def finish(j, result):
        value = base[j].astype(f32) + result
        out[j] = jnp.where(j < counts[0], value, 0.0).astype(bf16)

    convolve(coords, links, signal, y_bank, z_bank, weight, taps, finish)


class Arriving:
    def __init__(self, copy, ref):
        self.copy, self.ref = copy, ref
        copy.start()

    def get(self):
        if self.copy is not None:
            self.copy.wait()
            self.copy = None
        return self.ref


class Leaving:
    def __init__(self, copies, ref):
        self.copies, self.ref, self.sent = copies, ref, set()

    def send(self, *which):
        for i in which or range(len(self.copies)):
            if i not in self.sent:
                self.copies[i].start()
                self.sent.add(i)


def call(kernel, arrays, outs, scratch, microseconds, spare=()):
    own = [(i, to) for i, (_, to) in enumerate(arrays) if not callable(to)]
    count, total = len(arrays), len(arrays) + len(spare)

    def body(*refs):
        ins, results = refs[:count], refs[total : total + len(outs)]
        rest = refs[total + len(outs) :]
        buffers, rest = rest[: len(own)], rest[len(own) :]
        staged, rest = rest[: len(outs)], rest[len(outs) :]
        work, (in_sem, out_sem) = rest[:-2], rest[-2:]
        placed = {i: buffer for (i, _), buffer in zip(own, buffers)}
        arriving = []
        for i, (_, to) in enumerate(arrays):
            ref = placed[i] if i in placed else to(*work)
            source = ins[i].at[:, :, to] if isinstance(to, slice) else ins[i]
            arriving.append(Arriving(pltpu.make_async_copy(source, ref, in_sem.at[i]), ref))
        leaving = []
        for i, (_, _, *cut) in enumerate(outs):
            pairs = [(staged[i], results[i])]
            if cut:
                pairs = [(a.at[:, :, to], b.at[:, :, to]) for a, b in pairs for to in cut]
            leaving.append(
                Leaving(
                    [pltpu.make_async_copy(a, b, out_sem.at[2 * i + k]) for k, (a, b) in enumerate(pairs)],
                    staged[i],
                )
            )
        kernel(arriving, leaving, *work)
        for one in arriving:
            one.get()
        for one in leaving:
            one.send()
        for one in leaving:
            for copy in one.copies:
                copy.wait()

    hbm = pl.BlockSpec(memory_space=pltpu.HBM)
    buffers = []
    for i, to in own:
        shape = arrays[i][0].shape
        if isinstance(to, slice):
            shape = (*shape[:-1], to.stop - to.start)
        space = pltpu.SMEM if to == "smem" else pltpu.VMEM
        buffers.append(space(shape, arrays[i][0].dtype))
    buffers += [pltpu.VMEM(s, d) for s, d, *_ in (*outs, *scratch)]
    return pl.pallas_call(
        body,
        in_specs=[hbm] * total,
        out_specs=[hbm] * len(outs),
        out_shape=[jax.ShapeDtypeStruct(s, d) for s, d, *_ in outs],
        scratch_shapes=buffers
        + [pltpu.SemaphoreType.DMA((count,)), pltpu.SemaphoreType.DMA((2 * len(outs),))],
        compiler_params=pltpu.CompilerParams(vmem_limit_bytes=60 << 20),
        cost_estimate=pl.CostEstimate(
            flops=microseconds * 1_000_000_000,
            bytes_accessed=microseconds * 3_000_000,
            transcendentals=0,
        ),
    )(*[a for a, _ in arrays], *spare)


FIELD = ((BLOCKS, CHANS, VOXELS), bf16)
FACES = ((BLOCKS, CHANS, 128), bf16)
PLANE = ((8, CHANS, 128), bf16)
SIGNAL = ((BLOCKS + 1, CHANS, VOXELS), bf16)
BANK = ((BLOCKS + 33, CHANS, 128), bf16)
TAP_STACK = (((7 * CHANS, VOXELS), bf16),) * 4
SUMS = ((16, 8, 128), f32)
WORK = (((9, CHANS, 128), bf16),) * 4


def shifted(x, axes, step):
    count = lax.axis_size(axes)
    return lax.ppermute(x, axes, [(i, (i + step) % count) for i in range(count)])


def swap_planes(planes):
    y_low, y_high, z_low, z_high = planes
    return (
        shifted(y_low, MY, -1),
        shifted(y_high, MY, 1),
        shifted(z_low, MX, -1),
        shifted(z_high, MX, 1),
    )


def local(
    features, coords, counts, neighbours, fine_weights, down_weight, up_weight, norm_gain, norm_bias,
    coarse_weight,
):
    faces, pool, spread, y_spread, z_spread, patch, plain = map(jnp.asarray, tables())
    major = lax.axis_index(MX)
    minor = lax.axis_index(MY)
    where = jnp.stack([major, minor]).astype(jnp.int32)
    def plainly(*arrays):
        return tuple((x, None) for x in arrays)

    live = ((coords, "smem"), (counts, "smem"), (neighbours, "smem"))
    place_own = (
        lambda signal, *rest: signal.at[0:BLOCKS],
        lambda signal, y_bank, *rest: y_bank.at[0:BLOCKS],
        lambda signal, y_bank, z_bank, *rest: z_bank.at[0:BLOCKS],
    )
    *own, low_y, high_y, low_z, high_z = call(
        first_faces, (*plainly(features, faces), *live[:2]),
        (FACES, FACES) + (PLANE,) * 4, WORK, 3,
    )
    planes = swap_planes((low_y, high_y, low_z, high_z))
    (signal,) = call(activate, plainly(features), (FIELD,), (), 3)
    level, own_tile, message = call(
        first_conv,
        (*live, (fine_weights, None), *zip((signal, *own), place_own),
         *plainly(*planes, features, pool, down_weight), (where, "smem"), (coarse_weight.T, None)),
        (FIELD, ((8, COARSE), f32), ((16, 16, HALF_ROWS + 128), bf16, slice(0, HALF_ROWS), slice(HALF_ROWS, HALF_ROWS + 128))),
        (SIGNAL, BANK, BANK, *TAP_STACK, ((9, 16, COARSE), f32)), 8,
    )
    message = lax.all_to_all(message, MY, 0, 0)
    low_y, high_y, low_z, high_z = call(
        level_faces, (*live[:2], *plainly(level, faces, own_tile)),
        (((9, CHANS, 128), bf16),) * 2 + (PLANE,) * 2, (FACES, FACES, *WORK), 3,
    )
    planes = swap_planes((low_y, high_y, low_z, high_z))
    partial, strip = call(
        row_sums,
        ((message, slice(HALF_ROWS, HALF_ROWS + 128)), *plainly(own_tile, *planes[:2])),
        (SUMS, ((3, CHANS, 128), bf16)), (), 1, planes[2:],
    )
    near_half = message.reshape(COARSE, HALF_ROWS + 128)
    near_half, partial = lax.optimization_barrier((near_half, partial))
    partial = lax.all_to_all(partial, MX, 0, 0)
    far_half = lax.ppermute(near_half, "mx_1", [(0, 1), (1, 0)])
    strips = (shifted(strip, MX, -1), shifted(strip, MX, 1))
    second, *own, low_y, high_y, low_z, high_z, coarse = call(
        second_conv,
        ((where, "smem"),
         *plainly(partial, own_tile, norm_gain.reshape(1, COARSE), norm_bias.reshape(1, COARSE),
                  patch, plain, near_half, far_half, *strips, *planes, up_weight),
         *live, *plainly(fine_weights, spread, level, faces, y_spread, z_spread)),
        (FIELD, FIELD, FACES, FACES) + (PLANE,) * 4 + (((8, COARSE), bf16),),
        (FIELD, SIGNAL, BANK, BANK, *TAP_STACK, *WORK, ((8, 32, COARSE), f32), ((256, 256), bf16),
         ((128, COARSE), f32), ((128, COARSE), f32), ((2 * TAPS, 32, 128), bf16)), 14,
    )
    planes = swap_planes((low_y, high_y, low_z, high_z))
    (fine_out,) = call(
        third_conv, (*live, (fine_weights, None), *zip(own, place_own), *plainly(*planes, second)),
        (FIELD,), (SIGNAL, BANK, BANK, *TAP_STACK), 7,
    )
    return fine_out, coarse.reshape(2, 2, 2, COARSE)


def solution(mesh):
    split = Mesh(mesh.devices.reshape(8, 2, 4, 4), ("mx_0", "mx_1", "my_0", "my_1"))
    placed = (
        P(MX_MY, None, None), P(None, MX_MY), P(MX_MY), P(None, MX_MY),
        P(), P(), P(), P(), P(), P(None, MY),
    )
    return jax.shard_map(
        local,
        mesh=split,
        in_specs=placed,
        out_specs=(P(MX_MY, None, None), P(MX, MY, None, None)),
        check_vma=False,
    )
```
